512 devices in a mesh: pipe: 8 (over z_hi, x), expert: 64 (over y, z_lo, core).
Axes of the slice: x: 4, y: 8, z: 8 (z_hi: 2, z_lo: 4; z = z_hi * 4 + z_lo), core: 2. Of those that a mesh axis runs over, the one named last changes fastest.
Arguments:
- tokens: bfloat16 [8192, 3584], P('expert'), may hold values from -6 to 6
- expert_ids: int32 [8192, 8], P('expert'), may hold values from 0 to 63, all different within a row; in each aligned block of 128 rows (0 to 127, 128 to 255, ...) at most 17 rows name the same one
- gate_scale: float32 [8192, 8], P('expert'), may hold values from 0.1 to 0.6
- w_gate: bfloat16 [64, 3584, 1024], P('expert', None, 'pipe'), may hold values from -0.09375 to 0.09375
- w_up: bfloat16 [64, 3584, 1024], P('expert', None, 'pipe'), may hold values from -0.09375 to 0.09375
- w_down: bfloat16 [64, 1024, 3584], P('expert', 'pipe'), may hold values from -0.5 to 0.5
Outputs:
- mixed: bfloat16 [8192, 3584], P('expert', 'pipe')
The draws below stay inside these ranges and needn't reach their ends.
Inputs may be any that keep to these rules, and one draw needn't show every extreme that they name: `expert_ids`: the 8 ids of a token differ. Among the 128 tokens held at one position of the expert axis no expert is named more than 17 times, a bound that some block reaches.
All inputs are finite; a program needn't handle non-finite values.
Results may differ from the reference program's by a relative error of at most 0.0057.
Values may be sent and summed in bfloat16 or wider, within the bound.
No kernel may reach another device: no remote copies, remote signals or barrier semaphores. Data moves between devices by JAX's collectives and lax.ppermute only.
A program may use at most 128 MiB of HBM per device.

```python
import math
import jax
import jax.numpy as jnp
import numpy as np
from jax import lax

D = 3584
FF = 1024
TOPK = 8
TOK_DEV = 128
EXPERTS = 64
CAP = 17
TOKENS = 8192
N_PIPE = 8
N_EXPERT = 64


def steps_of(stream_key, shape, split, low, top_value):
    loudness = 1.0
    for position, blocks in split:
        heights = jax.random.uniform(jax.random.fold_in(jax.random.fold_in(stream_key, 6), position), (blocks,), jnp.float32, low / len(split), top_value / len(split))
        loudness = loudness * jnp.repeat(jnp.exp(heights), shape[position] // blocks).reshape((-1,) + (1,) * (len(shape) - 1 - position))
    return loudness


def assign_block(rng, own, number, rows, count, top, reach, slope):
    order = jax.random.permutation(rng, count)
    packed, ordinary = shares(count, rows * top, reach, slope, True), shares(count, rows * top, reach, slope, False)
    places = jnp.arange(count)

    def named(lengths, offset_by):
        used = int((lengths > 0).sum())
        fixed = max(1, used // 4)
        shifted = fixed + (places - fixed + offset_by * (used - fixed)) % max(1, count - fixed)
        return jnp.zeros((count,), jnp.int32).at[order[jnp.where(places < fixed, places, shifted)]].set(jnp.asarray(lengths, jnp.int32))

    lengths = jnp.where(number % 4 == 0, named(packed, number // 4), named(ordinary, number - number // 4 - 1))
    mixed = jax.random.permutation(jax.random.fold_in(own, 3), count)
    source_of, sink = mixed[0:count // 2 * 2:2], mixed[1:count // 2 * 2:2]
    slack = jnp.minimum(lengths[source_of] - 1, reach - lengths[sink]) // 2
    slack = jnp.where((source_of == order[0]) | (sink == order[0]) | (lengths[sink] == 0), 0, jnp.maximum(slack, 0))
    shifted = jax.random.randint(jax.random.fold_in(own, 4), (count // 2,), 0, 1 << 20) % (slack + 1)
    lengths = lengths.at[source_of].add(-shifted).at[sink].add(shifted)
    members = jnp.searchsorted(jnp.cumsum(lengths), jnp.arange(rows * top), side="right").astype(jnp.int32)
    grid = members.reshape(top, rows).T
    grid = grid[jax.random.permutation(jax.random.fold_in(own, 1), rows)]
    offset_by = jax.random.randint(jax.random.fold_in(own, 2), (rows, 1), 0, top)
    return jnp.take_along_axis(grid, (jnp.arange(top)[None, :] + offset_by) % top, axis=1)


def shares(amount, total, most, skew, full):
    loads = [(1 << 20) // math.isqrt(grade ** skew) + 1 for grade in range(1, amount + 1)]
    largest = most if full else min(most, max(-(-total // amount), total * loads[0] // sum(loads)))
    least = 1 if total - largest >= amount - 1 else 0
    given, rest = [largest] + [least] * (amount - 1), total - largest - least * (amount - 1)
    while rest > 0:
        movable = [i for i in range(1, amount) if given[i] < largest] or [i for i in range(1, amount) if given[i] < most]
        whole, left = sum([loads[i] for i in movable]), rest
        for i in movable:
            more = min(most - given[i], max(1, left * loads[i] // whole), rest)
            given[i] = given[i] + more
            rest = rest - more
    return np.array(given)


def scatter_about(stream_key, dims, spread, limit, pieces=(), kind=jnp.bfloat16):
    array = jax.random.normal(stream_key, dims, jnp.float32) * spread
    if len(pieces) > 0:
        array = steps_of(stream_key, dims, pieces, -0.22, 0.18) * array
    return jnp.clip(array, min=-limit, max=limit).astype(kind)


def setup_inputs(seed: int = 0) -> dict:
    seeds = jax.random.split(jax.random.key(seed), 7)
    tokens = scatter_about(seeds[0], (TOKENS, D), 1.0, 6.0, ((0, 64),))
    expert_ids_keys = jax.random.split(jax.random.fold_in(seeds[1], 1), TOKENS // TOK_DEV)
    expert_ids_turns = jax.random.permutation(jax.random.fold_in(seeds[1], 3), TOKENS // TOK_DEV)
    expert_ids = jax.vmap(lambda own, number: assign_block(jax.random.fold_in(seeds[1], 2), own, number, TOK_DEV, EXPERTS, TOPK, CAP, 1))(expert_ids_keys, expert_ids_turns).reshape((TOKENS, TOPK))
    gate_scale = jnp.clip(0.1 + 0.5 * jax.random.uniform(seeds[2], (TOKENS, TOPK), jnp.float32) ** steps_of(seeds[2], (TOKENS, TOPK), ((0, 64),), -0.2, 0.2), 0.1, 0.6)
    w_gate = scatter_about(seeds[3], (EXPERTS, D, FF), D ** -0.5, 0.09375, ((0, 64), (2, 8)))
    w_up = scatter_about(seeds[4], (EXPERTS, D, FF), D ** -0.5, 0.09375, ((0, 64), (2, 8)))
    w_down = scatter_about(seeds[5], (EXPERTS, FF, D), (FF // N_PIPE) ** -0.5, 0.5, ((0, 64), (1, 8)))
    return dict(tokens=tokens, expert_ids=expert_ids, gate_scale=gate_scale, w_gate=w_gate, w_up=w_up, w_down=w_down)


def reference(tokens, expert_ids, gate_scale, w_gate, w_up, w_down):
    total_pairs = TOKENS * TOPK
    flat_ids = expert_ids.reshape(-1)
    flat_scale = gate_scale.reshape(-1)
    most = N_EXPERT * CAP
    shard = FF // N_PIPE

    def one_expert(accum, index):
        chosen = jnp.nonzero(flat_ids == index, size=most, fill_value=total_pairs)[0].astype(jnp.int32)
        valid = chosen < total_pairs
        safe = jnp.minimum(chosen, total_pairs - 1).astype(jnp.int32)
        token_index = (safe // TOPK).astype(jnp.int32)
        rows = tokens[token_index]
        gate_all = w_gate[index]
        up_all = w_up[index]
        down_all = w_down[index]
        summed = jnp.zeros((most, D), jnp.float32)
        for part in range(N_PIPE):
            lower = part * shard
            gate_val = jnp.dot(rows, gate_all[:, lower:lower + shard], preferred_element_type=jnp.float32)
            up_val = jnp.dot(rows, up_all[:, lower:lower + shard], preferred_element_type=jnp.float32)
            hidden = (jax.nn.silu(gate_val) * up_val).astype(jnp.bfloat16)
            partial_out = jnp.dot(hidden, down_all[lower:lower + shard, :], preferred_element_type=jnp.float32).astype(jnp.bfloat16)
            summed = summed + partial_out.astype(jnp.float32)
        weight = jnp.where(valid, flat_scale[safe], jnp.float32(0.0))
        return accum.at[token_index].add(summed * weight[:, None]), None

    start = jnp.zeros((TOKENS, D), jnp.float32)
    accum, unused = lax.scan(one_expert, start, jnp.arange(EXPERTS, dtype=jnp.int32))
    return accum.astype(jnp.bfloat16)
```

```python
import jax
import jax.numpy as jnp
from jax import lax
from jax.experimental import pallas as pl
from jax.experimental.pallas import tpu as pltpu
from jax.sharding import PartitionSpec as P

BF = jnp.bfloat16
F32 = jnp.float32
LANES = 128
X = 4
VMEM = 56 * 1024 * 1024


def params():
    return pltpu.CompilerParams(vmem_limit_bytes=VMEM)


def in_vmem():
    return pl.BlockSpec(memory_space=pltpu.VMEM)


def in_hbm():
    return pl.BlockSpec(memory_space=pl.ANY)


def slots(ids, experts):
    tokens, topk = ids.shape
    lane = lax.broadcasted_iota(jnp.int32, (tokens, experts), 1)
    named = jnp.zeros((tokens, experts), F32)
    for k in range(topk):
        named += (ids[:, k : k + 1] == lane).astype(F32)
    row = lax.broadcasted_iota(jnp.int32, (tokens, tokens), 0)
    col = lax.broadcasted_iota(jnp.int32, (tokens, tokens), 1)
    contract = (((0,), (0,)), ((), ()))
    named = named.astype(BF)
    chosen = lax.dot_general(named, (row == col).astype(BF), contract, preferred_element_type=F32)
    place = lax.dot_general(named, (row < col).astype(BF), contract, preferred_element_type=F32)
    return jnp.where(chosen > 0.5, place, -1.0)


def at_slot(place, first, count, value):
    experts, tokens = place.shape
    if first is None:
        hit = jnp.broadcast_to((place == 16.0)[:, None, :], (experts, count, tokens))
    else:
        slot = lax.broadcasted_iota(jnp.int32, (experts, count, tokens), 1).astype(F32) + first
        hit = place[:, None, :] == slot
    return jnp.where(hit, value, 0.0).reshape(experts * count, tokens)


def dispatch_kernel(x_ref, ids_ref, tok_ref, out_ref):
    experts = out_ref.shape[0]
    tok = tok_ref[...]
    tiles = tok.shape[1] // LANES
    place = slots(ids_ref[...], experts)
    pick = at_slot(place, 0.0, 16, 1.0).astype(BF)
    rows = jnp.dot(pick, tok, preferred_element_type=F32).astype(BF)
    for c in range(tiles):
        out_ref[:, c * 16 : (c + 1) * 16, :] = rows[:, c * LANES : (c + 1) * LANES].reshape(experts, 16, LANES)
    last = at_slot(place, None, 8, 1.0)
    sub = lax.broadcasted_iota(jnp.int32, (experts, 8, tok.shape[0]), 1).reshape(last.shape)
    tail = jnp.zeros((experts * 8, LANES), F32)
    for c in range(tiles):
        mine = jnp.where(sub == c, last, 0.0).astype(BF)
        tail += jnp.dot(mine, tok[:, c * LANES : (c + 1) * LANES], preferred_element_type=F32)
    out_ref[:, tiles * 16 : tiles * 16 + 8, :] = tail.astype(BF).reshape(experts, 8, LANES)


def dispatch(x, ids, tokens, experts):
    count, width = tokens.shape
    quarter = width // X
    depth = quarter // LANES * 16 + 8
    return pl.pallas_call(
        dispatch_kernel,
        out_shape=jax.ShapeDtypeStruct((experts, depth, LANES), BF),
        grid_spec=pltpu.PrefetchScalarGridSpec(
            num_scalar_prefetch=1,
            grid=(1,),
            in_specs=[
                pl.BlockSpec(ids.shape, lambda i, x: (0, 0)),
                pl.BlockSpec((count, quarter), lambda i, x: (0, x[0])),
            ],
            out_specs=pl.BlockSpec((experts, depth, LANES), lambda i, x: (0, 0, 0)),
        ),
        compiler_params=params(),
        name="dispatch",
    )(x, ids, tokens)


def pack_kernel(x_ref, gate_ref, up_ref, down_ref, *rest):
    outs, sems = rest[:-1], rest[-1]
    quarter = gate_ref.shape[0] // X
    depth = down_ref.shape[0]
    copies = []

    def copy(src, dst):
        one = pltpu.make_async_copy(src, dst, sems.at[len(copies)])
        one.start()
        copies.append(one)

    for d, out in enumerate(outs, 1):
        q = lax.rem(x_ref[0] + d, X)
        part = pl.ds(pl.multiple_of(q * quarter, quarter), quarter)
        copy(gate_ref.at[part, :], out.at[pl.ds(0, quarter), :])
        copy(up_ref.at[part, :], out.at[pl.ds(quarter, quarter), :])
        for c in range(quarter // LANES):
            cols = pl.ds(pl.multiple_of(q * quarter + c * LANES, LANES), LANES)
            copy(down_ref.at[:, cols], out.at[pl.ds(2 * quarter + c * depth, depth), :])
    for one in copies:
        one.wait()


def pack(x, w_gate, w_up, w_down):
    quarter = w_gate.shape[0] // X
    rows = 2 * quarter + quarter // LANES * w_down.shape[0]
    shape = jax.ShapeDtypeStruct((rows, LANES), BF)
    count = (X - 1) * (2 + quarter // LANES)
    return pl.pallas_call(
        pack_kernel,
        out_shape=[shape] * (X - 1),
        in_specs=[pl.BlockSpec(memory_space=pltpu.SMEM)] + [in_hbm()] * 3,
        out_specs=[in_hbm()] * (X - 1),
        scratch_shapes=[pltpu.SemaphoreType.DMA((count,))],
        compiler_params=params(),
        name="pack",
    )(x, w_gate, w_up, w_down)


def stacked(chunks_ref):
    sources, depth, _ = chunks_ref.shape
    tiles = depth // 16
    main = [chunks_ref[:, c * 16 : (c + 1) * 16, :].reshape(sources * 16, LANES) for c in range(tiles)]
    tail = chunks_ref[:, tiles * 16 : tiles * 16 + 8, :].reshape(sources * 8, LANES)
    row = lax.broadcasted_iota(jnp.int32, (sources, sources * 8), 0)
    col = lax.broadcasted_iota(jnp.int32, (sources, sources * 8), 1)
    last = [
        jnp.dot((col == row * 8 + c).astype(BF), tail, preferred_element_type=F32).astype(BF) for c in range(tiles)
    ]
    return jnp.concatenate(main, axis=1), jnp.concatenate(last, axis=1)


def project_kernel(chunks_ref, gate_ref, up_ref, out_ref):
    main, last = stacked(chunks_ref)
    weight = jnp.concatenate([gate_ref[...], up_ref[...]], axis=1)
    count = main.shape[0]
    out_ref[pl.ds(0, count), :] = jnp.dot(main, weight, preferred_element_type=F32).astype(out_ref.dtype)
    out_ref[pl.ds(count, last.shape[0]), :] = jnp.dot(last, weight, preferred_element_type=F32).astype(out_ref.dtype)


def project(chunks, block, gate, up, gate_at, up_at, dtype):
    sources, depth, _ = chunks.shape
    quarter = depth // 16 * LANES

    def kernel(block_ref, *refs):
        project_kernel(*refs)

    return pl.pallas_call(
        kernel,
        out_shape=jax.ShapeDtypeStruct((sources * 17, 2 * LANES), dtype),
        grid_spec=pltpu.PrefetchScalarGridSpec(
            num_scalar_prefetch=1,
            grid=(1,),
            in_specs=[
                pl.BlockSpec(chunks.shape, lambda i, b: (0, 0, 0)),
                pl.BlockSpec((quarter, LANES), lambda i, b: (gate_at(b), 0)),
                pl.BlockSpec((quarter, LANES), lambda i, b: (up_at(b), 0)),
            ],
            out_specs=pl.BlockSpec((sources * 17, 2 * LANES), lambda i, b: (0, 0)),
        ),
        compiler_params=params(),
        name="project",
    )(block, chunks, gate, up)


def down_kernel(x_ref, own_ref, h1, h2, h3, p1, p2, p3, down_ref, out_ref):
    experts = out_ref.shape[0]
    hidden = jnp.concatenate([own_ref[...], h1[...], h2[...], h3[...]], axis=1)
    tiles = out_ref.shape[1] // 16
    depth = down_ref.shape[0]
    base = 2 * tiles * LANES
    main = hidden[: experts * 16]
    last = hidden[experts * 16 :]
    row = lax.broadcasted_iota(jnp.int32, (experts * 8, experts), 0)
    col = lax.broadcasted_iota(jnp.int32, (experts * 8, experts), 1)
    tail = jnp.zeros((experts * 8, LANES), F32)
    for c in range(tiles):
        rows = pl.ds(base + c * depth, depth)
        weight = jnp.concatenate(
            [down_ref[:, c * LANES : (c + 1) * LANES], p1[rows, :], p2[rows, :], p3[rows, :]], axis=0
        )
        out = jnp.dot(main, weight, preferred_element_type=F32).astype(BF)
        out_ref[:, c * 16 : (c + 1) * 16, :] = out.reshape(experts, 16, LANES)
        end = jnp.dot(last, weight, preferred_element_type=F32).astype(BF)
        tail += jnp.dot((row == col * 8 + c).astype(BF), end, preferred_element_type=F32)
    out_ref[:, tiles * 16 : tiles * 16 + 8, :] = tail.astype(BF).reshape(experts, 8, LANES)


def down(x, hiddens, packs, w_down, experts):
    depth, width = w_down.shape
    quarter = width // X
    chunk = quarter // LANES * 16 + 8
    whole = lambda a: pl.BlockSpec(a.shape, lambda i, x: (0, 0))
    return pl.pallas_call(
        down_kernel,
        out_shape=jax.ShapeDtypeStruct((experts, chunk, LANES), BF),
        grid_spec=pltpu.PrefetchScalarGridSpec(
            num_scalar_prefetch=1,
            grid=(1,),
            in_specs=[whole(a) for a in (*hiddens, *packs)]
            + [pl.BlockSpec((depth, quarter), lambda i, x: (0, x[0]))],
            out_specs=pl.BlockSpec((experts, chunk, LANES), lambda i, x: (0, 0, 0)),
        ),
        compiler_params=params(),
        name="down",
    )(x, *hiddens, *packs, w_down)


def combine_kernel(ids_ref, scale_ref, chunks_ref, out_ref):
    experts, depth, _ = chunks_ref.shape
    tiles = depth // 16
    ids, scale = ids_ref[...], scale_ref[...]
    tokens, topk = ids.shape
    place = slots(ids, experts)
    lane = lax.broadcasted_iota(jnp.int32, (tokens, experts), 1)
    weight = jnp.zeros((tokens, experts), F32)
    for k in range(topk):
        weight += jnp.where(ids[:, k : k + 1] == lane, scale[:, k : k + 1], 0.0)
    high = weight.astype(BF)
    low = (weight - high.astype(F32)).astype(BF)
    row = lax.broadcasted_iota(jnp.int32, (tokens, tokens), 0)
    col = lax.broadcasted_iota(jnp.int32, (tokens, tokens), 1)
    same = (row == col).astype(BF)
    contract = (((0,), (0,)), ((), ()))
    tail = chunks_ref[:, tiles * 16 : tiles * 16 + 8, :].reshape(experts * 8, LANES)
    sub = lax.broadcasted_iota(jnp.int32, (experts, 8, tokens), 1).reshape(experts * 8, tokens)
    main = jnp.concatenate(
        [chunks_ref[:, c * 16 : (c + 1) * 16, :].reshape(experts * 16, LANES) for c in range(tiles)], axis=1
    )
    total = jnp.zeros((tokens, tiles * LANES), F32)
    ends = [jnp.zeros((tokens, LANES), F32) for _ in range(tiles)]
    for part in (high, low):
        turned = lax.dot_general(part, same, contract, preferred_element_type=F32)
        coef = at_slot(place, 0.0, 16, turned[:, None, :]).astype(BF)
        total += lax.dot_general(coef, main, contract, preferred_element_type=F32)
        last = at_slot(place, None, 8, turned[:, None, :])
        for c in range(tiles):
            mine = jnp.where(sub == c, last, 0.0).astype(BF)
            ends[c] += lax.dot_general(mine, tail, contract, preferred_element_type=F32)
    out_ref[...] = (total + jnp.concatenate(ends, axis=1)).astype(out_ref.dtype)


def combine(ids, scale, chunks):
    tiles = chunks.shape[1] // 16
    return pl.pallas_call(
        combine_kernel,
        out_shape=jax.ShapeDtypeStruct((ids.shape[0], tiles * LANES), F32),
        in_specs=[in_vmem()] * 3,
        out_specs=in_vmem(),
        compiler_params=params(),
        name="combine",
    )(ids, scale, chunks)


def turn(d):
    return [(z * X + x, z * X + (x + d) % X) for z in range(2) for x in range(X)]


def body(tokens, expert_ids, gate_scale, w_gate, w_up, w_down):
    groups = lax.axis_size("expert")
    x = lax.rem(lax.axis_index("pipe"), X)
    xs = x.reshape(1)
    w_gate, w_up, w_down = w_gate[0], w_up[0], w_down[0]
    packed = pack(xs, w_gate, w_up, w_down)
    packs = [lax.ppermute(packed[d - 1], "pipe", turn(d)) for d in range(1, X)]
    buffer = dispatch(xs, expert_ids, tokens, groups)
    chunks = lax.all_to_all(buffer, "expert", split_axis=0, concat_axis=0, tiled=True)
    arrived = {}
    for d in (2, 1, 3):
        pk = packs[d - 1]
        part = project(chunks, xs, pk, pk, lambda b: 0, lambda b: 1, BF)
        arrived[d] = lax.ppermute(part, "pipe", turn(-d))
    own = project(chunks, xs, w_gate, w_up, lambda b: b[0], lambda b: b[0], F32)
    summed = own + arrived[1].astype(F32) + arrived[2].astype(F32) + arrived[3].astype(F32)
    hidden = (jax.nn.silu(summed[:, :LANES]) * summed[:, LANES:]).astype(BF)
    hiddens = [hidden] + [lax.ppermute(hidden, "pipe", turn(d)) for d in (1, 2, 3)]
    output = down(xs, hiddens, packs, w_down, groups)
    returned = lax.all_to_all(output, "expert", split_axis=0, concat_axis=0, tiled=True)
    mixed = combine(expert_ids, gate_scale, returned)
    half = mixed.shape[1] // 2
    z = lax.axis_index("pipe") // X
    first = jnp.where(z == 0, mixed[:, :half], mixed[:, half:])
    second = jnp.where(z == 0, mixed[:, half:], mixed[:, :half])
    to_first = [(z * X + x, 2 * x + z) for z in range(2) for x in range(X)]
    to_second = [(z * X + x, 2 * x + 1 - z) for z in range(2) for x in range(X)]
    a = lax.ppermute(first.astype(BF), "pipe", to_first)
    b = lax.ppermute(second.astype(BF), "pipe", to_second)
    return (a.astype(F32) + b.astype(F32)).astype(BF)


def solution(mesh):
    placed = (
        P("expert", None),
        P("expert", None),
        P("expert", None),
        P("expert", None, "pipe"),
        P("expert", None, "pipe"),
        P("expert", "pipe", None),
    )
    return jax.shard_map(
        body, mesh=mesh, in_specs=placed, out_specs=P("expert", "pipe"), check_vma=False
    )
```

```python
import jax
import jax.numpy as jnp
from jax import lax
from jax.experimental import pallas as pl
from jax.experimental.pallas import tpu as pltpu
from jax.sharding import PartitionSpec as P

BF = jnp.bfloat16
F32 = jnp.float32
LANES = 128
X = 4
VMEM = 24 * 1024 * 1024


def call(kernel, name, out_shape, in_specs, out_specs=None):
    if out_specs is None:
        out_specs = jax.tree.map(lambda _: in_vmem(), out_shape)
    return pl.pallas_call(
        kernel,
        out_shape=out_shape,
        in_specs=in_specs,
        out_specs=out_specs,
        compiler_params=pltpu.CompilerParams(vmem_limit_bytes=VMEM),
        name=name,
    )


def in_vmem():
    return pl.BlockSpec(memory_space=pltpu.VMEM)


def in_smem():
    return pl.BlockSpec(memory_space=pltpu.SMEM)


def slots(ids, experts):
    topk, tokens = ids.shape
    lane = lax.broadcasted_iota(jnp.int32, (experts, tokens), 0)
    named = jnp.zeros((experts, tokens), F32)
    for k in range(topk):
        named += (ids[k : k + 1, :] == lane).astype(F32)
    row = lax.broadcasted_iota(jnp.int32, (tokens, tokens), 0)
    col = lax.broadcasted_iota(jnp.int32, (tokens, tokens), 1)
    place = jnp.dot(named.astype(BF), (row < col).astype(BF), preferred_element_type=F32)
    return jnp.where(named > 0.5, place, -1.0)


def spread(tiles, rows):
    count = tiles[0].shape[0]
    sub = lax.broadcasted_iota(jnp.int32, (count, rows, LANES), 1)
    out = jnp.zeros((count, rows, LANES), F32)
    for c, tile in enumerate(tiles):
        out += jnp.where(sub == c, tile[:, None, :], 0.0)
    return out


def dispatch_kernel(x_ref, ids_ref, tok_ref, out_ref):
    experts = out_ref.shape[0]
    tokens, width = tok_ref.shape
    tiles = width // X // LANES
    quarter = width // X
    tok = tok_ref[:, pl.ds(pl.multiple_of(x_ref[0] * quarter, LANES), quarter)]
    place = slots(ids_ref[...], experts)
    slot = lax.broadcasted_iota(jnp.int32, (experts, 16, tokens), 1).astype(F32)
    pick = jnp.where(place[:, None, :] == slot, 1.0, 0.0).reshape(experts * 16, tokens).astype(BF)
    rows = jnp.dot(pick, tok, preferred_element_type=F32).astype(BF)
    for c in range(tiles):
        out_ref[:, c * 16 : (c + 1) * 16, :] = rows[:, c * LANES : (c + 1) * LANES].reshape(experts, 16, LANES)
    last = jnp.dot((place == 16.0).astype(BF), tok, preferred_element_type=F32)
    tail = spread([last[:, c * LANES : (c + 1) * LANES] for c in range(tiles)], 8)
    out_ref[:, tiles * 16 : tiles * 16 + 8, :] = tail.astype(BF)


def dispatch(x, ids, tokens, experts):
    depth = tokens.shape[1] // X // LANES * 16 + 8
    shape = jax.ShapeDtypeStruct((experts, depth, LANES), BF)
    return call(dispatch_kernel, "dispatch", shape, [in_smem(), in_vmem(), in_vmem()])(x, ids, tokens)


def pack_kernel(x_ref, gate_ref, up_ref, down_ref, *outs):
    quarter = gate_ref.shape[0] // X
    depth = down_ref.shape[0]

    def put_down(out, base, q):
        for z in range(2):
            p = z * X + q
            pair, odd = p // 2, lax.rem(p, 2)
            first = pair * (quarter // LANES) + 4 * odd
            half = pair * (quarter // LANES) + 3
            for c in range(4):
                tile = half if c == 3 else first + c
                cols = pl.ds(pl.multiple_of(tile * LANES, LANES), LANES)
                out[pl.ds(base + (z * 4 + c) * depth, depth), :] = down_ref[:, cols]

    for d, out in enumerate(outs[1:], 1):
        q = lax.rem(x_ref[0] + d, X)
        part = pl.ds(pl.multiple_of(q * quarter, quarter), quarter)
        out[pl.ds(0, quarter), :] = gate_ref[part, :]
        out[pl.ds(quarter, quarter), :] = up_ref[part, :]
        put_down(out, 2 * quarter, q)
    put_down(outs[0], 0, x_ref[0])


def pack(x, w_gate, w_up, w_down):
    depth = w_down.shape[0]
    rows = 2 * (w_gate.shape[0] // X) + 8 * depth
    shapes = [jax.ShapeDtypeStruct((r, LANES), BF) for r in [8 * depth] + [rows] * (X - 1)]
    return call(pack_kernel, "pack", shapes, [in_smem()] + [in_vmem()] * 3)(x, w_gate, w_up, w_down)


def swap_kernel(z_ref, own_ref, p1, p2, p3, out_ref):
    rows = own_ref.shape[0] // 2
    start = (1 - z_ref[0]) * rows
    for d, ref in enumerate((own_ref, p1, p2, p3)):
        base = ref.shape[0] - 2 * rows
        out_ref[pl.ds(d * rows, rows), :] = ref[pl.ds(pl.multiple_of(base + start, LANES), rows), :]


def swap(z, own, packs):
    shape = jax.ShapeDtypeStruct((X * own.shape[0] // 2, LANES), BF)
    return call(swap_kernel, "swap", shape, [in_smem()] + [in_vmem()] * 4)(z, own, *packs)


def stacked(chunks_ref):
    sources, depth, _ = chunks_ref.shape
    tiles = depth // 16
    main = [chunks_ref[:, c * 16 : (c + 1) * 16, :].reshape(sources * 16, LANES) for c in range(tiles)]
    tail = chunks_ref[:, tiles * 16 : tiles * 16 + 8, :].reshape(sources * 8, LANES)
    row = lax.broadcasted_iota(jnp.int32, (sources, sources * 8), 0)
    col = lax.broadcasted_iota(jnp.int32, (sources, sources * 8), 1)
    last = [
        jnp.dot((col == row * 8 + c).astype(BF), tail, preferred_element_type=F32).astype(BF) for c in range(tiles)
    ]
    return jnp.concatenate(main, axis=1), jnp.concatenate(last, axis=1)


def project_into(out_ref, main, last, gate, up):
    weight = jnp.concatenate([gate, up], axis=1)
    count = main.shape[0]
    out_ref[pl.ds(0, count), :] = jnp.dot(main, weight, preferred_element_type=F32).astype(out_ref.dtype)
    out_ref[pl.ds(count, last.shape[0]), :] = jnp.dot(last, weight, preferred_element_type=F32).astype(out_ref.dtype)


def project_sent_kernel(chunks_ref, *refs):
    main, last = stacked(chunks_ref)
    quarter = main.shape[1]
    for pack_ref, out_ref in zip(refs[: X - 1], refs[X - 1 :]):
        project_into(out_ref, main, last, pack_ref[pl.ds(0, quarter), :], pack_ref[pl.ds(quarter, quarter), :])


def project_sent(chunks, packs):
    shapes = [jax.ShapeDtypeStruct((chunks.shape[0] * 17, 2 * LANES), BF)] * len(packs)
    return call(project_sent_kernel, "project_sent", shapes, [in_vmem()] * (1 + len(packs)))(chunks, *packs)


def project_own_kernel(x_ref, chunks_ref, gate_ref, up_ref, out_ref):
    main, last = stacked(chunks_ref)
    quarter = main.shape[1]
    part = pl.ds(pl.multiple_of(x_ref[0] * quarter, quarter), quarter)
    project_into(out_ref, main, last, gate_ref[part, :], up_ref[part, :])


def project_own(x, chunks, gate, up):
    shape = jax.ShapeDtypeStruct((chunks.shape[0] * 17, 2 * LANES), F32)
    return call(project_own_kernel, "project_own", shape, [in_smem()] + [in_vmem()] * 3)(x, chunks, gate, up)


def down_kernel(x_ref, z_ref, *refs):
    hiddens, (own_ref, p1, p2, p3, other_ref, out_ref) = refs[: 2 * X], refs[2 * X :]
    experts = out_ref.shape[0]
    rows = own_ref.shape[0] // 2
    depth = rows // 4
    hidden = jnp.concatenate([ref[...] for ref in hiddens], axis=1)
    blocks = []
    for ref in (own_ref, p1, p2, p3):
        base = ref.shape[0] - 2 * rows + z_ref[0] * rows
        tiles = [ref[pl.ds(pl.multiple_of(base + c * depth, LANES), depth), :] for c in range(4)]
        blocks.append(jnp.concatenate(tiles, axis=1))
    for d in range(X):
        tiles = [other_ref[pl.ds(d * rows + c * depth, depth), :] for c in range(4)]
        blocks.append(jnp.concatenate(tiles, axis=1))
    weight = jnp.concatenate(blocks, axis=0)
    count = experts * 16
    main = jnp.dot(hidden[:count], weight, preferred_element_type=F32)
    last = jnp.dot(hidden[count:], weight, preferred_element_type=F32)
    for c in range(3):
        out_ref[:, c * 16 : (c + 1) * 16, :] = (
            main[:, c * LANES : (c + 1) * LANES].astype(BF).reshape(experts, 16, LANES)
        )
    half = main[:, 3 * LANES :]
    turned = pltpu.roll(half, LANES // 2, 1)
    odd = lax.rem(x_ref[0], 2) == 1
    low = jnp.where(odd, turned, half).reshape(experts, 16, LANES)[:, :8]
    high = jnp.where(odd, half, turned).reshape(experts, 16, LANES)[:, 8:]
    lane = lax.broadcasted_iota(jnp.int32, low.shape, 2)
    halves = jnp.where(lane < LANES // 2, low, high)
    tail = spread([last[:, c * LANES : (c + 1) * LANES] for c in range(4)], 8)
    out_ref[:, 48:64, :] = jnp.concatenate([halves, tail], axis=1).astype(BF)


def down(x, z, hiddens, own, packs, other, experts):
    shape = jax.ShapeDtypeStruct((experts, 64, LANES), BF)
    specs = [in_smem()] * 2 + [in_vmem()] * (2 * X + X + 1)
    return call(down_kernel, "down", shape, specs)(x, z, *hiddens, own, *packs, other)


def combine_kernel(x_ref, ids_ref, scale_ref, chunks_ref, out_ref):
    experts = chunks_ref.shape[0]
    ids, scale = ids_ref[...], scale_ref[...]
    topk, tokens = ids.shape
    place = slots(ids, experts)
    lane = lax.broadcasted_iota(jnp.int32, (experts, tokens), 0)
    weight = jnp.zeros((experts, tokens), F32)
    for k in range(topk):
        weight += jnp.where(ids[k : k + 1, :] == lane, scale[k : k + 1, :], 0.0)
    upper = weight.astype(BF).astype(F32)
    lower = weight - upper
    sub = lax.broadcasted_iota(jnp.int32, (experts, 16, tokens), 1)
    slot = sub.astype(F32)
    place = place[:, None, :]
    contract = (((0,), (0,)), ((), ()))
    main = jnp.concatenate(
        [chunks_ref[:, c * 16 : (c + 1) * 16, :].reshape(experts * 16, LANES) for c in range(3)], axis=1
    )
    rest = chunks_ref[:, 48:64, :].reshape(experts * 16, LANES)
    whole = jnp.zeros((tokens, 3 * LANES), F32)
    low = jnp.zeros((tokens, LANES), F32)
    high = jnp.zeros((tokens, LANES), F32)
    ends = [jnp.zeros((tokens, LANES), F32) for _ in range(4)]

    def times(hit, part, rows):
        coef = jnp.where(hit, part[:, None, :], 0.0).reshape(experts * 16, tokens).astype(BF)
        return lax.dot_general(coef, rows, contract, preferred_element_type=F32)

    for part in (upper, lower):
        whole += times(place == slot, part, main)
        low += times((place == slot) & (sub < 8), part, rest)
        high += times((place == slot + 8.0) & (sub < 8), part, rest)
        for c in range(4):
            ends[c] += times((place == 16.0) & (sub == 8 + c), part, rest)
    odd = lax.rem(x_ref[0], 2) == 1
    even_half = low + pltpu.roll(high, LANES // 2, 1) + ends[3]
    odd_half = pltpu.roll(low, LANES // 2, 1) + high + ends[3]
    half = jnp.where(odd, odd_half, even_half)
    total = jnp.concatenate([whole + jnp.concatenate(ends[:3], axis=1), half], axis=1)
    total = jnp.where(odd, pltpu.roll(total, LANES // 2, 1), total)
    out_ref[...] = total[:, : out_ref.shape[1]].astype(BF)


def combine(x, ids, scale, chunks, columns):
    shape = jax.ShapeDtypeStruct((ids.shape[1], columns), BF)
    return call(combine_kernel, "combine", shape, [in_smem()] + [in_vmem()] * 3)(x, ids, scale, chunks)


def shift(value, d):
    pairs = [(z * X + x, z * X + (x + d) % X) for z in range(2) for x in range(X)]
    return lax.ppermute(value, "pipe", pairs)


def cross(value):
    return lax.ppermute(value, "pipe", [(p, (p + X) % (2 * X)) for p in range(2 * X)])


def body(tokens, expert_ids, gate_scale, w_gate, w_up, w_down):
    groups = lax.axis_size("expert")
    pipe = lax.axis_index("pipe")
    x = (pipe & (X - 1)).reshape(1)
    z = (pipe >> 2).reshape(1)
    ids, scale = expert_ids.T, gate_scale.T
    w_gate, w_up, w_down = w_gate[0], w_up[0], w_down[0]
    buffer = dispatch(x, ids, tokens, groups)
    chunks = lax.all_to_all(buffer, "expert", split_axis=0, concat_axis=0, tiled=True)
    own_down, *sent = pack(x, w_gate, w_up, w_down)
    packs = [shift(sent[d - 1], d) for d in range(1, X)]
    other_down = cross(swap(z, own_down, packs))
    parts = project_sent(chunks, packs)
    arrived = [shift(parts[d - 1], -d) for d in (2, 1, 3)]
    summed = project_own(x, chunks, w_gate, w_up)
    for part in arrived:
        summed = summed + part.astype(F32)
    hidden = (jax.nn.silu(summed[:, :LANES]) * summed[:, LANES:]).astype(BF)
    swapped = cross(hidden)
    hiddens = [hidden] + [shift(hidden, d) for d in range(1, X)]
    hiddens += [swapped] + [shift(swapped, d) for d in range(1, X)]
    output = down(x, z, hiddens, own_down, packs, other_down, groups)
    returned = lax.all_to_all(output, "expert", split_axis=0, concat_axis=0, tiled=True)
    return combine(x, ids, scale, returned, tokens.shape[1] // (2 * X))


def solution(mesh):
    placed = (
        P("expert", None),
        P("expert", None),
        P("expert", None),
        P("expert", None, "pipe"),
        P("expert", None, "pipe"),
        P("expert", "pipe", None),
    )
    return jax.shard_map(
        body, mesh=mesh, in_specs=placed, out_specs=P("expert", "pipe"), check_vma=False
    )
```

```python
import jax
import jax.numpy as jnp
from jax import lax
from jax.experimental import pallas as pl
from jax.experimental.pallas import tpu as pltpu
from jax.sharding import PartitionSpec as P

BF = jnp.bfloat16
F32 = jnp.float32
LANES = 128
X = 4
VMEM = 24 * 1024 * 1024


def call(kernel, name, out_shape, in_specs, out_specs=None):
    if out_specs is None:
        out_specs = jax.tree.map(lambda _: in_vmem(), out_shape)
    return pl.pallas_call(
        kernel,
        out_shape=out_shape,
        in_specs=in_specs,
        out_specs=out_specs,
        compiler_params=pltpu.CompilerParams(vmem_limit_bytes=VMEM),
        name=name,
    )


def in_vmem():
    return pl.BlockSpec(memory_space=pltpu.VMEM)


def in_smem():
    return pl.BlockSpec(memory_space=pltpu.SMEM)


def slots(ids, experts):
    topk, tokens = ids.shape
    lane = lax.broadcasted_iota(jnp.int32, (experts, tokens), 0)
    named = jnp.zeros((experts, tokens), F32)
    for k in range(topk):
        named += (ids[k : k + 1, :] == lane).astype(F32)
    row = lax.broadcasted_iota(jnp.int32, (tokens, tokens), 0)
    col = lax.broadcasted_iota(jnp.int32, (tokens, tokens), 1)
    place = jnp.dot(named.astype(BF), (row < col).astype(BF), preferred_element_type=F32)
    return jnp.where(named > 0.5, place, -1.0)


def spread(tiles, rows):
    count = tiles[0].shape[0]
    sub = lax.broadcasted_iota(jnp.int32, (count, rows, LANES), 1)
    out = jnp.zeros((count, rows, LANES), F32)
    for c, tile in enumerate(tiles):
        out += jnp.where(sub == c, tile[:, None, :], 0.0)
    return out


def dispatch_kernel(x_ref, ids_ref, tok_ref, out_ref):
    experts = out_ref.shape[0]
    tokens, width = tok_ref.shape
    tiles = width // X // LANES
    quarter = width // X
    tok = tok_ref[:, pl.ds(pl.multiple_of(x_ref[0] * quarter, LANES), quarter)]
    place = slots(ids_ref[...], experts)
    slot = lax.broadcasted_iota(jnp.int32, (experts, 16, tokens), 1).astype(F32)
    pick = jnp.where(place[:, None, :] == slot, 1.0, 0.0).reshape(experts * 16, tokens).astype(BF)
    rows = jnp.dot(pick, tok, preferred_element_type=F32).astype(BF)
    for c in range(tiles):
        out_ref[:, c * 16 : (c + 1) * 16, :] = rows[:, c * LANES : (c + 1) * LANES].reshape(experts, 16, LANES)
    last = jnp.dot((place == 16.0).astype(BF), tok, preferred_element_type=F32)
    tail = spread([last[:, c * LANES : (c + 1) * LANES] for c in range(tiles)], 8)
    out_ref[:, tiles * 16 : tiles * 16 + 8, :] = tail.astype(BF)


def dispatch(x, ids, tokens, experts):
    depth = tokens.shape[1] // X // LANES * 16 + 8
    shape = jax.ShapeDtypeStruct((experts, depth, LANES), BF)
    return call(dispatch_kernel, "dispatch", shape, [in_smem(), in_vmem(), in_vmem()])(x, ids, tokens)


def pack_kernel(x_ref, gate_ref, up_ref, down_ref, *outs):
    quarter = gate_ref.shape[0] // X
    depth = down_ref.shape[0]

    def put_down(out, base, q):
        for z in range(2):
            p = z * X + q
            pair, odd = p // 2, lax.rem(p, 2)
            first = pair * (quarter // LANES) + 4 * odd
            half = pair * (quarter // LANES) + 3
            for c in range(4):
                tile = half if c == 3 else first + c
                cols = pl.ds(pl.multiple_of(tile * LANES, LANES), LANES)
                out[pl.ds(base + (z * 4 + c) * depth, depth), :] = down_ref[:, cols]

    for d, out in enumerate(outs[1:], 1):
        q = lax.rem(x_ref[0] + d, X)
        part = pl.ds(pl.multiple_of(q * quarter, quarter), quarter)
        out[pl.ds(0, quarter), :] = gate_ref[part, :]
        out[pl.ds(quarter, quarter), :] = up_ref[part, :]
        put_down(out, 2 * quarter, q)
    put_down(outs[0], 0, x_ref[0])


def pack(x, w_gate, w_up, w_down):
    depth = w_down.shape[0]
    rows = 2 * (w_gate.shape[0] // X) + 8 * depth
    shapes = [jax.ShapeDtypeStruct((r, LANES), BF) for r in [8 * depth] + [rows] * (X - 1)]
    return call(pack_kernel, "pack", shapes, [in_smem()] + [in_vmem()] * 3)(x, w_gate, w_up, w_down)


def swap_kernel(z_ref, own_ref, p1, p2, p3, out_ref):
    rows = own_ref.shape[0] // 2
    start = (1 - z_ref[0]) * rows
    for d, ref in enumerate((own_ref, p1, p2, p3)):
        base = ref.shape[0] - 2 * rows
        out_ref[pl.ds(d * rows, rows), :] = ref[pl.ds(pl.multiple_of(base + start, LANES), rows), :]


def swap(z, own, packs):
    shape = jax.ShapeDtypeStruct((X * own.shape[0] // 2, LANES), BF)
    return call(swap_kernel, "swap", shape, [in_smem()] + [in_vmem()] * 4)(z, own, *packs)


def stacked(chunks_ref):
    sources, depth, _ = chunks_ref.shape
    tiles = depth // 16
    main = [chunks_ref[:, c * 16 : (c + 1) * 16, :].reshape(sources * 16, LANES) for c in range(tiles)]
    tail = chunks_ref[:, tiles * 16 : tiles * 16 + 8, :].reshape(sources * 8, LANES)
    row = lax.broadcasted_iota(jnp.int32, (sources, sources * 8), 0)
    col = lax.broadcasted_iota(jnp.int32, (sources, sources * 8), 1)
    last = [
        jnp.dot((col == row * 8 + c).astype(BF), tail, preferred_element_type=F32).astype(BF) for c in range(tiles)
    ]
    return jnp.concatenate(main, axis=1), jnp.concatenate(last, axis=1)


def project_into(out_ref, main, last, gate, up):
    weight = jnp.concatenate([gate, up], axis=1)
    count = main.shape[0]
    out_ref[pl.ds(0, count), :] = jnp.dot(main, weight, preferred_element_type=F32).astype(out_ref.dtype)
    out_ref[pl.ds(count, last.shape[0]), :] = jnp.dot(last, weight, preferred_element_type=F32).astype(out_ref.dtype)


def project_kernel(x_ref, chunks_ref, gate_ref, up_ref, *refs):
    packs, out_ref = refs[:-1], refs[-1]
    main, last = stacked(chunks_ref)
    quarter = main.shape[1]
    x = x_ref[0]
    for d, pack_ref in enumerate(packs, 1):
        gate, up = pack_ref[pl.ds(0, quarter), :], pack_ref[pl.ds(quarter, quarter), :]
        project_into(out_ref.at[lax.rem(x + X - d, X)], main, last, gate, up)
    part = pl.ds(pl.multiple_of(x * quarter, quarter), quarter)
    project_into(out_ref.at[x], main, last, gate_ref[part, :], up_ref[part, :])


def project(x, chunks, gate, up, packs):
    shape = jax.ShapeDtypeStruct((X, chunks.shape[0] * 17, 2 * LANES), BF)
    return call(project_kernel, "project", shape, [in_smem()] + [in_vmem()] * (3 + len(packs)))(
        x, chunks, gate, up, *packs
    )


def activate_kernel(parts_ref, out_ref):
    total = parts_ref[0].astype(F32)
    for d in range(1, X):
        total += parts_ref[d].astype(F32)
    gate, up = total[:, :LANES], total[:, LANES:]
    out_ref[...] = (gate / (1.0 + jnp.exp(-gate)) * up).astype(BF)


def activate(parts):
    shape = jax.ShapeDtypeStruct((parts.shape[1], LANES), BF)
    return call(activate_kernel, "activate", shape, [in_vmem()])(parts)


def down_kernel(x_ref, z_ref, *refs):
    near_ref, far_ref, own_ref, p1, p2, p3, other_ref, out_ref = refs
    experts = out_ref.shape[0]
    rows = own_ref.shape[0] // 2
    depth = rows // 4
    source = [lax.rem(x_ref[0] + X - d, X) for d in range(X)]
    hidden = jnp.concatenate([ref[s] for ref in (near_ref, far_ref) for s in source], axis=1)
    blocks = []
    for ref in (own_ref, p1, p2, p3):
        base = ref.shape[0] - 2 * rows + z_ref[0] * rows
        tiles = [ref[pl.ds(pl.multiple_of(base + c * depth, LANES), depth), :] for c in range(4)]
        blocks.append(jnp.concatenate(tiles, axis=1))
    for d in range(X):
        tiles = [other_ref[pl.ds(d * rows + c * depth, depth), :] for c in range(4)]
        blocks.append(jnp.concatenate(tiles, axis=1))
    weight = jnp.concatenate(blocks, axis=0)
    count = experts * 16
    main = jnp.dot(hidden[:count], weight, preferred_element_type=F32)
    last = jnp.dot(hidden[count:], weight, preferred_element_type=F32)
    for c in range(3):
        out_ref[:, c * 16 : (c + 1) * 16, :] = (
            main[:, c * LANES : (c + 1) * LANES].astype(BF).reshape(experts, 16, LANES)
        )
    half = main[:, 3 * LANES :]
    turned = pltpu.roll(half, LANES // 2, 1)
    odd = lax.rem(x_ref[0], 2) == 1
    low = jnp.where(odd, turned, half).reshape(experts, 16, LANES)[:, :8]
    high = jnp.where(odd, half, turned).reshape(experts, 16, LANES)[:, 8:]
    lane = lax.broadcasted_iota(jnp.int32, low.shape, 2)
    halves = jnp.where(lane < LANES // 2, low, high)
    tail = spread([last[:, c * LANES : (c + 1) * LANES] for c in range(4)], 8)
    out_ref[:, 48:64, :] = jnp.concatenate([halves, tail], axis=1).astype(BF)


def down(x, z, near, far, own, packs, other, experts):
    shape = jax.ShapeDtypeStruct((experts, 64, LANES), BF)
    specs = [in_smem()] * 2 + [in_vmem()] * (X + 3)
    return call(down_kernel, "down", shape, specs)(x, z, near, far, own, *packs, other)


def combine_kernel(x_ref, ids_ref, scale_ref, chunks_ref, out_ref):
    experts = chunks_ref.shape[0]
    ids, scale = ids_ref[...], scale_ref[...]
    topk, tokens = ids.shape
    place = slots(ids, experts)
    lane = lax.broadcasted_iota(jnp.int32, (experts, tokens), 0)
    weight = jnp.zeros((experts, tokens), F32)
    for k in range(topk):
        weight += jnp.where(ids[k : k + 1, :] == lane, scale[k : k + 1, :], 0.0)
    upper = weight.astype(BF).astype(F32)
    lower = weight - upper
    sub = lax.broadcasted_iota(jnp.int32, (experts, 16, tokens), 1)
    slot = sub.astype(F32)
    place = place[:, None, :]
    contract = (((0,), (0,)), ((), ()))
    main = jnp.concatenate(
        [chunks_ref[:, c * 16 : (c + 1) * 16, :].reshape(experts * 16, LANES) for c in range(3)], axis=1
    )
    rest = chunks_ref[:, 48:64, :].reshape(experts * 16, LANES)
    whole = jnp.zeros((tokens, 3 * LANES), F32)
    low = jnp.zeros((tokens, LANES), F32)
    high = jnp.zeros((tokens, LANES), F32)
    ends = [jnp.zeros((tokens, LANES), F32) for _ in range(4)]

    def times(hit, part, rows):
        coef = jnp.where(hit, part[:, None, :], 0.0).reshape(experts * 16, tokens).astype(BF)
        return lax.dot_general(coef, rows, contract, preferred_element_type=F32)

    for part in (upper, lower):
        whole += times(place == slot, part, main)
        low += times((place == slot) & (sub < 8), part, rest)
        high += times((place == slot + 8.0) & (sub < 8), part, rest)
        for c in range(4):
            ends[c] += times((place == 16.0) & (sub == 8 + c), part, rest)
    odd = lax.rem(x_ref[0], 2) == 1
    even_half = low + pltpu.roll(high, LANES // 2, 1) + ends[3]
    odd_half = pltpu.roll(low, LANES // 2, 1) + high + ends[3]
    half = jnp.where(odd, odd_half, even_half)
    total = jnp.concatenate([whole + jnp.concatenate(ends[:3], axis=1), half], axis=1)
    total = jnp.where(odd, pltpu.roll(total, LANES // 2, 1), total)
    out_ref[...] = total[:, : out_ref.shape[1]].astype(BF)


def combine(x, ids, scale, chunks, columns):
    shape = jax.ShapeDtypeStruct((ids.shape[1], columns), BF)
    return call(combine_kernel, "combine", shape, [in_smem()] + [in_vmem()] * 3)(x, ids, scale, chunks)


def shift(value, d):
    pairs = [(z * X + x, z * X + (x + d) % X) for z in range(2) for x in range(X)]
    return lax.ppermute(value, "pipe", pairs)


def cross(value):
    return lax.ppermute(value, "pipe", [(p, (p + X) % (2 * X)) for p in range(2 * X)])


def across(value):
    groups = [[z * X + x for x in range(X)] for z in range(2)]
    return lax.all_to_all(value, "pipe", split_axis=0, concat_axis=0, axis_index_groups=groups, tiled=True)


def body(tokens, expert_ids, gate_scale, w_gate, w_up, w_down):
    groups = lax.axis_size("expert")
    pipe = lax.axis_index("pipe")
    x = (pipe & (X - 1)).reshape(1)
    z = (pipe >> 2).reshape(1)
    ids, scale = expert_ids.T, gate_scale.T
    w_gate, w_up, w_down = w_gate[0], w_up[0], w_down[0]
    buffer = dispatch(x, ids, tokens, groups)
    chunks = lax.all_to_all(buffer, "expert", split_axis=0, concat_axis=0, tiled=True)
    own_down, *sent = pack(x, w_gate, w_up, w_down)
    packs = [shift(sent[d - 1], d) for d in range(1, X)]
    other_down = cross(swap(z, own_down, packs))
    arrived = across(project(x, chunks, w_gate, w_up, packs))
    hidden = activate(arrived)
    swapped = cross(hidden)
    near = across(jnp.broadcast_to(hidden[None], (X, *hidden.shape)))
    far = across(jnp.broadcast_to(swapped[None], (X, *swapped.shape)))
    output = down(x, z, near, far, own_down, packs, other_down, groups)
    returned = lax.all_to_all(output, "expert", split_axis=0, concat_axis=0, tiled=True)
    return combine(x, ids, scale, returned, tokens.shape[1] // (2 * X))


def solution(mesh):
    placed = (
        P("expert", None),
        P("expert", None),
        P("expert", None),
        P("expert", None, "pipe"),
        P("expert", None, "pipe"),
        P("expert", "pipe", None),
    )
    return jax.shard_map(
        body, mesh=mesh, in_specs=placed, out_specs=P("expert", "pipe"), check_vma=False
    )
```

```python
import jax
import jax.numpy as jnp
from jax import lax
from jax.experimental import pallas as pl
from jax.experimental.pallas import tpu as pltpu
from jax.sharding import PartitionSpec as P

BF = jnp.bfloat16
F32 = jnp.float32
LANES = 128
X = 4
VMEM = 24 * 1024 * 1024


def call(kernel, name, out_shape, in_specs, out_specs=None):
    if out_specs is None:
        out_specs = jax.tree.map(lambda _: in_vmem(), out_shape)
    return pl.pallas_call(
        kernel,
        out_shape=out_shape,
        in_specs=in_specs,
        out_specs=out_specs,
        compiler_params=pltpu.CompilerParams(vmem_limit_bytes=VMEM),
        name=name,
    )


def in_vmem():
    return pl.BlockSpec(memory_space=pltpu.VMEM)


def in_smem():
    return pl.BlockSpec(memory_space=pltpu.SMEM)


def slots(ids, experts):
    topk, tokens = ids.shape
    lane = lax.broadcasted_iota(jnp.int32, (experts, tokens), 0)
    named = jnp.zeros((experts, tokens), F32)
    for k in range(topk):
        named += (ids[k : k + 1, :] == lane).astype(F32)
    row = lax.broadcasted_iota(jnp.int32, (tokens, tokens), 0)
    col = lax.broadcasted_iota(jnp.int32, (tokens, tokens), 1)
    place = jnp.dot(named.astype(BF), (row < col).astype(BF), preferred_element_type=F32)
    return jnp.where(named > 0.5, place, -1.0)


def spread(tiles, rows):
    count = tiles[0].shape[0]
    sub = lax.broadcasted_iota(jnp.int32, (count, rows, LANES), 1)
    out = jnp.zeros((count, rows, LANES), F32)
    for c, tile in enumerate(tiles):
        out += jnp.where(sub == c, tile[:, None, :], 0.0)
    return out


def dispatch_kernel(x_ref, ids_ref, tok_ref, out_ref):
    experts = out_ref.shape[0]
    tokens, width = tok_ref.shape
    tiles = width // X // LANES
    quarter = width // X
    tok = tok_ref[:, pl.ds(pl.multiple_of(x_ref[0] * quarter, LANES), quarter)]
    place = slots(ids_ref[...], experts)
    slot = lax.broadcasted_iota(jnp.int32, (experts, 16, tokens), 1).astype(F32)
    pick = jnp.where(place[:, None, :] == slot, 1.0, 0.0).reshape(experts * 16, tokens).astype(BF)
    rows = jnp.dot(pick, tok, preferred_element_type=F32).astype(BF)
    for c in range(tiles):
        out_ref[:, c * 16 : (c + 1) * 16, :] = rows[:, c * LANES : (c + 1) * LANES].reshape(experts, 16, LANES)
    last = jnp.dot((place == 16.0).astype(BF), tok, preferred_element_type=F32)
    tail = spread([last[:, c * LANES : (c + 1) * LANES] for c in range(tiles)], 8)
    out_ref[:, tiles * 16 : tiles * 16 + 8, :] = tail.astype(BF)


def dispatch(x, ids, tokens, experts):
    depth = tokens.shape[1] // X // LANES * 16 + 8
    shape = jax.ShapeDtypeStruct((experts, depth, LANES), BF)
    return call(dispatch_kernel, "dispatch", shape, [in_smem(), in_vmem(), in_vmem()])(x, ids, tokens)


def pack_kernel(x_ref, gate_ref, up_ref, down_ref, *outs):
    quarter = gate_ref.shape[0] // X
    depth = down_ref.shape[0]

    def put_down(out, base, q):
        for z in range(2):
            p = z * X + q
            pair, odd = p // 2, lax.rem(p, 2)
            first = pair * (quarter // LANES) + 4 * odd
            half = pair * (quarter // LANES) + 3
            for c in range(4):
                tile = half if c == 3 else first + c
                cols = pl.ds(pl.multiple_of(tile * LANES, LANES), LANES)
                out[pl.ds(base + (z * 4 + c) * depth, depth), :] = down_ref[:, cols]

    for d, out in enumerate(outs[1:], 1):
        q = lax.rem(x_ref[0] + d, X)
        part = pl.ds(pl.multiple_of(q * quarter, quarter), quarter)
        out[pl.ds(0, quarter), :] = gate_ref[part, :]
        out[pl.ds(quarter, quarter), :] = up_ref[part, :]
        put_down(out, 2 * quarter, q)
    put_down(outs[0], 0, x_ref[0])


def pack(x, w_gate, w_up, w_down):
    depth = w_down.shape[0]
    rows = 2 * (w_gate.shape[0] // X) + 8 * depth
    shapes = [jax.ShapeDtypeStruct((r, LANES), BF) for r in [8 * depth] + [rows] * (X - 1)]
    return call(pack_kernel, "pack", shapes, [in_smem()] + [in_vmem()] * 3)(x, w_gate, w_up, w_down)


def swap_kernel(z_ref, own_ref, p1, p2, p3, out_ref):
    rows = own_ref.shape[0] // 2
    start = (1 - z_ref[0]) * rows
    for d, ref in enumerate((own_ref, p1, p2, p3)):
        base = ref.shape[0] - 2 * rows
        out_ref[pl.ds(d * rows, rows), :] = ref[pl.ds(pl.multiple_of(base + start, LANES), rows), :]


def swap(z, own, packs):
    shape = jax.ShapeDtypeStruct((X * own.shape[0] // 2, LANES), BF)
    return call(swap_kernel, "swap", shape, [in_smem()] + [in_vmem()] * 4)(z, own, *packs)


def stacked(chunks_ref):
    sources, depth, _ = chunks_ref.shape
    tiles = depth // 16
    main = [chunks_ref[:, c * 16 : (c + 1) * 16, :].reshape(sources * 16, LANES) for c in range(tiles)]
    tail = chunks_ref[:, tiles * 16 : tiles * 16 + 8, :].reshape(sources * 8, LANES)
    row = lax.broadcasted_iota(jnp.int32, (sources, sources * 8), 0)
    col = lax.broadcasted_iota(jnp.int32, (sources, sources * 8), 1)
    last = [
        jnp.dot((col == row * 8 + c).astype(BF), tail, preferred_element_type=F32).astype(BF) for c in range(tiles)
    ]
    return jnp.concatenate(main, axis=1), jnp.concatenate(last, axis=1)


def project_into(out_ref, main, last, gate, up):
    weight = jnp.concatenate([gate, up], axis=1)
    count = main.shape[0]
    out_ref[pl.ds(0, count), :] = jnp.dot(main, weight, preferred_element_type=F32).astype(out_ref.dtype)
    out_ref[pl.ds(count, last.shape[0]), :] = jnp.dot(last, weight, preferred_element_type=F32).astype(out_ref.dtype)


def project_sent_kernel(chunks_ref, *refs):
    main, last = stacked(chunks_ref)
    quarter = main.shape[1]
    for pack_ref, out_ref in zip(refs[: X - 1], refs[X - 1 :]):
        project_into(out_ref, main, last, pack_ref[pl.ds(0, quarter), :], pack_ref[pl.ds(quarter, quarter), :])


def project_sent(chunks, packs):
    shapes = [jax.ShapeDtypeStruct((chunks.shape[0] * 17, 2 * LANES), BF)] * len(packs)
    return call(project_sent_kernel, "project_sent", shapes, [in_vmem()] * (1 + len(packs)))(chunks, *packs)


def project_own_kernel(x_ref, chunks_ref, gate_ref, up_ref, out_ref):
    main, last = stacked(chunks_ref)
    quarter = main.shape[1]
    part = pl.ds(pl.multiple_of(x_ref[0] * quarter, quarter), quarter)
    project_into(out_ref, main, last, gate_ref[part, :], up_ref[part, :])


def project_own(x, chunks, gate, up):
    shape = jax.ShapeDtypeStruct((chunks.shape[0] * 17, 2 * LANES), F32)
    return call(project_own_kernel, "project_own", shape, [in_smem()] + [in_vmem()] * 3)(x, chunks, gate, up)


def down_kernel(x_ref, z_ref, *refs):
    hiddens, (own_ref, p1, p2, p3, other_ref, out_ref) = refs[: 2 * X], refs[2 * X :]
    experts = out_ref.shape[0]
    rows = own_ref.shape[0] // 2
    depth = rows // 4
    hidden = jnp.concatenate([ref[...] for ref in hiddens], axis=1)
    blocks = []
    for ref in (own_ref, p1, p2, p3):
        base = ref.shape[0] - 2 * rows + z_ref[0] * rows
        tiles = [ref[pl.ds(pl.multiple_of(base + c * depth, LANES), depth), :] for c in range(4)]
        blocks.append(jnp.concatenate(tiles, axis=1))
    for d in range(X):
        tiles = [other_ref[pl.ds(d * rows + c * depth, depth), :] for c in range(4)]
        blocks.append(jnp.concatenate(tiles, axis=1))
    weight = jnp.concatenate(blocks, axis=0)
    count = experts * 16
    main = jnp.dot(hidden[:count], weight, preferred_element_type=F32)
    last = jnp.dot(hidden[count:], weight, preferred_element_type=F32)
    for c in range(3):
        out_ref[:, c * 16 : (c + 1) * 16, :] = (
            main[:, c * LANES : (c + 1) * LANES].astype(BF).reshape(experts, 16, LANES)
        )
    half = main[:, 3 * LANES :]
    turned = pltpu.roll(half, LANES // 2, 1)
    odd = lax.rem(x_ref[0], 2) == 1
    low = jnp.where(odd, turned, half).reshape(experts, 16, LANES)[:, :8]
    high = jnp.where(odd, half, turned).reshape(experts, 16, LANES)[:, 8:]
    lane = lax.broadcasted_iota(jnp.int32, low.shape, 2)
    halves = jnp.where(lane < LANES // 2, low, high)
    tail = spread([last[:, c * LANES : (c + 1) * LANES] for c in range(4)], 8)
    out_ref[:, 48:64, :] = jnp.concatenate([halves, tail], axis=1).astype(BF)


def down(x, z, hiddens, own, packs, other, experts):
    shape = jax.ShapeDtypeStruct((experts, 64, LANES), BF)
    specs = [in_smem()] * 2 + [in_vmem()] * (2 * X + X + 1)
    return call(down_kernel, "down", shape, specs)(x, z, *hiddens, own, *packs, other)


def combine_kernel(x_ref, ids_ref, scale_ref, chunks_ref, out_ref):
    experts = chunks_ref.shape[0]
    ids, scale = ids_ref[...], scale_ref[...]
    topk, tokens = ids.shape
    place = slots(ids, experts)
    lane = lax.broadcasted_iota(jnp.int32, (experts, tokens), 0)
    weight = jnp.zeros((experts, tokens), F32)
    for k in range(topk):
        weight += jnp.where(ids[k : k + 1, :] == lane, scale[k : k + 1, :], 0.0)
    upper = weight.astype(BF).astype(F32)
    lower = weight - upper
    sub = lax.broadcasted_iota(jnp.int32, (experts, 16, tokens), 1)
    slot = sub.astype(F32)
    place = place[:, None, :]
    contract = (((0,), (0,)), ((), ()))
    main = jnp.concatenate(
        [chunks_ref[:, c * 16 : (c + 1) * 16, :].reshape(experts * 16, LANES) for c in range(3)], axis=1
    )
    rest = chunks_ref[:, 48:64, :].reshape(experts * 16, LANES)
    whole = jnp.zeros((tokens, 3 * LANES), F32)
    low = jnp.zeros((tokens, LANES), F32)
    high = jnp.zeros((tokens, LANES), F32)
    ends = [jnp.zeros((tokens, LANES), F32) for _ in range(4)]

    def times(hit, part, rows):
        coef = jnp.where(hit, part[:, None, :], 0.0).reshape(experts * 16, tokens).astype(BF)
        return lax.dot_general(coef, rows, contract, preferred_element_type=F32)

    for part in (upper, lower):
        whole += times(place == slot, part, main)
        low += times((place == slot) & (sub < 8), part, rest)
        high += times((place == slot + 8.0) & (sub < 8), part, rest)
        for c in range(4):
            ends[c] += times((place == 16.0) & (sub == 8 + c), part, rest)
    odd = lax.rem(x_ref[0], 2) == 1
    even_half = low + pltpu.roll(high, LANES // 2, 1) + ends[3]
    odd_half = pltpu.roll(low, LANES // 2, 1) + high + ends[3]
    half = jnp.where(odd, odd_half, even_half)
    total = jnp.concatenate([whole + jnp.concatenate(ends[:3], axis=1), half], axis=1)
    total = jnp.where(odd, pltpu.roll(total, LANES // 2, 1), total)
    out_ref[...] = total[:, : out_ref.shape[1]].astype(BF)


def combine(x, ids, scale, chunks, columns):
    shape = jax.ShapeDtypeStruct((ids.shape[1], columns), BF)
    return call(combine_kernel, "combine", shape, [in_smem()] + [in_vmem()] * 3)(x, ids, scale, chunks)


def shift(value, d):
    pairs = [(z * X + x, z * X + (x + d) % X) for z in range(2) for x in range(X)]
    return lax.ppermute(value, "pipe", pairs)


def cross(value):
    return lax.ppermute(value, "pipe", [(p, (p + X) % (2 * X)) for p in range(2 * X)])


def body(tokens, expert_ids, gate_scale, w_gate, w_up, w_down):
    groups = lax.axis_size("expert")
    pipe = lax.axis_index("pipe")
    x = (pipe & (X - 1)).reshape(1)
    z = (pipe >> 2).reshape(1)
    ids, scale = expert_ids.T, gate_scale.T
    w_gate, w_up, w_down = w_gate[0], w_up[0], w_down[0]
    buffer = dispatch(x, ids, tokens, groups)
    chunks = lax.all_to_all(buffer, "expert", split_axis=0, concat_axis=0, tiled=True)
    own_down, *sent = pack(x, w_gate, w_up, w_down)
    packs = [shift(sent[d - 1], d) for d in range(1, X)]
    other_down = cross(swap(z, own_down, packs))
    parts = project_sent(chunks, packs)
    arrived = [shift(parts[d - 1], -d) for d in (2, 1, 3)]
    chunks, other_down = lax.optimization_barrier((chunks, other_down))
    summed = project_own(x, chunks, w_gate, w_up)
    for part in arrived:
        summed = summed + part.astype(F32)
    hidden = (jax.nn.silu(summed[:, :LANES]) * summed[:, LANES:]).astype(BF)
    swapped = cross(hidden)
    hiddens = [hidden] + [shift(hidden, d) for d in range(1, X)]
    hiddens += [swapped] + [shift(swapped, d) for d in range(1, X)]
    output = down(x, z, hiddens, own_down, packs, other_down, groups)
    returned = lax.all_to_all(output, "expert", split_axis=0, concat_axis=0, tiled=True)
    return combine(x, ids, scale, returned, tokens.shape[1] // (2 * X))


def solution(mesh):
    placed = (
        P("expert", None),
        P("expert", None),
        P("expert", None),
        P("expert", None, "pipe"),
        P("expert", None, "pipe"),
        P("expert", "pipe", None),
    )
    return jax.shard_map(
        body, mesh=mesh, in_specs=placed, out_specs=P("expert", "pipe"), check_vma=False
    )
```

```python
import jax
import jax.numpy as jnp
from jax import lax
from jax.experimental import pallas as pl
from jax.experimental.pallas import tpu as pltpu
from jax.sharding import PartitionSpec as P

BF = jnp.bfloat16
F32 = jnp.float32
LANES = 128
X = 4
VMEM = 24 * 1024 * 1024


def call(kernel, name, out_shape, in_specs, out_specs=None):
    if out_specs is None:
        out_specs = jax.tree.map(lambda _: in_vmem(), out_shape)
    return pl.pallas_call(
        kernel,
        out_shape=out_shape,
        in_specs=in_specs,
        out_specs=out_specs,
        compiler_params=pltpu.CompilerParams(vmem_limit_bytes=VMEM),
        name=name,
    )


def in_vmem():
    return pl.BlockSpec(memory_space=pltpu.VMEM)


def in_smem():
    return pl.BlockSpec(memory_space=pltpu.SMEM)


def slots(ids, experts):
    topk, tokens = ids.shape
    lane = lax.broadcasted_iota(jnp.int32, (experts, tokens), 0)
    named = jnp.zeros((experts, tokens), F32)
    for k in range(topk):
        named += (ids[k : k + 1, :] == lane).astype(F32)
    row = lax.broadcasted_iota(jnp.int32, (tokens, tokens), 0)
    col = lax.broadcasted_iota(jnp.int32, (tokens, tokens), 1)
    place = jnp.dot(named.astype(BF), (row < col).astype(BF), preferred_element_type=F32)
    return jnp.where(named > 0.5, place, -1.0)


def spread(tiles, rows):
    count = tiles[0].shape[0]
    sub = lax.broadcasted_iota(jnp.int32, (count, rows, LANES), 1)
    out = jnp.zeros((count, rows, LANES), F32)
    for c, tile in enumerate(tiles):
        out += jnp.where(sub == c, tile[:, None, :], 0.0)
    return out


def dispatch_kernel(x_ref, ids_ref, tok_ref, out_ref):
    experts = out_ref.shape[0]
    tokens, width = tok_ref.shape
    tiles = width // X // LANES
    quarter = width // X
    tok = tok_ref[:, pl.ds(pl.multiple_of(x_ref[0] * quarter, LANES), quarter)]
    place = slots(ids_ref[...], experts)
    slot = lax.broadcasted_iota(jnp.int32, (experts, 16, tokens), 1).astype(F32)
    pick = jnp.where(place[:, None, :] == slot, 1.0, 0.0).reshape(experts * 16, tokens).astype(BF)
    rows = jnp.dot(pick, tok, preferred_element_type=F32).astype(BF)
    for c in range(tiles):
        out_ref[:, c * 16 : (c + 1) * 16, :] = rows[:, c * LANES : (c + 1) * LANES].reshape(experts, 16, LANES)
    last = jnp.dot((place == 16.0).astype(BF), tok, preferred_element_type=F32)
    tail = spread([last[:, c * LANES : (c + 1) * LANES] for c in range(tiles)], 8)
    out_ref[:, tiles * 16 : tiles * 16 + 8, :] = tail.astype(BF)


def dispatch(x, ids, tokens, experts):
    depth = tokens.shape[1] // X // LANES * 16 + 8
    shape = jax.ShapeDtypeStruct((experts, depth, LANES), BF)
    return call(dispatch_kernel, "dispatch", shape, [in_smem(), in_vmem(), in_vmem()])(x, ids, tokens)


def pack_kernel(x_ref, gate_ref, up_ref, down_ref, *outs):
    quarter = gate_ref.shape[0] // X
    depth = down_ref.shape[0]

    def put_down(out, base, q):
        for z in range(2):
            p = z * X + q
            pair, odd = p // 2, lax.rem(p, 2)
            first = pair * (quarter // LANES) + 4 * odd
            half = pair * (quarter // LANES) + 3
            for c in range(4):
                tile = half if c == 3 else first + c
                cols = pl.ds(pl.multiple_of(tile * LANES, LANES), LANES)
                out[pl.ds(base + (z * 4 + c) * depth, depth), :] = down_ref[:, cols]

    for d, out in enumerate(outs[1:], 1):
        q = lax.rem(x_ref[0] + d, X)
        part = pl.ds(pl.multiple_of(q * quarter, quarter), quarter)
        out[pl.ds(0, quarter), :] = gate_ref[part, :]
        out[pl.ds(quarter, quarter), :] = up_ref[part, :]
        put_down(out, 2 * quarter, q)
    put_down(outs[0], 0, x_ref[0])


def pack(x, w_gate, w_up, w_down):
    depth = w_down.shape[0]
    rows = 2 * (w_gate.shape[0] // X) + 8 * depth
    shapes = [jax.ShapeDtypeStruct((r, LANES), BF) for r in [8 * depth] + [rows] * (X - 1)]
    return call(pack_kernel, "pack", shapes, [in_smem()] + [in_vmem()] * 3)(x, w_gate, w_up, w_down)


def swap_kernel(z_ref, own_ref, p1, p2, p3, out_ref):
    rows = own_ref.shape[0] // 2
    start = (1 - z_ref[0]) * rows
    for d, ref in enumerate((own_ref, p1, p2, p3)):
        base = ref.shape[0] - 2 * rows
        out_ref[pl.ds(d * rows, rows), :] = ref[pl.ds(pl.multiple_of(base + start, LANES), rows), :]


def swap(z, own, packs):
    shape = jax.ShapeDtypeStruct((X * own.shape[0] // 2, LANES), BF)
    return call(swap_kernel, "swap", shape, [in_smem()] + [in_vmem()] * 4)(z, own, *packs)


def stacked(chunks_ref):
    sources, depth, _ = chunks_ref.shape
    tiles = depth // 16
    main = [chunks_ref[:, c * 16 : (c + 1) * 16, :].reshape(sources * 16, LANES) for c in range(tiles)]
    tail = chunks_ref[:, tiles * 16 : tiles * 16 + 8, :].reshape(sources * 8, LANES)
    row = lax.broadcasted_iota(jnp.int32, (sources, sources * 8), 0)
    col = lax.broadcasted_iota(jnp.int32, (sources, sources * 8), 1)
    last = [
        jnp.dot((col == row * 8 + c).astype(BF), tail, preferred_element_type=F32).astype(BF) for c in range(tiles)
    ]
    return jnp.concatenate(main, axis=1), jnp.concatenate(last, axis=1)


def project_into(out_ref, main, last, gate, up):
    weight = jnp.concatenate([gate, up], axis=1)
    count = main.shape[0]
    out_ref[pl.ds(0, count), :] = jnp.dot(main, weight, preferred_element_type=F32).astype(out_ref.dtype)
    out_ref[pl.ds(count, last.shape[0]), :] = jnp.dot(last, weight, preferred_element_type=F32).astype(out_ref.dtype)


def project_kernel(x_ref, chunks_ref, gate_ref, up_ref, *refs):
    packs, out_ref = refs[:-1], refs[-1]
    main, last = stacked(chunks_ref)
    quarter = main.shape[1]
    x = x_ref[0]
    for d, pack_ref in enumerate(packs, 1):
        gate, up = pack_ref[pl.ds(0, quarter), :], pack_ref[pl.ds(quarter, quarter), :]
        project_into(out_ref.at[lax.rem(x + X - d, X)], main, last, gate, up)
    part = pl.ds(pl.multiple_of(x * quarter, quarter), quarter)
    project_into(out_ref.at[x], main, last, gate_ref[part, :], up_ref[part, :])


def project(x, chunks, gate, up, packs):
    shape = jax.ShapeDtypeStruct((X, chunks.shape[0] * 17, 2 * LANES), BF)
    return call(project_kernel, "project", shape, [in_smem()] + [in_vmem()] * (3 + len(packs)))(
        x, chunks, gate, up, *packs
    )


def activate_kernel(parts_ref, out_ref):
    total = parts_ref[0].astype(F32)
    for d in range(1, X):
        total += parts_ref[d].astype(F32)
    gate, up = total[:, :LANES], total[:, LANES:]
    out_ref[...] = (gate / (1.0 + jnp.exp(-gate)) * up).astype(BF)


def activate(parts):
    shape = jax.ShapeDtypeStruct((parts.shape[1], LANES), BF)
    return call(activate_kernel, "activate", shape, [in_vmem()])(parts)


def down_kernel(x_ref, z_ref, *refs):
    hiddens, (own_ref, p1, p2, p3, other_ref, out_ref) = refs[: 2 * X], refs[2 * X :]
    experts = out_ref.shape[0]
    rows = own_ref.shape[0] // 2
    depth = rows // 4
    hidden = jnp.concatenate([ref[...] for ref in hiddens], axis=1)
    blocks = []
    for ref in (own_ref, p1, p2, p3):
        base = ref.shape[0] - 2 * rows + z_ref[0] * rows
        tiles = [ref[pl.ds(pl.multiple_of(base + c * depth, LANES), depth), :] for c in range(4)]
        blocks.append(jnp.concatenate(tiles, axis=1))
    for d in range(X):
        tiles = [other_ref[pl.ds(d * rows + c * depth, depth), :] for c in range(4)]
        blocks.append(jnp.concatenate(tiles, axis=1))
    weight = jnp.concatenate(blocks, axis=0)
    count = experts * 16
    main = jnp.dot(hidden[:count], weight, preferred_element_type=F32)
    last = jnp.dot(hidden[count:], weight, preferred_element_type=F32)
    for c in range(3):
        out_ref[:, c * 16 : (c + 1) * 16, :] = (
            main[:, c * LANES : (c + 1) * LANES].astype(BF).reshape(experts, 16, LANES)
        )
    half = main[:, 3 * LANES :]
    turned = pltpu.roll(half, LANES // 2, 1)
    odd = lax.rem(x_ref[0], 2) == 1
    low = jnp.where(odd, turned, half).reshape(experts, 16, LANES)[:, :8]
    high = jnp.where(odd, half, turned).reshape(experts, 16, LANES)[:, 8:]
    lane = lax.broadcasted_iota(jnp.int32, low.shape, 2)
    halves = jnp.where(lane < LANES // 2, low, high)
    tail = spread([last[:, c * LANES : (c + 1) * LANES] for c in range(4)], 8)
    out_ref[:, 48:64, :] = jnp.concatenate([halves, tail], axis=1).astype(BF)


def down(x, z, hiddens, own, packs, other, experts):
    shape = jax.ShapeDtypeStruct((experts, 64, LANES), BF)
    specs = [in_smem()] * 2 + [in_vmem()] * (2 * X + X + 1)
    return call(down_kernel, "down", shape, specs)(x, z, *hiddens, own, *packs, other)


def combine_kernel(x_ref, ids_ref, scale_ref, chunks_ref, out_ref):
    experts = chunks_ref.shape[0]
    ids, scale = ids_ref[...], scale_ref[...]
    topk, tokens = ids.shape
    place = slots(ids, experts)
    lane = lax.broadcasted_iota(jnp.int32, (experts, tokens), 0)
    weight = jnp.zeros((experts, tokens), F32)
    for k in range(topk):
        weight += jnp.where(ids[k : k + 1, :] == lane, scale[k : k + 1, :], 0.0)
    upper = weight.astype(BF).astype(F32)
    lower = weight - upper
    sub = lax.broadcasted_iota(jnp.int32, (experts, 16, tokens), 1)
    slot = sub.astype(F32)
    place = place[:, None, :]
    contract = (((0,), (0,)), ((), ()))
    main = jnp.concatenate(
        [chunks_ref[:, c * 16 : (c + 1) * 16, :].reshape(experts * 16, LANES) for c in range(3)], axis=1
    )
    rest = chunks_ref[:, 48:64, :].reshape(experts * 16, LANES)
    whole = jnp.zeros((tokens, 3 * LANES), F32)
    low = jnp.zeros((tokens, LANES), F32)
    high = jnp.zeros((tokens, LANES), F32)
    ends = [jnp.zeros((tokens, LANES), F32) for _ in range(4)]

    def times(hit, part, rows):
        coef = jnp.where(hit, part[:, None, :], 0.0).reshape(experts * 16, tokens).astype(BF)
        return lax.dot_general(coef, rows, contract, preferred_element_type=F32)

    for part in (upper, lower):
        whole += times(place == slot, part, main)
        low += times((place == slot) & (sub < 8), part, rest)
        high += times((place == slot + 8.0) & (sub < 8), part, rest)
        for c in range(4):
            ends[c] += times((place == 16.0) & (sub == 8 + c), part, rest)
    odd = lax.rem(x_ref[0], 2) == 1
    even_half = low + pltpu.roll(high, LANES // 2, 1) + ends[3]
    odd_half = pltpu.roll(low, LANES // 2, 1) + high + ends[3]
    half = jnp.where(odd, odd_half, even_half)
    total = jnp.concatenate([whole + jnp.concatenate(ends[:3], axis=1), half], axis=1)
    total = jnp.where(odd, pltpu.roll(total, LANES // 2, 1), total)
    out_ref[...] = total[:, : out_ref.shape[1]].astype(BF)


def combine(x, ids, scale, chunks, columns):
    shape = jax.ShapeDtypeStruct((ids.shape[1], columns), BF)
    return call(combine_kernel, "combine", shape, [in_smem()] + [in_vmem()] * 3)(x, ids, scale, chunks)


def shift(value, d):
    pairs = [(z * X + x, z * X + (x + d) % X) for z in range(2) for x in range(X)]
    return lax.ppermute(value, "pipe", pairs)


def cross(value):
    return lax.ppermute(value, "pipe", [(p, (p + X) % (2 * X)) for p in range(2 * X)])


def across(value):
    groups = [[z * X + x for x in range(X)] for z in range(2)]
    return lax.all_to_all(value, "pipe", split_axis=0, concat_axis=0, axis_index_groups=groups, tiled=True)


def body(tokens, expert_ids, gate_scale, w_gate, w_up, w_down):
    groups = lax.axis_size("expert")
    pipe = lax.axis_index("pipe")
    x = (pipe & (X - 1)).reshape(1)
    z = (pipe >> 2).reshape(1)
    ids, scale = expert_ids.T, gate_scale.T
    w_gate, w_up, w_down = w_gate[0], w_up[0], w_down[0]
    buffer = dispatch(x, ids, tokens, groups)
    chunks = lax.all_to_all(buffer, "expert", split_axis=0, concat_axis=0, tiled=True)
    own_down, *sent = pack(x, w_gate, w_up, w_down)
    packs = [shift(sent[d - 1], d) for d in range(1, X)]
    other_down = cross(swap(z, own_down, packs))
    arrived = across(project(x, chunks, w_gate, w_up, packs))
    arrived, other_down = lax.optimization_barrier((arrived, other_down))
    hidden = activate(arrived)
    swapped = cross(hidden)
    hiddens = [hidden] + [shift(hidden, d) for d in range(1, X)]
    hiddens += [swapped] + [shift(swapped, d) for d in range(1, X)]
    output = down(x, z, hiddens, own_down, packs, other_down, groups)
    returned = lax.all_to_all(output, "expert", split_axis=0, concat_axis=0, tiled=True)
    return combine(x, ids, scale, returned, tokens.shape[1] // (2 * X))


def solution(mesh):
    placed = (
        P("expert", None),
        P("expert", None),
        P("expert", None),
        P("expert", None, "pipe"),
        P("expert", None, "pipe"),
        P("expert", "pipe", None),
    )
    return jax.shard_map(
        body, mesh=mesh, in_specs=placed, out_specs=P("expert", "pipe"), check_vma=False
    )
```

```python
import jax
import jax.numpy as jnp
from jax import lax
from jax.experimental import pallas as pl
from jax.experimental.pallas import tpu as pltpu
from jax.sharding import PartitionSpec as P

BF = jnp.bfloat16
F32 = jnp.float32
LANES = 128
X = 4
VMEM = 12 * 1024 * 1024


def call(kernel, name, out_shape, in_specs, out_specs=None):
    if out_specs is None:
        out_specs = jax.tree.map(lambda _: in_vmem(), out_shape)
    return pl.pallas_call(
        kernel,
        out_shape=out_shape,
        in_specs=in_specs,
        out_specs=out_specs,
        compiler_params=pltpu.CompilerParams(vmem_limit_bytes=VMEM),
        name=name,
    )


def in_vmem():
    return pl.BlockSpec(memory_space=pltpu.VMEM)


def in_smem():
    return pl.BlockSpec(memory_space=pltpu.SMEM)


def slots(ids, experts):
    topk, tokens = ids.shape
    lane = lax.broadcasted_iota(jnp.int32, (experts, tokens), 0)
    named = jnp.zeros((experts, tokens), F32)
    for k in range(topk):
        named += (ids[k : k + 1, :] == lane).astype(F32)
    row = lax.broadcasted_iota(jnp.int32, (tokens, tokens), 0)
    col = lax.broadcasted_iota(jnp.int32, (tokens, tokens), 1)
    place = jnp.dot(named.astype(BF), (row < col).astype(BF), preferred_element_type=F32)
    return jnp.where(named > 0.5, place, -1.0)


def spread(tiles, rows):
    count = tiles[0].shape[0]
    sub = lax.broadcasted_iota(jnp.int32, (count, rows, LANES), 1)
    out = jnp.zeros((count, rows, LANES), F32)
    for c, tile in enumerate(tiles):
        out += jnp.where(sub == c, tile[:, None, :], 0.0)
    return out


def dispatch_kernel(x_ref, ids_ref, tok_ref, out_ref):
    experts = out_ref.shape[0]
    tokens, width = tok_ref.shape
    tiles = width // X // LANES
    quarter = width // X
    tok = tok_ref[:, pl.ds(pl.multiple_of(x_ref[0] * quarter, LANES), quarter)]
    place = slots(ids_ref[...], experts)
    slot = lax.broadcasted_iota(jnp.int32, (experts, 16, tokens), 1).astype(F32)
    pick = jnp.where(place[:, None, :] == slot, 1.0, 0.0).reshape(experts * 16, tokens).astype(BF)
    rows = jnp.dot(pick, tok, preferred_element_type=F32).astype(BF)
    for c in range(tiles):
        out_ref[:, c * 16 : (c + 1) * 16, :] = rows[:, c * LANES : (c + 1) * LANES].reshape(experts, 16, LANES)
    last = jnp.dot((place == 16.0).astype(BF), tok, preferred_element_type=F32)
    tail = spread([last[:, c * LANES : (c + 1) * LANES] for c in range(tiles)], 8)
    out_ref[:, tiles * 16 : tiles * 16 + 8, :] = tail.astype(BF)


def dispatch(x, ids, tokens, experts):
    depth = tokens.shape[1] // X // LANES * 16 + 8
    shape = jax.ShapeDtypeStruct((experts, depth, LANES), BF)
    return call(dispatch_kernel, "dispatch", shape, [in_smem(), in_vmem(), in_vmem()])(x, ids, tokens)


def pack_kernel(x_ref, gate_ref, up_ref, down_ref, *outs):
    quarter = gate_ref.shape[0] // X
    depth = down_ref.shape[0]

    def put_down(out, base, q):
        for z in range(2):
            p = z * X + q
            pair, odd = p // 2, lax.rem(p, 2)
            first = pair * (quarter // LANES) + 4 * odd
            half = pair * (quarter // LANES) + 3
            for c in range(4):
                tile = half if c == 3 else first + c
                cols = pl.ds(pl.multiple_of(tile * LANES, LANES), LANES)
                out[pl.ds(base + (z * 4 + c) * depth, depth), :] = down_ref[:, cols]

    for d, out in enumerate(outs):
        q = lax.rem(x_ref[0] + d, X)
        part = pl.ds(pl.multiple_of(q * quarter, quarter), quarter)
        out[pl.ds(0, quarter), :] = gate_ref[part, :]
        out[pl.ds(quarter, quarter), :] = up_ref[part, :]
        put_down(out, 2 * quarter, q)


def pack(x, w_gate, w_up, w_down):
    depth = w_down.shape[0]
    rows = 2 * (w_gate.shape[0] // X) + 8 * depth
    shapes = [jax.ShapeDtypeStruct((r, LANES), BF) for r in [rows] * X]
    return call(pack_kernel, "pack", shapes, [in_smem()] + [in_vmem()] * 3)(x, w_gate, w_up, w_down)


def swap_kernel(z_ref, own_ref, p1, p2, p3, out_ref):
    rows = out_ref.shape[0] // X
    start = (1 - z_ref[0]) * rows
    for d, ref in enumerate((own_ref, p1, p2, p3)):
        base = ref.shape[0] - 2 * rows
        out_ref[pl.ds(d * rows, rows), :] = ref[pl.ds(pl.multiple_of(base + start, LANES), rows), :]


def swap(z, own, packs):
    shape = jax.ShapeDtypeStruct((X * 4 * LANES, LANES), BF)
    return call(swap_kernel, "swap", shape, [in_smem()] + [in_vmem()] * 4)(z, own, *packs)


def stacked(chunks_ref):
    sources, depth, _ = chunks_ref.shape
    tiles = depth // 16
    main = [chunks_ref[:, c * 16 : (c + 1) * 16, :].reshape(sources * 16, LANES) for c in range(tiles)]
    tail = chunks_ref[:, tiles * 16 : tiles * 16 + 8, :].reshape(sources * 8, LANES)
    row = lax.broadcasted_iota(jnp.int32, (sources, sources * 8), 0)
    col = lax.broadcasted_iota(jnp.int32, (sources, sources * 8), 1)
    last = [
        jnp.dot((col == row * 8 + c).astype(BF), tail, preferred_element_type=F32).astype(BF) for c in range(tiles)
    ]
    return jnp.concatenate(main, axis=1), jnp.concatenate(last, axis=1)


def project_into(out_ref, main, last, gate, up):
    weight = jnp.concatenate([gate, up], axis=1)
    count = main.shape[0]
    out_ref[pl.ds(0, count), :] = jnp.dot(main, weight, preferred_element_type=F32).astype(out_ref.dtype)
    out_ref[pl.ds(count, last.shape[0]), :] = jnp.dot(last, weight, preferred_element_type=F32).astype(out_ref.dtype)


def project_kernel(x_ref, chunks_ref, *refs):
    packs, (out_ref, rows_ref, sems) = refs[:X], refs[X:]
    main, last = stacked(chunks_ref)
    quarter = main.shape[1]
    copies = []
    for d, pack_ref in enumerate(packs):
        gate, up = pack_ref[pl.ds(0, quarter), :], pack_ref[pl.ds(quarter, quarter), :]
        project_into(rows_ref.at[d], main, last, gate, up)
        copies.append(pltpu.make_async_copy(rows_ref.at[d], out_ref.at[lax.rem(x_ref[0] + X - d, X)], sems.at[d]))
        copies[d].start()
    for copy in copies:
        copy.wait()


def project(x, chunks, packs):
    shape = (X, chunks.shape[0] * 17, 2 * LANES)
    return pl.pallas_call(
        project_kernel,
        out_shape=jax.ShapeDtypeStruct(shape, BF),
        in_specs=[in_smem()] + [in_vmem()] * (1 + len(packs)),
        out_specs=pl.BlockSpec(memory_space=pltpu.HBM),
        scratch_shapes=[pltpu.VMEM(shape, BF), pltpu.SemaphoreType.DMA((X,))],
        compiler_params=pltpu.CompilerParams(vmem_limit_bytes=VMEM),
        name="project",
    )(x, chunks, *packs)


def activate_kernel(parts_ref, out_ref):
    total = parts_ref[0].astype(F32)
    for d in range(1, X):
        total += parts_ref[d].astype(F32)
    gate, up = total[:, :LANES], total[:, LANES:]
    out_ref[...] = (gate / (1.0 + jnp.exp(-gate)) * up).astype(BF)


def activate(parts):
    shape = jax.ShapeDtypeStruct((parts.shape[1], LANES), BF)
    return call(activate_kernel, "activate", shape, [in_vmem()])(parts)


def down_kernel(x_ref, z_ref, *refs):
    hiddens, (own_ref, p1, p2, p3, other_ref, out_ref) = refs[: 2 * X], refs[2 * X :]
    experts = out_ref.shape[0]
    rows = other_ref.shape[0] // X
    depth = rows // 4
    hidden = jnp.concatenate([ref[...] for ref in hiddens], axis=1)
    blocks = []
    for ref in (own_ref, p1, p2, p3):
        base = ref.shape[0] - 2 * rows + z_ref[0] * rows
        tiles = [ref[pl.ds(pl.multiple_of(base + c * depth, LANES), depth), :] for c in range(4)]
        blocks.append(jnp.concatenate(tiles, axis=1))
    for d in range(X):
        tiles = [other_ref[pl.ds(d * rows + c * depth, depth), :] for c in range(4)]
        blocks.append(jnp.concatenate(tiles, axis=1))
    weight = jnp.concatenate(blocks, axis=0)
    count = experts * 16
    main = jnp.dot(hidden[:count], weight, preferred_element_type=F32)
    last = jnp.dot(hidden[count:], weight, preferred_element_type=F32)
    for c in range(3):
        out_ref[:, c * 16 : (c + 1) * 16, :] = (
            main[:, c * LANES : (c + 1) * LANES].astype(BF).reshape(experts, 16, LANES)
        )
    half = main[:, 3 * LANES :]
    turned = pltpu.roll(half, LANES // 2, 1)
    odd = lax.rem(x_ref[0], 2) == 1
    low = jnp.where(odd, turned, half).reshape(experts, 16, LANES)[:, :8]
    high = jnp.where(odd, half, turned).reshape(experts, 16, LANES)[:, 8:]
    lane = lax.broadcasted_iota(jnp.int32, low.shape, 2)
    halves = jnp.where(lane < LANES // 2, low, high)
    tail = spread([last[:, c * LANES : (c + 1) * LANES] for c in range(4)], 8)
    out_ref[:, 48:64, :] = jnp.concatenate([halves, tail], axis=1).astype(BF)


def down(x, z, hiddens, own, packs, other, experts):
    shape = jax.ShapeDtypeStruct((experts, 64, LANES), BF)
    specs = [in_smem()] * 2 + [in_vmem()] * (2 * X + X + 1)
    return call(down_kernel, "down", shape, specs)(x, z, *hiddens, own, *packs, other)


def combine_kernel(x_ref, ids_ref, scale_ref, chunks_ref, out_ref):
    experts = chunks_ref.shape[0]
    ids, scale = ids_ref[...], scale_ref[...]
    topk, tokens = ids.shape
    place = slots(ids, experts)
    lane = lax.broadcasted_iota(jnp.int32, (experts, tokens), 0)
    weight = jnp.zeros((experts, tokens), F32)
    for k in range(topk):
        weight += jnp.where(ids[k : k + 1, :] == lane, scale[k : k + 1, :], 0.0)
    upper = weight.astype(BF).astype(F32)
    lower = weight - upper
    sub = lax.broadcasted_iota(jnp.int32, (experts, 16, tokens), 1)
    slot = sub.astype(F32)
    place = place[:, None, :]
    contract = (((0,), (0,)), ((), ()))
    main = jnp.concatenate(
        [chunks_ref[:, c * 16 : (c + 1) * 16, :].reshape(experts * 16, LANES) for c in range(3)], axis=1
    )
    rest = chunks_ref[:, 48:64, :].reshape(experts * 16, LANES)
    whole = jnp.zeros((tokens, 3 * LANES), F32)
    low = jnp.zeros((tokens, LANES), F32)
    high = jnp.zeros((tokens, LANES), F32)
    ends = [jnp.zeros((tokens, LANES), F32) for _ in range(4)]

    def times(hit, part, rows):
        coef = jnp.where(hit, part[:, None, :], 0.0).reshape(experts * 16, tokens).astype(BF)
        return lax.dot_general(coef, rows, contract, preferred_element_type=F32)

    for part in (upper, lower):
        whole += times(place == slot, part, main)
        low += times((place == slot) & (sub < 8), part, rest)
        high += times((place == slot + 8.0) & (sub < 8), part, rest)
        for c in range(4):
            ends[c] += times((place == 16.0) & (sub == 8 + c), part, rest)
    odd = lax.rem(x_ref[0], 2) == 1
    even_half = low + pltpu.roll(high, LANES // 2, 1) + ends[3]
    odd_half = pltpu.roll(low, LANES // 2, 1) + high + ends[3]
    half = jnp.where(odd, odd_half, even_half)
    total = jnp.concatenate([whole + jnp.concatenate(ends[:3], axis=1), half], axis=1)
    total = jnp.where(odd, pltpu.roll(total, LANES // 2, 1), total)
    out_ref[...] = total[:, : out_ref.shape[1]].astype(BF)


def combine(x, ids, scale, chunks, columns):
    shape = jax.ShapeDtypeStruct((ids.shape[1], columns), BF)
    return call(combine_kernel, "combine", shape, [in_smem()] + [in_vmem()] * 3)(x, ids, scale, chunks)


def shift(value, d):
    pairs = [(z * X + x, z * X + (x + d) % X) for z in range(2) for x in range(X)]
    return lax.ppermute(value, "pipe", pairs)


def cross(value):
    return lax.ppermute(value, "pipe", [(p, (p + X) % (2 * X)) for p in range(2 * X)])


def across(value):
    groups = [[z * X + x for x in range(X)] for z in range(2)]
    return lax.all_to_all(value, "pipe", split_axis=0, concat_axis=0, axis_index_groups=groups, tiled=True)


def body(tokens, expert_ids, gate_scale, w_gate, w_up, w_down):
    groups = lax.axis_size("expert")
    pipe = lax.axis_index("pipe")
    x = (pipe & (X - 1)).reshape(1)
    z = (pipe >> 2).reshape(1)
    ids, scale = expert_ids.T, gate_scale.T
    w_gate, w_up, w_down = w_gate[0], w_up[0], w_down[0]
    buffer = dispatch(x, ids, tokens, groups)
    chunks = lax.all_to_all(buffer, "expert", split_axis=0, concat_axis=0, tiled=True)
    own, *sent = pack(x, w_gate, w_up, w_down)
    packs = [shift(sent[d - 1], d) for d in range(1, X)]
    to_swap = swap(z, own, packs)
    chunks, to_swap = lax.optimization_barrier((chunks, to_swap))
    other_down = cross(to_swap)
    arrived = across(project(x, chunks, [own] + packs))
    arrived, other_down = lax.optimization_barrier((arrived, other_down))
    hidden = activate(arrived)
    swapped = cross(hidden)
    hiddens = [hidden] + [shift(hidden, d) for d in range(1, X)]
    hiddens += [swapped] + [shift(swapped, d) for d in range(1, X)]
    output = down(x, z, hiddens, own, packs, other_down, groups)
    returned = lax.all_to_all(output, "expert", split_axis=0, concat_axis=0, tiled=True)
    return combine(x, ids, scale, returned, tokens.shape[1] // (2 * X))


def solution(mesh):
    placed = (
        P("expert", None),
        P("expert", None),
        P("expert", None),
        P("expert", None, "pipe"),
        P("expert", None, "pipe"),
        P("expert", "pipe", None),
    )
    return jax.shard_map(
        body, mesh=mesh, in_specs=placed, out_specs=P("expert", "pipe"), check_vma=False
    )
```

```python
import jax
import jax.numpy as jnp
from jax import lax
from jax.experimental import pallas as pl
from jax.experimental.pallas import tpu as pltpu
from jax.sharding import PartitionSpec as P

BF = jnp.bfloat16
F32 = jnp.float32
LANES = 128
X = 4
PARTS = 4
HOLD = 50_000_000_000
FULL = 60 * 1024 * 1024
VMEM = 16 * 1024 * 1024


def call(kernel, name, out_shape, in_specs, out_specs=None, scratch=(), vmem=VMEM, cost=None):
    if out_specs is None:
        out_specs = jax.tree.map(lambda _: in_vmem(), out_shape)
    return pl.pallas_call(
        kernel,
        out_shape=out_shape,
        in_specs=in_specs,
        out_specs=out_specs,
        scratch_shapes=scratch,
        compiler_params=pltpu.CompilerParams(vmem_limit_bytes=vmem),
        cost_estimate=cost,
        name=name,
    )


def in_vmem():
    return pl.BlockSpec(memory_space=pltpu.VMEM)


def anywhere():
    return pl.BlockSpec(memory_space=pl.ANY)


def in_smem():
    return pl.BlockSpec(memory_space=pltpu.SMEM)


def slots(ids, experts):
    topk, tokens = ids.shape
    lane = lax.broadcasted_iota(jnp.int32, (experts, tokens), 0)
    named = jnp.zeros((experts, tokens), F32)
    for k in range(topk):
        named += (ids[k : k + 1, :] == lane).astype(F32)
    row = lax.broadcasted_iota(jnp.int32, (tokens, tokens), 0)
    col = lax.broadcasted_iota(jnp.int32, (tokens, tokens), 1)
    place = jnp.dot(named.astype(BF), (row < col).astype(BF), preferred_element_type=F32)
    return jnp.where(named > 0.5, place, -1.0)


def spread(tiles, rows):
    count = tiles[0].shape[0]
    sub = lax.broadcasted_iota(jnp.int32, (count, rows, LANES), 1)
    out = jnp.zeros((count, rows, LANES), F32)
    for c, tile in enumerate(tiles):
        out += jnp.where(sub == c, tile[:, None, :], 0.0)
    return out


def dispatch_kernel(x_ref, ids_ref, tok_ref, out_ref, own_ref, rows_ref, sem, sems):
    experts = out_ref.shape[0]
    tokens, quarter = own_ref.shape
    tiles = quarter // LANES
    part = pl.ds(pl.multiple_of(x_ref[0] * quarter, LANES), quarter)
    fetch = pltpu.make_async_copy(tok_ref.at[:, part], own_ref, sem)
    fetch.start()
    place = slots(ids_ref[...], experts)
    fetch.wait()
    tok = own_ref[...]
    last = jnp.dot((place == 16.0).astype(BF), tok, preferred_element_type=F32)
    tail = spread([last[:, c * LANES : (c + 1) * LANES] for c in range(tiles)], 8)
    rows_ref[:, tiles * 16 : tiles * 16 + 8, :] = tail.astype(BF)
    count = experts // PARTS
    slot = lax.broadcasted_iota(jnp.int32, (count, 16, tokens), 1).astype(F32)
    copies = []
    for g in range(PARTS):
        group = slice(g * count, (g + 1) * count)
        pick = jnp.where(place[group][:, None, :] == slot, 1.0, 0.0).reshape(count * 16, tokens).astype(BF)
        rows = jnp.dot(pick, tok, preferred_element_type=F32).astype(BF)
        for c in range(tiles):
            rows_ref[group, c * 16 : (c + 1) * 16, :] = rows[:, c * LANES : (c + 1) * LANES].reshape(count, 16, LANES)
        some = pl.ds(g * count, count)
        copies.append(pltpu.make_async_copy(rows_ref.at[some], out_ref.at[some], sems.at[g]))
        copies[g].start()
    for copy in copies:
        copy.wait()


def dispatch(x, ids, tokens, experts):
    count, width = tokens.shape
    quarter = width // X
    shape = (experts, quarter // LANES * 16 + 8, LANES)
    scratch = [
        pltpu.VMEM((count, quarter), BF),
        pltpu.VMEM(shape, BF),
        pltpu.SemaphoreType.DMA,
        pltpu.SemaphoreType.DMA((PARTS,)),
    ]
    specs = [in_smem(), in_vmem(), anywhere()]
    out = jax.ShapeDtypeStruct(shape, BF)
    return call(dispatch_kernel, "dispatch", out, specs, anywhere(), scratch, FULL)(x, ids, tokens)


def pack_kernel(x_ref, gate_ref, up_ref, down_ref, *outs):
    quarter = gate_ref.shape[0] // X
    depth = down_ref.shape[0]

    def put_down(out, base, q):
        for z in range(2):
            p = z * X + q
            pair, odd = p // 2, lax.rem(p, 2)
            first = pair * (quarter // LANES) + 4 * odd
            half = pair * (quarter // LANES) + 3
            for c in range(4):
                tile = half if c == 3 else first + c
                cols = pl.ds(pl.multiple_of(tile * LANES, LANES), LANES)
                out[pl.ds(base + (z * 4 + c) * depth, depth), :] = down_ref[:, cols]

    for d, out in enumerate(outs):
        q = lax.rem(x_ref[0] + d, X)
        part = pl.ds(pl.multiple_of(q * quarter, quarter), quarter)
        out[pl.ds(0, quarter), :] = gate_ref[part, :]
        out[pl.ds(quarter, quarter), :] = up_ref[part, :]
        put_down(out, 2 * quarter, q)


def pack(x, w_gate, w_up, w_down):
    depth = w_down.shape[0]
    rows = 2 * (w_gate.shape[0] // X) + 8 * depth
    shapes = [jax.ShapeDtypeStruct((r, LANES), BF) for r in [rows] * X]
    return call(pack_kernel, "pack", shapes, [in_smem()] + [in_vmem()] * 3)(x, w_gate, w_up, w_down)


def unpack_kernel(z_ref, *refs):
    packs, (weight_ref, out_ref) = refs[:X], refs[X:]
    quarter = weight_ref.shape[1]
    rows = out_ref.shape[0] // X
    start = pl.multiple_of(2 * quarter + (1 - z_ref[0]) * rows, LANES)
    for d, ref in enumerate(packs):
        weight_ref[d, :, pl.ds(0, LANES)] = ref[pl.ds(0, quarter), :]
        weight_ref[d, :, pl.ds(LANES, LANES)] = ref[pl.ds(quarter, quarter), :]
        out_ref[pl.ds(d * rows, rows), :] = ref[pl.ds(start, rows), :]


def unpack(z, packs, quarter):
    rows = (packs[0].shape[0] - 2 * quarter) // 2
    shapes = [
        jax.ShapeDtypeStruct((X, quarter, 2 * LANES), BF),
        jax.ShapeDtypeStruct((X * rows, LANES), BF),
    ]
    return call(unpack_kernel, "unpack", shapes, [in_smem()] + [in_vmem()] * X)(z, *packs)


def assemble_kernel(z_ref, *refs):
    packs, (other_ref, out_ref) = refs[:X], refs[X:]
    rows = other_ref.shape[0] // X
    depth = rows // 4
    for d, ref in enumerate(packs):
        base = ref.shape[0] - 2 * rows + z_ref[0] * rows
        for c in range(4):
            cols = pl.ds(c * LANES, LANES)
            out_ref[pl.ds(d * depth, depth), cols] = ref[pl.ds(pl.multiple_of(base + c * depth, LANES), depth), :]
            out_ref[pl.ds((X + d) * depth, depth), cols] = other_ref[pl.ds(d * rows + c * depth, depth), :]


def assemble(z, packs, other):
    shape = jax.ShapeDtypeStruct((other.shape[0] // 2, 4 * LANES), BF)
    specs = [in_smem()] + [in_vmem()] * (X + 1)
    cost = pl.CostEstimate(flops=HOLD, bytes_accessed=4 * other.size, transcendentals=0)
    return call(assemble_kernel, "assemble", shape, specs, cost=cost)(z, *packs, other)


def stacked(chunks_ref):
    sources, depth, _ = chunks_ref.shape
    tiles = depth // 16
    main = [chunks_ref[:, c * 16 : (c + 1) * 16, :].reshape(sources * 16, LANES) for c in range(tiles)]
    tail = chunks_ref[:, tiles * 16 : tiles * 16 + 8, :].reshape(sources * 8, LANES)
    row = lax.broadcasted_iota(jnp.int32, (sources, sources * 8), 0)
    col = lax.broadcasted_iota(jnp.int32, (sources, sources * 8), 1)
    last = [
        jnp.dot((col == row * 8 + c).astype(BF), tail, preferred_element_type=F32).astype(BF) for c in range(tiles)
    ]
    return jnp.concatenate(main, axis=1), jnp.concatenate(last, axis=1)


def project_into(out_ref, main, last, weight):
    count = main.shape[0]
    out_ref[pl.ds(0, count), :] = jnp.dot(main, weight, preferred_element_type=F32).astype(out_ref.dtype)
    out_ref[pl.ds(count, last.shape[0]), :] = jnp.dot(last, weight, preferred_element_type=F32).astype(out_ref.dtype)


def project(chunks, weight, blocks, dtype, name):
    def kernel(chunks_ref, weight_ref, *outs):
        main, last = stacked(chunks_ref)
        for d, out_ref in zip(blocks, outs):
            project_into(out_ref, main, last, weight_ref[d])

    shapes = [jax.ShapeDtypeStruct((chunks.shape[0] * 17, 2 * LANES), dtype)] * len(blocks)
    return call(kernel, name, shapes, [in_vmem()] * 2)(chunks, weight)


def activate_kernel(own_ref, *refs):
    parts, out_ref = refs[:-1], refs[-1]
    total = own_ref[...]
    for ref in parts:
        total += ref[...].astype(F32)
    gate, up = total[:, :LANES], total[:, LANES:]
    out_ref[...] = (gate / (1.0 + jnp.exp(-gate)) * up).astype(BF)


def activate(own, parts):
    shape = jax.ShapeDtypeStruct((own.shape[0], LANES), BF)
    return call(activate_kernel, "activate", shape, [in_vmem()] * (1 + len(parts)))(own, *parts)


def down_kernel(x_ref, weight_ref, *refs):
    hiddens, out_ref = refs[:-1], refs[-1]
    experts = out_ref.shape[0]
    hidden = jnp.concatenate([ref[...] for ref in hiddens], axis=1)
    weight = weight_ref[...]
    count = experts * 16
    main = jnp.dot(hidden[:count], weight, preferred_element_type=F32)
    last = jnp.dot(hidden[count:], weight, preferred_element_type=F32)
    for c in range(3):
        out_ref[:, c * 16 : (c + 1) * 16, :] = (
            main[:, c * LANES : (c + 1) * LANES].astype(BF).reshape(experts, 16, LANES)
        )
    half = main[:, 3 * LANES :]
    turned = pltpu.roll(half, LANES // 2, 1)
    odd = lax.rem(x_ref[0], 2) == 1
    low = jnp.where(odd, turned, half).reshape(experts, 16, LANES)[:, :8]
    high = jnp.where(odd, half, turned).reshape(experts, 16, LANES)[:, 8:]
    lane = lax.broadcasted_iota(jnp.int32, low.shape, 2)
    halves = jnp.where(lane < LANES // 2, low, high)
    tail = spread([last[:, c * LANES : (c + 1) * LANES] for c in range(4)], 8)
    out_ref[:, 48:64, :] = jnp.concatenate([halves, tail], axis=1).astype(BF)


def down(x, weight, hiddens, experts):
    shape = jax.ShapeDtypeStruct((experts, 64, LANES), BF)
    specs = [in_smem()] + [in_vmem()] * (1 + len(hiddens))
    return call(down_kernel, "down", shape, specs)(x, weight, *hiddens)


def combine_kernel(x_ref, ids_ref, scale_ref, chunks_ref, out_ref):
    experts = chunks_ref.shape[0]
    ids, scale = ids_ref[...], scale_ref[...]
    topk, tokens = ids.shape
    place = slots(ids, experts)
    lane = lax.broadcasted_iota(jnp.int32, (experts, tokens), 0)
    weight = jnp.zeros((experts, tokens), F32)
    for k in range(topk):
        weight += jnp.where(ids[k : k + 1, :] == lane, scale[k : k + 1, :], 0.0)
    upper = weight.astype(BF).astype(F32)
    lower = weight - upper
    sub = lax.broadcasted_iota(jnp.int32, (experts, 16, tokens), 1)
    slot = sub.astype(F32)
    place = place[:, None, :]
    contract = (((0,), (0,)), ((), ()))
    main = jnp.concatenate(
        [chunks_ref[:, c * 16 : (c + 1) * 16, :].reshape(experts * 16, LANES) for c in range(3)], axis=1
    )
    rest = chunks_ref[:, 48:64, :].reshape(experts * 16, LANES)
    whole = jnp.zeros((tokens, 3 * LANES), F32)
    low = jnp.zeros((tokens, LANES), F32)
    high = jnp.zeros((tokens, LANES), F32)
    ends = [jnp.zeros((tokens, LANES), F32) for _ in range(4)]

    def times(hit, part, rows):
        coef = jnp.where(hit, part[:, None, :], 0.0).reshape(experts * 16, tokens).astype(BF)
        return lax.dot_general(coef, rows, contract, preferred_element_type=F32)

    for part in (upper, lower):
        whole += times(place == slot, part, main)
        low += times((place == slot) & (sub < 8), part, rest)
        high += times((place == slot + 8.0) & (sub < 8), part, rest)
        for c in range(4):
            ends[c] += times((place == 16.0) & (sub == 8 + c), part, rest)
    odd = lax.rem(x_ref[0], 2) == 1
    even_half = low + pltpu.roll(high, LANES // 2, 1) + ends[3]
    odd_half = pltpu.roll(low, LANES // 2, 1) + high + ends[3]
    half = jnp.where(odd, odd_half, even_half)
    total = jnp.concatenate([whole + jnp.concatenate(ends[:3], axis=1), half], axis=1)
    total = jnp.where(odd, pltpu.roll(total, LANES // 2, 1), total)
    out_ref[...] = total[:, : out_ref.shape[1]].astype(BF)


def combine(x, ids, scale, chunks, columns):
    shape = jax.ShapeDtypeStruct((ids.shape[1], columns), BF)
    return call(combine_kernel, "combine", shape, [in_smem()] + [in_vmem()] * 3)(x, ids, scale, chunks)


def shift(value, d):
    pairs = [(z * X + x, z * X + (x + d) % X) for z in range(2) for x in range(X)]
    return lax.ppermute(value, "pipe", pairs)


def cross(value):
    return lax.ppermute(value, "pipe", [(p, (p + X) % (2 * X)) for p in range(2 * X)])


def body(tokens, expert_ids, gate_scale, w_gate, w_up, w_down):
    groups = lax.axis_size("expert")
    pipe = lax.axis_index("pipe")
    x = (pipe & (X - 1)).reshape(1)
    z = (pipe >> 2).reshape(1)
    ids, scale = expert_ids.T, gate_scale.T
    w_gate, w_up, w_down = w_gate[0], w_up[0], w_down[0]
    buffer = dispatch(x, ids, tokens, groups)
    chunks = lax.all_to_all(buffer, "expert", split_axis=0, concat_axis=0, tiled=True)
    own, *sent = pack(x, w_gate, w_up, w_down)
    packs = [own] + [shift(sent[d - 1], d) for d in range(1, X)]
    projection, to_swap = unpack(z, packs, tokens.shape[1] // X)
    parts = project(chunks, projection, (2, 1, 3), BF, "project_sent")
    arrived = [shift(part, -d) for d, part in zip((2, 1, 3), parts)]
    weight = assemble(z, packs, cross(to_swap))
    chunks, weight = lax.optimization_barrier((chunks, weight))
    (mine,) = project(chunks, projection, (0,), F32, "project_own")
    hidden = activate(mine, arrived)
    swapped = cross(hidden)
    hiddens = [hidden] + [shift(hidden, d) for d in range(1, X)]
    hiddens += [swapped] + [shift(swapped, d) for d in range(1, X)]
    output = down(x, weight, hiddens, groups)
    returned = lax.all_to_all(output, "expert", split_axis=0, concat_axis=0, tiled=True)
    return combine(x, ids, scale, returned, tokens.shape[1] // (2 * X))


def solution(mesh):
    placed = (
        P("expert", None),
        P("expert", None),
        P("expert", None),
        P("expert", None, "pipe"),
        P("expert", None, "pipe"),
        P("expert", "pipe", None),
    )
    return jax.shard_map(
        body, mesh=mesh, in_specs=placed, out_specs=P("expert", "pipe"), check_vma=False
    )
```

```python
import jax
import jax.numpy as jnp
from jax import lax
from jax.experimental import pallas as pl
from jax.experimental.pallas import tpu as pltpu
from jax.sharding import PartitionSpec as P

BF = jnp.bfloat16
F32 = jnp.float32
LANES = 128
X = 4
PARTS = 4
FULL = 60 * 1024 * 1024
VMEM = 16 * 1024 * 1024


def call(kernel, name, out_shape, in_specs, out_specs=None, scratch=(), vmem=VMEM, cost=None):
    if out_specs is None:
        out_specs = jax.tree.map(lambda _: in_vmem(), out_shape)
    return pl.pallas_call(
        kernel,
        out_shape=out_shape,
        in_specs=in_specs,
        out_specs=out_specs,
        scratch_shapes=scratch,
        compiler_params=pltpu.CompilerParams(vmem_limit_bytes=vmem),
        cost_estimate=cost,
        name=name,
    )


def in_vmem():
    return pl.BlockSpec(memory_space=pltpu.VMEM)


def anywhere():
    return pl.BlockSpec(memory_space=pl.ANY)


def in_smem():
    return pl.BlockSpec(memory_space=pltpu.SMEM)


def slots(ids, experts):
    topk, tokens = ids.shape
    lane = lax.broadcasted_iota(jnp.int32, (experts, tokens), 0)
    named = jnp.zeros((experts, tokens), F32)
    for k in range(topk):
        named += (ids[k : k + 1, :] == lane).astype(F32)
    row = lax.broadcasted_iota(jnp.int32, (tokens, tokens), 0)
    col = lax.broadcasted_iota(jnp.int32, (tokens, tokens), 1)
    place = jnp.dot(named.astype(BF), (row < col).astype(BF), preferred_element_type=F32)
    return jnp.where(named > 0.5, place, -1.0)


def spread(tiles, rows):
    count = tiles[0].shape[0]
    sub = lax.broadcasted_iota(jnp.int32, (count, rows, LANES), 1)
    out = jnp.zeros((count, rows, LANES), F32)
    for c, tile in enumerate(tiles):
        out += jnp.where(sub == c, tile[:, None, :], 0.0)
    return out


def dispatch_kernel(x_ref, ids_ref, tok_ref, out_ref, own_ref, rows_ref, sem, sems):
    experts = out_ref.shape[0]
    tokens, quarter = own_ref.shape
    tiles = quarter // LANES
    part = pl.ds(pl.multiple_of(x_ref[0] * quarter, LANES), quarter)
    fetch = pltpu.make_async_copy(tok_ref.at[:, part], own_ref, sem)
    fetch.start()
    place = slots(ids_ref[...], experts)
    fetch.wait()
    tok = own_ref[...]
    last = jnp.dot((place == 16.0).astype(BF), tok, preferred_element_type=F32)
    tail = spread([last[:, c * LANES : (c + 1) * LANES] for c in range(tiles)], 8)
    rows_ref[:, tiles * 16 : tiles * 16 + 8, :] = tail.astype(BF)
    count = experts // PARTS
    slot = lax.broadcasted_iota(jnp.int32, (count, 16, tokens), 1).astype(F32)
    copies = []
    for g in range(PARTS):
        group = slice(g * count, (g + 1) * count)
        pick = jnp.where(place[group][:, None, :] == slot, 1.0, 0.0).reshape(count * 16, tokens).astype(BF)
        rows = jnp.dot(pick, tok, preferred_element_type=F32).astype(BF)
        for c in range(tiles):
            rows_ref[group, c * 16 : (c + 1) * 16, :] = rows[:, c * LANES : (c + 1) * LANES].reshape(count, 16, LANES)
        some = pl.ds(g * count, count)
        copies.append(pltpu.make_async_copy(rows_ref.at[some], out_ref.at[some], sems.at[g]))
        copies[g].start()
    for copy in copies:
        copy.wait()


def dispatch(x, ids, tokens, experts):
    count, width = tokens.shape
    quarter = width // X
    shape = (experts, quarter // LANES * 16 + 8, LANES)
    scratch = [
        pltpu.VMEM((count, quarter), BF),
        pltpu.VMEM(shape, BF),
        pltpu.SemaphoreType.DMA,
        pltpu.SemaphoreType.DMA((PARTS,)),
    ]
    specs = [in_smem(), in_vmem(), anywhere()]
    out = jax.ShapeDtypeStruct(shape, BF)
    return call(dispatch_kernel, "dispatch", out, specs, anywhere(), scratch, FULL)(x, ids, tokens)


def pack_kernel(x_ref, z_ref, gate_ref, up_ref, down_ref, *outs):
    near, far = outs[:X], outs[X:]
    quarter = gate_ref.shape[0] // X
    depth = down_ref.shape[0]

    def put_down(out, base, z, q):
        p = z * X + q
        first = p // 2 * (quarter // LANES)
        for c in range(4):
            tile = first + 3 if c == 3 else first + c + 4 * lax.rem(p, 2)
            cols = pl.ds(pl.multiple_of(tile * LANES, LANES), LANES)
            out[pl.ds(base + c * depth, depth), :] = down_ref[:, cols]

    for d in range(X):
        q = lax.rem(x_ref[0] + d, X)
        part = pl.ds(pl.multiple_of(q * quarter, quarter), quarter)
        near[d][pl.ds(0, quarter), :] = gate_ref[part, :]
        near[d][pl.ds(quarter, quarter), :] = up_ref[part, :]
        put_down(near[d], 2 * quarter, z_ref[0], q)
        put_down(far[d], 0, 1 - z_ref[0], q)


def pack(x, z, w_gate, w_up, w_down):
    rows = 2 * (w_gate.shape[0] // X) + 4 * w_down.shape[0]
    shapes = [jax.ShapeDtypeStruct((r, LANES), BF) for r in [rows] * X + [4 * w_down.shape[0]] * X]
    outs = call(pack_kernel, "pack", shapes, [in_smem()] * 2 + [in_vmem()] * 3)(x, z, w_gate, w_up, w_down)
    return outs[:X], outs[X:]


def assemble_kernel(*refs):
    near, far, out_ref = refs[:X], refs[X : 2 * X], refs[2 * X]
    rows = far[0].shape[0]
    depth = rows // 4
    for d in range(X):
        base = near[d].shape[0] - rows
        for c in range(4):
            cols = pl.ds(c * LANES, LANES)
            out_ref[pl.ds(d * depth, depth), cols] = near[d][pl.ds(base + c * depth, depth), :]
            out_ref[pl.ds((X + d) * depth, depth), cols] = far[d][pl.ds(c * depth, depth), :]


def assemble(near, far):
    shape = jax.ShapeDtypeStruct((2 * far[0].shape[0], 4 * LANES), BF)
    return call(assemble_kernel, "assemble", shape, [in_vmem()] * (2 * X))(*near, *far)


def stacked(chunks_ref):
    sources, depth, _ = chunks_ref.shape
    tiles = depth // 16
    main = [chunks_ref[:, c * 16 : (c + 1) * 16, :].reshape(sources * 16, LANES) for c in range(tiles)]
    tail = chunks_ref[:, tiles * 16 : tiles * 16 + 8, :].reshape(sources * 8, LANES)
    row = lax.broadcasted_iota(jnp.int32, (sources, sources * 8), 0)
    col = lax.broadcasted_iota(jnp.int32, (sources, sources * 8), 1)
    last = [
        jnp.dot((col == row * 8 + c).astype(BF), tail, preferred_element_type=F32).astype(BF) for c in range(tiles)
    ]
    return jnp.concatenate(main, axis=1), jnp.concatenate(last, axis=1)


def project(chunks, packs, dtype, name):
    sources, depth, _ = chunks.shape
    quarter = depth // 16 * LANES

    def kernel(chunks_ref, *refs):
        count = len(packs)
        sent, outs, (weight_ref, sems) = refs[:count], refs[count : 2 * count], refs[2 * count :]
        copies = []
        for d in range(count):
            for half in range(2):
                rows, cols = pl.ds(half * quarter, quarter), pl.ds(half * LANES, LANES)
                copy = pltpu.make_async_copy(sent[d].at[rows, :], weight_ref.at[d, :, cols], sems.at[d, half])
                copy.start()
                copies.append(copy)
        main, last = stacked(chunks_ref)
        for d in range(count):
            copies[2 * d].wait()
            copies[2 * d + 1].wait()
            weight = weight_ref[d]
            outs[d][pl.ds(0, sources * 16), :] = jnp.dot(main, weight, preferred_element_type=F32).astype(dtype)
            outs[d][pl.ds(sources * 16, sources), :] = jnp.dot(last, weight, preferred_element_type=F32).astype(dtype)

    shapes = [jax.ShapeDtypeStruct((sources * 17, 2 * LANES), dtype)] * len(packs)
    scratch = [pltpu.VMEM((len(packs), quarter, 2 * LANES), BF), pltpu.SemaphoreType.DMA((len(packs), 2))]
    specs = [in_vmem()] + [anywhere()] * len(packs)
    return call(kernel, name, shapes, specs, scratch=scratch)(chunks, *packs)


def activate_kernel(own_ref, *refs):
    parts, out_ref = refs[:-1], refs[-1]
    total = own_ref[...]
    for ref in parts:
        total += ref[...].astype(F32)
    gate, up = total[:, :LANES], total[:, LANES:]
    out_ref[...] = (gate / (1.0 + jnp.exp(-gate)) * up).astype(BF)


def activate(own, parts):
    shape = jax.ShapeDtypeStruct((own.shape[0], LANES), BF)
    return call(activate_kernel, "activate", shape, [in_vmem()] * (1 + len(parts)))(own, *parts)


def down_kernel(x_ref, weight_ref, *refs):
    hiddens, out_ref = refs[:-1], refs[-1]
    experts = out_ref.shape[0]
    hidden = jnp.concatenate([ref[...] for ref in hiddens], axis=1)
    weight = weight_ref[...]
    count = experts * 16
    main = jnp.dot(hidden[:count], weight, preferred_element_type=F32)
    last = jnp.dot(hidden[count:], weight, preferred_element_type=F32)
    for c in range(3):
        out_ref[:, c * 16 : (c + 1) * 16, :] = (
            main[:, c * LANES : (c + 1) * LANES].astype(BF).reshape(experts, 16, LANES)
        )
    half = main[:, 3 * LANES :]
    turned = pltpu.roll(half, LANES // 2, 1)
    odd = lax.rem(x_ref[0], 2) == 1
    low = jnp.where(odd, turned, half).reshape(experts, 16, LANES)[:, :8]
    high = jnp.where(odd, half, turned).reshape(experts, 16, LANES)[:, 8:]
    lane = lax.broadcasted_iota(jnp.int32, low.shape, 2)
    halves = jnp.where(lane < LANES // 2, low, high)
    tail = spread([last[:, c * LANES : (c + 1) * LANES] for c in range(4)], 8)
    out_ref[:, 48:64, :] = jnp.concatenate([halves, tail], axis=1).astype(BF)


def down(x, weight, hiddens, experts):
    shape = jax.ShapeDtypeStruct((experts, 64, LANES), BF)
    specs = [in_smem()] + [in_vmem()] * (1 + len(hiddens))
    return call(down_kernel, "down", shape, specs)(x, weight, *hiddens)


def combine_kernel(x_ref, ids_ref, scale_ref, chunks_ref, out_ref):
    experts = chunks_ref.shape[0]
    ids, scale = ids_ref[...], scale_ref[...]
    topk, tokens = ids.shape
    place = slots(ids, experts)
    lane = lax.broadcasted_iota(jnp.int32, (experts, tokens), 0)
    weight = jnp.zeros((experts, tokens), F32)
    for k in range(topk):
        weight += jnp.where(ids[k : k + 1, :] == lane, scale[k : k + 1, :], 0.0)
    upper = weight.astype(BF).astype(F32)
    lower = weight - upper
    sub = lax.broadcasted_iota(jnp.int32, (experts, 16, tokens), 1)
    slot = sub.astype(F32)
    place = place[:, None, :]
    contract = (((0,), (0,)), ((), ()))
    main = jnp.concatenate(
        [chunks_ref[:, c * 16 : (c + 1) * 16, :].reshape(experts * 16, LANES) for c in range(3)], axis=1
    )
    rest = chunks_ref[:, 48:64, :].reshape(experts * 16, LANES)
    whole = jnp.zeros((tokens, 3 * LANES), F32)
    low = jnp.zeros((tokens, LANES), F32)
    high = jnp.zeros((tokens, LANES), F32)
    ends = [jnp.zeros((tokens, LANES), F32) for _ in range(4)]

    def times(hit, part, rows):
        coef = jnp.where(hit, part[:, None, :], 0.0).reshape(experts * 16, tokens).astype(BF)
        return lax.dot_general(coef, rows, contract, preferred_element_type=F32)

    for part in (upper, lower):
        whole += times(place == slot, part, main)
        low += times((place == slot) & (sub < 8), part, rest)
        high += times((place == slot + 8.0) & (sub < 8), part, rest)
        for c in range(4):
            ends[c] += times((place == 16.0) & (sub == 8 + c), part, rest)
    odd = lax.rem(x_ref[0], 2) == 1
    even_half = low + pltpu.roll(high, LANES // 2, 1) + ends[3]
    odd_half = pltpu.roll(low, LANES // 2, 1) + high + ends[3]
    half = jnp.where(odd, odd_half, even_half)
    total = jnp.concatenate([whole + jnp.concatenate(ends[:3], axis=1), half], axis=1)
    total = jnp.where(odd, pltpu.roll(total, LANES // 2, 1), total)
    out_ref[...] = total[:, : out_ref.shape[1]].astype(BF)


def combine(x, ids, scale, chunks, columns):
    shape = jax.ShapeDtypeStruct((ids.shape[1], columns), BF)
    return call(combine_kernel, "combine", shape, [in_smem()] + [in_vmem()] * 3)(x, ids, scale, chunks)


def shift(value, d):
    pairs = [(z * X + x, z * X + (x + d) % X) for z in range(2) for x in range(X)]
    return lax.ppermute(value, "pipe", pairs)


def cross(value, d=0):
    pairs = [(z * X + x, (1 - z) * X + (x + d) % X) for z in range(2) for x in range(X)]
    return lax.ppermute(value, "pipe", pairs)


def body(tokens, expert_ids, gate_scale, w_gate, w_up, w_down):
    groups = lax.axis_size("expert")
    pipe = lax.axis_index("pipe")
    x = (pipe & (X - 1)).reshape(1)
    z = (pipe >> 2).reshape(1)
    ids, scale = expert_ids.T, gate_scale.T
    w_gate, w_up, w_down = w_gate[0], w_up[0], w_down[0]
    buffer = dispatch(x, ids, tokens, groups)
    chunks = lax.all_to_all(buffer, "expert", split_axis=0, concat_axis=0, tiled=True)
    near, far = pack(x, z, w_gate, w_up, w_down)
    near = [near[0]] + [shift(near[d], d) for d in range(1, X)]
    far = [cross(far[d], d) for d in range(X)]
    chunks, *far = lax.optimization_barrier((chunks, *far))
    parts = project(chunks, [near[d] for d in (2, 1, 3)], BF, "project_sent")
    arrived = [shift(part, -d) for d, part in zip((2, 1, 3), parts)]
    (mine,) = project(chunks, near[:1], F32, "project_own")
    weight = assemble(near, far)
    hidden = activate(mine, arrived)
    swapped = cross(hidden)
    hiddens = [hidden] + [shift(hidden, d) for d in range(1, X)]
    hiddens += [swapped] + [shift(swapped, d) for d in range(1, X)]
    output = down(x, weight, hiddens, groups)
    returned = lax.all_to_all(output, "expert", split_axis=0, concat_axis=0, tiled=True)
    return combine(x, ids, scale, returned, tokens.shape[1] // (2 * X))


def solution(mesh):
    placed = (
        P("expert", None),
        P("expert", None),
        P("expert", None),
        P("expert", None, "pipe"),
        P("expert", None, "pipe"),
        P("expert", "pipe", None),
    )
    return jax.shard_map(
        body, mesh=mesh, in_specs=placed, out_specs=P("expert", "pipe"), check_vma=False
    )
```

```python
import jax
import jax.numpy as jnp
from jax import lax
from jax.experimental import pallas as pl
from jax.experimental.pallas import tpu as pltpu
from jax.sharding import PartitionSpec as P

BF = jnp.bfloat16
F32 = jnp.float32
LANES = 128
X = 4
PARTS = 4
HOLD = 50_000_000_000
FULL = 60 * 1024 * 1024
VMEM = 16 * 1024 * 1024


def call(kernel, name, out_shape, in_specs, out_specs=None, scratch=(), vmem=VMEM, cost=None):
    if out_specs is None:
        out_specs = jax.tree.map(lambda _: in_vmem(), out_shape)
    return pl.pallas_call(
        kernel,
        out_shape=out_shape,
        in_specs=in_specs,
        out_specs=out_specs,
        scratch_shapes=scratch,
        compiler_params=pltpu.CompilerParams(vmem_limit_bytes=vmem),
        cost_estimate=cost,
        name=name,
    )


def in_vmem():
    return pl.BlockSpec(memory_space=pltpu.VMEM)


def anywhere():
    return pl.BlockSpec(memory_space=pl.ANY)


def in_smem():
    return pl.BlockSpec(memory_space=pltpu.SMEM)


def slots(ids, experts):
    topk, tokens = ids.shape
    lane = lax.broadcasted_iota(jnp.int32, (experts, tokens), 0)
    named = jnp.zeros((experts, tokens), F32)
    for k in range(topk):
        named += (ids[k : k + 1, :] == lane).astype(F32)
    row = lax.broadcasted_iota(jnp.int32, (tokens, tokens), 0)
    col = lax.broadcasted_iota(jnp.int32, (tokens, tokens), 1)
    place = jnp.dot(named.astype(BF), (row < col).astype(BF), preferred_element_type=F32)
    return jnp.where(named > 0.5, place, -1.0)


def spread(tiles, rows):
    count = tiles[0].shape[0]
    sub = lax.broadcasted_iota(jnp.int32, (count, rows, LANES), 1)
    out = jnp.zeros((count, rows, LANES), F32)
    for c, tile in enumerate(tiles):
        out += jnp.where(sub == c, tile[:, None, :], 0.0)
    return out


def dispatch_kernel(x_ref, ids_ref, tok_ref, out_ref, own_ref, rows_ref, sem, sems):
    experts = out_ref.shape[0]
    tokens, quarter = own_ref.shape
    tiles = quarter // LANES
    part = pl.ds(pl.multiple_of(x_ref[0] * quarter, LANES), quarter)
    fetch = pltpu.make_async_copy(tok_ref.at[:, part], own_ref, sem)
    fetch.start()
    place = slots(ids_ref[...], experts)
    fetch.wait()
    tok = own_ref[...]
    last = jnp.dot((place == 16.0).astype(BF), tok, preferred_element_type=F32)
    tail = spread([last[:, c * LANES : (c + 1) * LANES] for c in range(tiles)], 8)
    rows_ref[:, tiles * 16 : tiles * 16 + 8, :] = tail.astype(BF)
    count = experts // PARTS
    slot = lax.broadcasted_iota(jnp.int32, (count, 16, tokens), 1).astype(F32)
    copies = []
    for g in range(PARTS):
        group = slice(g * count, (g + 1) * count)
        pick = jnp.where(place[group][:, None, :] == slot, 1.0, 0.0).reshape(count * 16, tokens).astype(BF)
        rows = jnp.dot(pick, tok, preferred_element_type=F32).astype(BF)
        for c in range(tiles):
            rows_ref[group, c * 16 : (c + 1) * 16, :] = rows[:, c * LANES : (c + 1) * LANES].reshape(count, 16, LANES)
        some = pl.ds(g * count, count)
        copies.append(pltpu.make_async_copy(rows_ref.at[some], out_ref.at[some], sems.at[g]))
        copies[g].start()
    for copy in copies:
        copy.wait()


def dispatch(x, ids, tokens, experts):
    count, width = tokens.shape
    quarter = width // X
    shape = (experts, quarter // LANES * 16 + 8, LANES)
    scratch = [
        pltpu.VMEM((count, quarter), BF),
        pltpu.VMEM(shape, BF),
        pltpu.SemaphoreType.DMA,
        pltpu.SemaphoreType.DMA((PARTS,)),
    ]
    specs = [in_smem(), in_vmem(), anywhere()]
    out = jax.ShapeDtypeStruct(shape, BF)
    return call(dispatch_kernel, "dispatch", out, specs, anywhere(), scratch, FULL)(x, ids, tokens)


def pack_kernel(x_ref, z_ref, gate_ref, up_ref, down_ref, *outs):
    near, far = outs[:X], outs[X]
    quarter = gate_ref.shape[0] // X
    depth = down_ref.shape[0]

    def put_down(out, base, z, q):
        p = z * X + q
        first = p // 2 * (quarter // LANES)
        for c in range(4):
            tile = first + 3 if c == 3 else first + c + 4 * lax.rem(p, 2)
            cols = pl.ds(pl.multiple_of(tile * LANES, LANES), LANES)
            out[pl.ds(base + c * depth, depth), :] = down_ref[:, cols]

    for d in range(X):
        q = lax.rem(x_ref[0] + d, X)
        part = pl.ds(pl.multiple_of(q * quarter, quarter), quarter)
        near[d][pl.ds(0, quarter), :] = gate_ref[part, :]
        near[d][pl.ds(quarter, quarter), :] = up_ref[part, :]
        put_down(near[d], 2 * quarter, z_ref[0], q)
        put_down(far, 4 * d * depth, 1 - z_ref[0], q)


def pack(x, z, w_gate, w_up, w_down):
    rows = 2 * (w_gate.shape[0] // X) + 4 * w_down.shape[0]
    shapes = [jax.ShapeDtypeStruct((r, LANES), BF) for r in [rows] * X + [4 * X * w_down.shape[0]]]
    outs = call(pack_kernel, "pack", shapes, [in_smem()] * 2 + [in_vmem()] * 3)(x, z, w_gate, w_up, w_down)
    return outs[:X], outs[X]


def split_kernel(rows_ref, *outs):
    count = outs[0].shape[0]
    for d, out_ref in enumerate(outs):
        out_ref[...] = rows_ref[pl.ds(d * count, count), :]


def split(rows):
    shapes = [jax.ShapeDtypeStruct((rows.shape[0] // X, LANES), BF)] * X
    cost = pl.CostEstimate(flops=HOLD, bytes_accessed=4 * rows.size, transcendentals=0)
    return call(split_kernel, "split", shapes, [in_vmem()], cost=cost)(rows)


def assemble_kernel(*refs):
    near, far, out_ref = refs[:X], refs[X : 2 * X], refs[2 * X]
    rows = far[0].shape[0]
    depth = rows // 4
    for d in range(X):
        base = near[d].shape[0] - rows
        for c in range(4):
            cols = pl.ds(c * LANES, LANES)
            out_ref[pl.ds(d * depth, depth), cols] = near[d][pl.ds(base + c * depth, depth), :]
            out_ref[pl.ds((X + d) * depth, depth), cols] = far[d][pl.ds(c * depth, depth), :]


def assemble(near, far):
    shape = jax.ShapeDtypeStruct((2 * far[0].shape[0], 4 * LANES), BF)
    return call(assemble_kernel, "assemble", shape, [in_vmem()] * (2 * X))(*near, *far)


def stacked(chunks_ref):
    sources, depth, _ = chunks_ref.shape
    tiles = depth // 16
    main = [chunks_ref[:, c * 16 : (c + 1) * 16, :].reshape(sources * 16, LANES) for c in range(tiles)]
    tail = chunks_ref[:, tiles * 16 : tiles * 16 + 8, :].reshape(sources * 8, LANES)
    row = lax.broadcasted_iota(jnp.int32, (sources, sources * 8), 0)
    col = lax.broadcasted_iota(jnp.int32, (sources, sources * 8), 1)
    last = [
        jnp.dot((col == row * 8 + c).astype(BF), tail, preferred_element_type=F32).astype(BF) for c in range(tiles)
    ]
    return jnp.concatenate(main, axis=1), jnp.concatenate(last, axis=1)


def project(chunks, packs, dtype, name):
    sources, depth, _ = chunks.shape
    quarter = depth // 16 * LANES

    def kernel(chunks_ref, *refs):
        count = len(packs)
        sent, outs, (weight_ref, sems) = refs[:count], refs[count : 2 * count], refs[2 * count :]
        copies = []
        for d in range(count):
            for half in range(2):
                rows, cols = pl.ds(half * quarter, quarter), pl.ds(half * LANES, LANES)
                copy = pltpu.make_async_copy(sent[d].at[rows, :], weight_ref.at[d, :, cols], sems.at[d, half])
                copy.start()
                copies.append(copy)
        main, last = stacked(chunks_ref)
        for d in range(count):
            copies[2 * d].wait()
            copies[2 * d + 1].wait()
            weight = weight_ref[d]
            outs[d][pl.ds(0, sources * 16), :] = jnp.dot(main, weight, preferred_element_type=F32).astype(dtype)
            outs[d][pl.ds(sources * 16, sources), :] = jnp.dot(last, weight, preferred_element_type=F32).astype(dtype)

    shapes = [jax.ShapeDtypeStruct((sources * 17, 2 * LANES), dtype)] * len(packs)
    scratch = [pltpu.VMEM((len(packs), quarter, 2 * LANES), BF), pltpu.SemaphoreType.DMA((len(packs), 2))]
    specs = [in_vmem()] + [anywhere()] * len(packs)
    return call(kernel, name, shapes, specs, scratch=scratch)(chunks, *packs)


def activate_kernel(own_ref, *refs):
    parts, out_ref = refs[:-1], refs[-1]
    total = own_ref[...]
    for ref in parts:
        total += ref[...].astype(F32)
    gate, up = total[:, :LANES], total[:, LANES:]
    out_ref[...] = (gate / (1.0 + jnp.exp(-gate)) * up).astype(BF)


def activate(own, parts):
    shape = jax.ShapeDtypeStruct((own.shape[0], LANES), BF)
    return call(activate_kernel, "activate", shape, [in_vmem()] * (1 + len(parts)))(own, *parts)


def down_kernel(x_ref, weight_ref, *refs):
    hiddens, out_ref = refs[:-1], refs[-1]
    experts = out_ref.shape[0]
    hidden = jnp.concatenate([ref[...] for ref in hiddens], axis=1)
    weight = weight_ref[...]
    count = experts * 16
    main = jnp.dot(hidden[:count], weight, preferred_element_type=F32)
    last = jnp.dot(hidden[count:], weight, preferred_element_type=F32)
    for c in range(3):
        out_ref[:, c * 16 : (c + 1) * 16, :] = (
            main[:, c * LANES : (c + 1) * LANES].astype(BF).reshape(experts, 16, LANES)
        )
    half = main[:, 3 * LANES :]
    turned = pltpu.roll(half, LANES // 2, 1)
    odd = lax.rem(x_ref[0], 2) == 1
    low = jnp.where(odd, turned, half).reshape(experts, 16, LANES)[:, :8]
    high = jnp.where(odd, half, turned).reshape(experts, 16, LANES)[:, 8:]
    lane = lax.broadcasted_iota(jnp.int32, low.shape, 2)
    halves = jnp.where(lane < LANES // 2, low, high)
    tail = spread([last[:, c * LANES : (c + 1) * LANES] for c in range(4)], 8)
    out_ref[:, 48:64, :] = jnp.concatenate([halves, tail], axis=1).astype(BF)


def down(x, weight, hiddens, experts):
    shape = jax.ShapeDtypeStruct((experts, 64, LANES), BF)
    specs = [in_smem()] + [in_vmem()] * (1 + len(hiddens))
    return call(down_kernel, "down", shape, specs)(x, weight, *hiddens)


def combine_kernel(x_ref, ids_ref, scale_ref, chunks_ref, out_ref):
    experts = chunks_ref.shape[0]
    ids, scale = ids_ref[...], scale_ref[...]
    topk, tokens = ids.shape
    place = slots(ids, experts)
    lane = lax.broadcasted_iota(jnp.int32, (experts, tokens), 0)
    weight = jnp.zeros((experts, tokens), F32)
    for k in range(topk):
        weight += jnp.where(ids[k : k + 1, :] == lane, scale[k : k + 1, :], 0.0)
    upper = weight.astype(BF).astype(F32)
    lower = weight - upper
    sub = lax.broadcasted_iota(jnp.int32, (experts, 16, tokens), 1)
    slot = sub.astype(F32)
    place = place[:, None, :]
    contract = (((0,), (0,)), ((), ()))
    main = jnp.concatenate(
        [chunks_ref[:, c * 16 : (c + 1) * 16, :].reshape(experts * 16, LANES) for c in range(3)], axis=1
    )
    rest = chunks_ref[:, 48:64, :].reshape(experts * 16, LANES)
    whole = jnp.zeros((tokens, 3 * LANES), F32)
    low = jnp.zeros((tokens, LANES), F32)
    high = jnp.zeros((tokens, LANES), F32)
    ends = [jnp.zeros((tokens, LANES), F32) for _ in range(4)]

    def times(hit, part, rows):
        coef = jnp.where(hit, part[:, None, :], 0.0).reshape(experts * 16, tokens).astype(BF)
        return lax.dot_general(coef, rows, contract, preferred_element_type=F32)

    for part in (upper, lower):
        whole += times(place == slot, part, main)
        low += times((place == slot) & (sub < 8), part, rest)
        high += times((place == slot + 8.0) & (sub < 8), part, rest)
        for c in range(4):
            ends[c] += times((place == 16.0) & (sub == 8 + c), part, rest)
    odd = lax.rem(x_ref[0], 2) == 1
    even_half = low + pltpu.roll(high, LANES // 2, 1) + ends[3]
    odd_half = pltpu.roll(low, LANES // 2, 1) + high + ends[3]
    half = jnp.where(odd, odd_half, even_half)
    total = jnp.concatenate([whole + jnp.concatenate(ends[:3], axis=1), half], axis=1)
    total = jnp.where(odd, pltpu.roll(total, LANES // 2, 1), total)
    out_ref[...] = total[:, : out_ref.shape[1]].astype(BF)


def combine(x, ids, scale, chunks, columns):
    shape = jax.ShapeDtypeStruct((ids.shape[1], columns), BF)
    return call(combine_kernel, "combine", shape, [in_smem()] + [in_vmem()] * 3)(x, ids, scale, chunks)


def shift(value, d):
    pairs = [(z * X + x, z * X + (x + d) % X) for z in range(2) for x in range(X)]
    return lax.ppermute(value, "pipe", pairs)


def cross(value):
    return lax.ppermute(value, "pipe", [(p, (p + X) % (2 * X)) for p in range(2 * X)])


def body(tokens, expert_ids, gate_scale, w_gate, w_up, w_down):
    groups = lax.axis_size("expert")
    pipe = lax.axis_index("pipe")
    x = (pipe & (X - 1)).reshape(1)
    z = (pipe >> 2).reshape(1)
    ids, scale = expert_ids.T, gate_scale.T
    w_gate, w_up, w_down = w_gate[0], w_up[0], w_down[0]
    buffer = dispatch(x, ids, tokens, groups)
    chunks = lax.all_to_all(buffer, "expert", split_axis=0, concat_axis=0, tiled=True)
    near, far = pack(x, z, w_gate, w_up, w_down)
    near = [near[0]] + [shift(near[d], d) for d in range(1, X)]
    far = split(cross(far))
    parts = project(chunks, [near[d] for d in (2, 1, 3)], BF, "project_sent")
    arrived = [shift(part, -d) for d, part in zip((2, 1, 3), parts)]
    chunks, *far = lax.optimization_barrier((chunks, *far))
    (mine,) = project(chunks, near[:1], F32, "project_own")
    far = [far[0]] + [shift(far[d], d) for d in range(1, X)]
    mine, weight = lax.optimization_barrier((mine, assemble(near, far)))
    hidden = activate(mine, arrived)
    swapped = cross(hidden)
    hiddens = [hidden] + [shift(hidden, d) for d in range(1, X)]
    hiddens += [swapped] + [shift(swapped, d) for d in range(1, X)]
    output = down(x, weight, hiddens, groups)
    returned = lax.all_to_all(output, "expert", split_axis=0, concat_axis=0, tiled=True)
    return combine(x, ids, scale, returned, tokens.shape[1] // (2 * X))


def solution(mesh):
    placed = (
        P("expert", None),
        P("expert", None),
        P("expert", None),
        P("expert", None, "pipe"),
        P("expert", None, "pipe"),
        P("expert", "pipe", None),
    )
    return jax.shard_map(
        body, mesh=mesh, in_specs=placed, out_specs=P("expert", "pipe"), check_vma=False
    )
```

```python
import jax
import jax.numpy as jnp
from jax import lax
from jax.experimental import pallas as pl
from jax.experimental.pallas import tpu as pltpu
from jax.sharding import PartitionSpec as P

BF = jnp.bfloat16
F32 = jnp.float32
LANES = 128
X = 4
PARTS = 4
HOLD = 50_000_000_000
FULL = 60 * 1024 * 1024
VMEM = 16 * 1024 * 1024


def call(kernel, name, out_shape, in_specs, out_specs=None, scratch=(), vmem=VMEM, cost=None):
    if out_specs is None:
        out_specs = jax.tree.map(lambda _: in_vmem(), out_shape)
    return pl.pallas_call(
        kernel,
        out_shape=out_shape,
        in_specs=in_specs,
        out_specs=out_specs,
        scratch_shapes=scratch,
        compiler_params=pltpu.CompilerParams(vmem_limit_bytes=vmem),
        cost_estimate=cost,
        name=name,
    )


def in_vmem():
    return pl.BlockSpec(memory_space=pltpu.VMEM)


def anywhere():
    return pl.BlockSpec(memory_space=pl.ANY)


def in_smem():
    return pl.BlockSpec(memory_space=pltpu.SMEM)


def slots(ids, experts):
    topk, tokens = ids.shape
    lane = lax.broadcasted_iota(jnp.int32, (experts, tokens), 0)
    named = jnp.zeros((experts, tokens), F32)
    for k in range(topk):
        named += (ids[k : k + 1, :] == lane).astype(F32)
    row = lax.broadcasted_iota(jnp.int32, (tokens, tokens), 0)
    col = lax.broadcasted_iota(jnp.int32, (tokens, tokens), 1)
    place = jnp.dot(named.astype(BF), (row < col).astype(BF), preferred_element_type=F32)
    return jnp.where(named > 0.5, place, -1.0)


def spread(tiles, rows):
    count = tiles[0].shape[0]
    sub = lax.broadcasted_iota(jnp.int32, (count, rows, LANES), 1)
    out = jnp.zeros((count, rows, LANES), F32)
    for c, tile in enumerate(tiles):
        out += jnp.where(sub == c, tile[:, None, :], 0.0)
    return out


def dispatch_kernel(x_ref, ids_ref, tok_ref, out_ref, own_ref, rows_ref, sem, sems):
    experts = out_ref.shape[0]
    tokens, quarter = own_ref.shape
    tiles = quarter // LANES
    part = pl.ds(pl.multiple_of(x_ref[0] * quarter, LANES), quarter)
    fetch = pltpu.make_async_copy(tok_ref.at[:, part], own_ref, sem)
    fetch.start()
    place = slots(ids_ref[...], experts)
    fetch.wait()
    tok = own_ref[...]
    last = jnp.dot((place == 16.0).astype(BF), tok, preferred_element_type=F32)
    tail = spread([last[:, c * LANES : (c + 1) * LANES] for c in range(tiles)], 8)
    rows_ref[:, tiles * 16 : tiles * 16 + 8, :] = tail.astype(BF)
    count = experts // PARTS
    slot = lax.broadcasted_iota(jnp.int32, (count, 16, tokens), 1).astype(F32)
    copies = []
    for g in range(PARTS):
        group = slice(g * count, (g + 1) * count)
        pick = jnp.where(place[group][:, None, :] == slot, 1.0, 0.0).reshape(count * 16, tokens).astype(BF)
        rows = jnp.dot(pick, tok, preferred_element_type=F32).astype(BF)
        for c in range(tiles):
            rows_ref[group, c * 16 : (c + 1) * 16, :] = rows[:, c * LANES : (c + 1) * LANES].reshape(count, 16, LANES)
        some = pl.ds(g * count, count)
        copies.append(pltpu.make_async_copy(rows_ref.at[some], out_ref.at[some], sems.at[g]))
        copies[g].start()
    for copy in copies:
        copy.wait()


def dispatch(x, ids, tokens, experts):
    count, width = tokens.shape
    quarter = width // X
    shape = (experts, quarter // LANES * 16 + 8, LANES)
    scratch = [
        pltpu.VMEM((count, quarter), BF),
        pltpu.VMEM(shape, BF),
        pltpu.SemaphoreType.DMA,
        pltpu.SemaphoreType.DMA((PARTS,)),
    ]
    specs = [in_smem(), in_vmem(), anywhere()]
    out = jax.ShapeDtypeStruct(shape, BF)
    return call(dispatch_kernel, "dispatch", out, specs, anywhere(), scratch, FULL)(x, ids, tokens)


def pack_kernel(x_ref, gate_ref, up_ref, down_ref, *refs):
    both, downs, (rows_ref, sems) = refs[:X], refs[X : 2 * X], refs[2 * X :]
    quarter = gate_ref.shape[0] // X
    depth = down_ref.shape[0]
    fetch = pltpu.make_async_copy(down_ref, rows_ref, sems.at[0])
    fetch.start()
    copies = []
    for d in (2, 1, 3, 0):
        q = lax.rem(x_ref[0] + d, X)
        part = pl.ds(pl.multiple_of(q * quarter, quarter), quarter)
        for half, ref in enumerate((gate_ref, up_ref)):
            rows = pl.ds(half * quarter, quarter)
            copies.append(pltpu.make_async_copy(ref.at[part, :], both[d].at[rows, :], sems.at[1 + len(copies)]))
            copies[-1].start()
    fetch.wait()
    for d in range(X):
        q = lax.rem(x_ref[0] + d, X)
        for z in range(2):
            p = z * X + q
            first = p // 2 * (quarter // LANES)
            for c in range(4):
                tile = first + 3 if c == 3 else first + c + 4 * lax.rem(p, 2)
                cols = pl.ds(pl.multiple_of(tile * LANES, LANES), LANES)
                downs[d][pl.ds((z * 4 + c) * depth, depth), :] = rows_ref[:, cols]
    for copy in copies:
        copy.wait()


def pack(x, w_gate, w_up, w_down):
    depth = w_down.shape[0]
    both = jax.ShapeDtypeStruct((2 * (w_gate.shape[0] // X), LANES), BF)
    downs = jax.ShapeDtypeStruct((8 * depth, LANES), BF)
    scratch = [pltpu.VMEM(w_down.shape, BF), pltpu.SemaphoreType.DMA((1 + 2 * X,))]
    specs = [in_smem()] + [anywhere()] * 3
    outs = call(pack_kernel, "pack", [both] * X + [downs] * X, specs, scratch=scratch, vmem=FULL)(x, w_gate, w_up, w_down)
    return outs[:X], outs[X:]


def swap_kernel(z_ref, *refs):
    downs, (out_ref, sems) = refs[:X], refs[X:]
    rows = out_ref.shape[0] // X
    start = pl.multiple_of((1 - z_ref[0]) * rows, rows)
    copies = []
    for d, ref in enumerate(downs):
        copies.append(pltpu.make_async_copy(ref.at[pl.ds(start, rows), :], out_ref.at[pl.ds(d * rows, rows), :], sems.at[d]))
        copies[d].start()
    for copy in copies:
        copy.wait()


def swap(z, downs):
    shape = jax.ShapeDtypeStruct((X * downs[0].shape[0] // 2, LANES), BF)
    scratch = [pltpu.SemaphoreType.DMA((X,))]
    return call(swap_kernel, "swap", shape, [in_smem()] + [anywhere()] * X, scratch=scratch, vmem=FULL)(z, *downs)


def assemble_kernel(z_ref, *refs):
    downs, (other_ref, out_ref) = refs[:X], refs[X:]
    rows = other_ref.shape[0] // X
    depth = rows // 4
    start = z_ref[0] * rows
    for d, ref in enumerate(downs):
        for c in range(4):
            cols = pl.ds(c * LANES, LANES)
            out_ref[pl.ds(d * depth, depth), cols] = ref[pl.ds(pl.multiple_of(start + c * depth, LANES), depth), :]
            out_ref[pl.ds((X + d) * depth, depth), cols] = other_ref[pl.ds(d * rows + c * depth, depth), :]


def assemble(z, downs, other):
    shape = jax.ShapeDtypeStruct((other.shape[0] // 2, 4 * LANES), BF)
    cost = pl.CostEstimate(flops=HOLD, bytes_accessed=4 * other.size, transcendentals=0)
    return call(assemble_kernel, "assemble", shape, [in_smem()] + [in_vmem()] * (X + 1), cost=cost)(z, *downs, other)


def stacked(chunks_ref):
    sources, depth, _ = chunks_ref.shape
    tiles = depth // 16
    main = [chunks_ref[:, c * 16 : (c + 1) * 16, :].reshape(sources * 16, LANES) for c in range(tiles)]
    tail = chunks_ref[:, tiles * 16 : tiles * 16 + 8, :].reshape(sources * 8, LANES)
    row = lax.broadcasted_iota(jnp.int32, (sources, sources * 8), 0)
    col = lax.broadcasted_iota(jnp.int32, (sources, sources * 8), 1)
    last = [
        jnp.dot((col == row * 8 + c).astype(BF), tail, preferred_element_type=F32).astype(BF) for c in range(tiles)
    ]
    return jnp.concatenate(main, axis=1), jnp.concatenate(last, axis=1)


def project(chunks, packs, dtype, name):
    sources, depth, _ = chunks.shape
    quarter = depth // 16 * LANES

    def kernel(chunks_ref, *refs):
        count = len(packs)
        sent, outs, (weight_ref, sems) = refs[:count], refs[count : 2 * count], refs[2 * count :]
        copies = []
        for d in range(count):
            for half in range(2):
                rows, cols = pl.ds(half * quarter, quarter), pl.ds(half * LANES, LANES)
                copy = pltpu.make_async_copy(sent[d].at[rows, :], weight_ref.at[d, :, cols], sems.at[d, half])
                copy.start()
                copies.append(copy)
        main, last = stacked(chunks_ref)
        for d in range(count):
            copies[2 * d].wait()
            copies[2 * d + 1].wait()
            weight = weight_ref[d]
            outs[d][pl.ds(0, sources * 16), :] = jnp.dot(main, weight, preferred_element_type=F32).astype(dtype)
            outs[d][pl.ds(sources * 16, sources), :] = jnp.dot(last, weight, preferred_element_type=F32).astype(dtype)

    shapes = [jax.ShapeDtypeStruct((sources * 17, 2 * LANES), dtype)] * len(packs)
    scratch = [pltpu.VMEM((len(packs), quarter, 2 * LANES), BF), pltpu.SemaphoreType.DMA((len(packs), 2))]
    specs = [in_vmem()] + [anywhere()] * len(packs)
    return call(kernel, name, shapes, specs, scratch=scratch)(chunks, *packs)


def activate_kernel(own_ref, *refs):
    parts, out_ref = refs[:-1], refs[-1]
    total = own_ref[...]
    for ref in parts:
        total += ref[...].astype(F32)
    gate, up = total[:, :LANES], total[:, LANES:]
    out_ref[...] = (gate / (1.0 + jnp.exp(-gate)) * up).astype(BF)


def activate(own, parts):
    shape = jax.ShapeDtypeStruct((own.shape[0], LANES), BF)
    return call(activate_kernel, "activate", shape, [in_vmem()] * (1 + len(parts)))(own, *parts)


def down_kernel(x_ref, weight_ref, *refs):
    hiddens, out_ref = refs[:-1], refs[-1]
    experts = out_ref.shape[0]
    hidden = jnp.concatenate([ref[...] for ref in hiddens], axis=1)
    weight = weight_ref[...]
    count = experts * 16
    main = jnp.dot(hidden[:count], weight, preferred_element_type=F32)
    last = jnp.dot(hidden[count:], weight, preferred_element_type=F32)
    for c in range(3):
        out_ref[:, c * 16 : (c + 1) * 16, :] = (
            main[:, c * LANES : (c + 1) * LANES].astype(BF).reshape(experts, 16, LANES)
        )
    half = main[:, 3 * LANES :]
    turned = pltpu.roll(half, LANES // 2, 1)
    odd = lax.rem(x_ref[0], 2) == 1
    low = jnp.where(odd, turned, half).reshape(experts, 16, LANES)[:, :8]
    high = jnp.where(odd, half, turned).reshape(experts, 16, LANES)[:, 8:]
    lane = lax.broadcasted_iota(jnp.int32, low.shape, 2)
    halves = jnp.where(lane < LANES // 2, low, high)
    tail = spread([last[:, c * LANES : (c + 1) * LANES] for c in range(4)], 8)
    out_ref[:, 48:64, :] = jnp.concatenate([halves, tail], axis=1).astype(BF)


def down(x, weight, hiddens, experts):
    shape = jax.ShapeDtypeStruct((experts, 64, LANES), BF)
    specs = [in_smem()] + [in_vmem()] * (1 + len(hiddens))
    return call(down_kernel, "down", shape, specs)(x, weight, *hiddens)


def combine_kernel(x_ref, ids_ref, scale_ref, chunks_ref, out_ref):
    experts = chunks_ref.shape[0]
    ids, scale = ids_ref[...], scale_ref[...]
    topk, tokens = ids.shape
    place = slots(ids, experts)
    lane = lax.broadcasted_iota(jnp.int32, (experts, tokens), 0)
    weight = jnp.zeros((experts, tokens), F32)
    for k in range(topk):
        weight += jnp.where(ids[k : k + 1, :] == lane, scale[k : k + 1, :], 0.0)
    upper = weight.astype(BF).astype(F32)
    lower = weight - upper
    sub = lax.broadcasted_iota(jnp.int32, (experts, 16, tokens), 1)
    slot = sub.astype(F32)
    place = place[:, None, :]
    contract = (((0,), (0,)), ((), ()))
    main = jnp.concatenate(
        [chunks_ref[:, c * 16 : (c + 1) * 16, :].reshape(experts * 16, LANES) for c in range(3)], axis=1
    )
    rest = chunks_ref[:, 48:64, :].reshape(experts * 16, LANES)
    whole = jnp.zeros((tokens, 3 * LANES), F32)
    low = jnp.zeros((tokens, LANES), F32)
    high = jnp.zeros((tokens, LANES), F32)
    ends = [jnp.zeros((tokens, LANES), F32) for _ in range(4)]

    def times(hit, part, rows):
        coef = jnp.where(hit, part[:, None, :], 0.0).reshape(experts * 16, tokens).astype(BF)
        return lax.dot_general(coef, rows, contract, preferred_element_type=F32)

    for part in (upper, lower):
        whole += times(place == slot, part, main)
        low += times((place == slot) & (sub < 8), part, rest)
        high += times((place == slot + 8.0) & (sub < 8), part, rest)
        for c in range(4):
            ends[c] += times((place == 16.0) & (sub == 8 + c), part, rest)
    odd = lax.rem(x_ref[0], 2) == 1
    even_half = low + pltpu.roll(high, LANES // 2, 1) + ends[3]
    odd_half = pltpu.roll(low, LANES // 2, 1) + high + ends[3]
    half = jnp.where(odd, odd_half, even_half)
    total = jnp.concatenate([whole + jnp.concatenate(ends[:3], axis=1), half], axis=1)
    total = jnp.where(odd, pltpu.roll(total, LANES // 2, 1), total)
    out_ref[...] = total[:, : out_ref.shape[1]].astype(BF)


def combine(x, ids, scale, chunks, columns):
    shape = jax.ShapeDtypeStruct((ids.shape[1], columns), BF)
    return call(combine_kernel, "combine", shape, [in_smem()] + [in_vmem()] * 3)(x, ids, scale, chunks)


def shift(value, d):
    pairs = [(z * X + x, z * X + (x + d) % X) for z in range(2) for x in range(X)]
    return lax.ppermute(value, "pipe", pairs)


def cross(value):
    return lax.ppermute(value, "pipe", [(p, (p + X) % (2 * X)) for p in range(2 * X)])


def body(tokens, expert_ids, gate_scale, w_gate, w_up, w_down):
    groups = lax.axis_size("expert")
    pipe = lax.axis_index("pipe")
    x = (pipe & (X - 1)).reshape(1)
    z = (pipe >> 2).reshape(1)
    ids, scale = expert_ids.T, gate_scale.T
    w_gate, w_up, w_down = w_gate[0], w_up[0], w_down[0]
    buffer = dispatch(x, ids, tokens, groups)
    chunks = lax.all_to_all(buffer, "expert", split_axis=0, concat_axis=0, tiled=True)
    both, downs = pack(x, w_gate, w_up, w_down)
    both = [both[0]] + [shift(both[d], d) for d in range(1, X)]
    downs = [downs[0]] + [shift(downs[d], d) for d in range(1, X)]
    held = lax.optimization_barrier((*both, *downs))
    both, downs = held[:X], held[X:]
    other = cross(swap(z, downs))
    parts = project(chunks, [both[d] for d in (2, 1, 3)], BF, "project_sent")
    arrived = [shift(part, -d) for d, part in zip((2, 1, 3), parts)]
    chunks, weight = lax.optimization_barrier((chunks, assemble(z, downs, other)))
    (mine,) = project(chunks, both[:1], F32, "project_own")
    hidden = activate(mine, arrived)
    swapped = cross(hidden)
    hiddens = [hidden] + [shift(hidden, d) for d in range(1, X)]
    hiddens += [swapped] + [shift(swapped, d) for d in range(1, X)]
    output = down(x, weight, hiddens, groups)
    returned = lax.all_to_all(output, "expert", split_axis=0, concat_axis=0, tiled=True)
    return combine(x, ids, scale, returned, tokens.shape[1] // (2 * X))


def solution(mesh):
    placed = (
        P("expert", None),
        P("expert", None),
        P("expert", None),
        P("expert", None, "pipe"),
        P("expert", None, "pipe"),
        P("expert", "pipe", None),
    )
    return jax.shard_map(
        body, mesh=mesh, in_specs=placed, out_specs=P("expert", "pipe"), check_vma=False
    )
```

```python
import jax
import jax.numpy as jnp
from jax import lax
from jax.experimental import pallas as pl
from jax.experimental.pallas import tpu as pltpu
from jax.sharding import PartitionSpec as P

BF = jnp.bfloat16
F32 = jnp.float32
LANES = 128
X = 4
ORDER = (1, 3, 2)
PARTS = 4
HOLD = 50_000_000_000
FULL = 60 * 1024 * 1024
VMEM = 16 * 1024 * 1024


def call(kernel, name, out_shape, in_specs, out_specs=None, scratch=(), vmem=VMEM, cost=None):
    if out_specs is None:
        out_specs = jax.tree.map(lambda _: in_vmem(), out_shape)
    return pl.pallas_call(
        kernel,
        out_shape=out_shape,
        in_specs=in_specs,
        out_specs=out_specs,
        scratch_shapes=scratch,
        compiler_params=pltpu.CompilerParams(vmem_limit_bytes=vmem),
        cost_estimate=cost,
        name=name,
    )


def in_vmem():
    return pl.BlockSpec(memory_space=pltpu.VMEM)


def anywhere():
    return pl.BlockSpec(memory_space=pl.ANY)


def in_smem():
    return pl.BlockSpec(memory_space=pltpu.SMEM)


def slots(ids, experts):
    topk, tokens = ids.shape
    lane = lax.broadcasted_iota(jnp.int32, (experts, tokens), 0)
    named = jnp.zeros((experts, tokens), F32)
    for k in range(topk):
        named += (ids[k : k + 1, :] == lane).astype(F32)
    row = lax.broadcasted_iota(jnp.int32, (tokens, tokens), 0)
    col = lax.broadcasted_iota(jnp.int32, (tokens, tokens), 1)
    place = jnp.dot(named.astype(BF), (row < col).astype(BF), preferred_element_type=F32)
    return jnp.where(named > 0.5, place, -1.0)


def spread(tiles, rows):
    count = tiles[0].shape[0]
    sub = lax.broadcasted_iota(jnp.int32, (count, rows, LANES), 1)
    out = jnp.zeros((count, rows, LANES), F32)
    for c, tile in enumerate(tiles):
        out += jnp.where(sub == c, tile[:, None, :], 0.0)
    return out


def dispatch_kernel(x_ref, ids_ref, tok_ref, out_ref, own_ref, rows_ref, sem, sems):
    experts = out_ref.shape[0]
    tokens, quarter = own_ref.shape
    tiles = quarter // LANES
    part = pl.ds(pl.multiple_of(x_ref[0] * quarter, LANES), quarter)
    fetch = pltpu.make_async_copy(tok_ref.at[:, part], own_ref, sem)
    fetch.start()
    place = slots(ids_ref[...], experts)
    fetch.wait()
    tok = own_ref[...]
    last = jnp.dot((place == 16.0).astype(BF), tok, preferred_element_type=F32)
    tail = spread([last[:, c * LANES : (c + 1) * LANES] for c in range(tiles)], 8)
    rows_ref[:, tiles * 16 : tiles * 16 + 8, :] = tail.astype(BF)
    count = experts // PARTS
    slot = lax.broadcasted_iota(jnp.int32, (count, 16, tokens), 1).astype(F32)
    copies = []
    for g in range(PARTS):
        group = slice(g * count, (g + 1) * count)
        pick = jnp.where(place[group][:, None, :] == slot, 1.0, 0.0).reshape(count * 16, tokens).astype(BF)
        rows = jnp.dot(pick, tok, preferred_element_type=F32).astype(BF)
        for c in range(tiles):
            rows_ref[group, c * 16 : (c + 1) * 16, :] = rows[:, c * LANES : (c + 1) * LANES].reshape(count, 16, LANES)
        some = pl.ds(g * count, count)
        copies.append(pltpu.make_async_copy(rows_ref.at[some], out_ref.at[some], sems.at[g]))
        copies[g].start()
    for copy in copies:
        copy.wait()


def dispatch(x, ids, tokens, experts):
    count, width = tokens.shape
    quarter = width // X
    shape = (experts, quarter // LANES * 16 + 8, LANES)
    scratch = [
        pltpu.VMEM((count, quarter), BF),
        pltpu.VMEM(shape, BF),
        pltpu.SemaphoreType.DMA,
        pltpu.SemaphoreType.DMA((PARTS,)),
    ]
    specs = [in_smem(), in_vmem(), anywhere()]
    out = jax.ShapeDtypeStruct(shape, BF)
    return call(dispatch_kernel, "dispatch", out, specs, anywhere(), scratch, FULL)(x, ids, tokens)


def pack_kernel(x_ref, gate_ref, up_ref, down_ref, *refs):
    both, downs, (rows_ref, sems) = refs[:X], refs[X : 2 * X], refs[2 * X :]
    quarter = gate_ref.shape[0] // X
    depth = down_ref.shape[0]
    fetch = pltpu.make_async_copy(down_ref, rows_ref, sems.at[0])
    fetch.start()
    copies = []
    for d in (2, 1, 3, 0):
        q = lax.rem(x_ref[0] + d, X)
        part = pl.ds(pl.multiple_of(q * quarter, quarter), quarter)
        for half, ref in enumerate((gate_ref, up_ref)):
            rows = pl.ds(half * quarter, quarter)
            copies.append(pltpu.make_async_copy(ref.at[part, :], both[d].at[rows, :], sems.at[1 + len(copies)]))
            copies[-1].start()
    fetch.wait()
    for d in range(X):
        q = lax.rem(x_ref[0] + d, X)
        for z in range(2):
            p = z * X + q
            first = p // 2 * (quarter // LANES)
            for c in range(4):
                tile = first + 3 if c == 3 else first + c + 4 * lax.rem(p, 2)
                cols = pl.ds(pl.multiple_of(tile * LANES, LANES), LANES)
                downs[d][pl.ds((z * 4 + c) * depth, depth), :] = rows_ref[:, cols]
    for copy in copies:
        copy.wait()


def pack(x, w_gate, w_up, w_down):
    depth = w_down.shape[0]
    both = jax.ShapeDtypeStruct((2 * (w_gate.shape[0] // X), LANES), BF)
    downs = jax.ShapeDtypeStruct((8 * depth, LANES), BF)
    scratch = [pltpu.VMEM(w_down.shape, BF), pltpu.SemaphoreType.DMA((1 + 2 * X,))]
    specs = [in_smem()] + [anywhere()] * 3
    outs = call(pack_kernel, "pack", [both] * X + [downs] * X, specs, scratch=scratch, vmem=FULL)(x, w_gate, w_up, w_down)
    return outs[:X], outs[X:]


def swap_kernel(z_ref, *refs):
    downs, (out_ref, sems) = refs[:X], refs[X:]
    rows = out_ref.shape[0] // X
    start = pl.multiple_of((1 - z_ref[0]) * rows, rows)
    copies = []
    for d, ref in enumerate(downs):
        copies.append(pltpu.make_async_copy(ref.at[pl.ds(start, rows), :], out_ref.at[pl.ds(d * rows, rows), :], sems.at[d]))
        copies[d].start()
    for copy in copies:
        copy.wait()


def swap(z, downs):
    shape = jax.ShapeDtypeStruct((X * downs[0].shape[0] // 2, LANES), BF)
    scratch = [pltpu.SemaphoreType.DMA((X,))]
    return call(swap_kernel, "swap", shape, [in_smem()] + [anywhere()] * X, scratch=scratch, vmem=FULL)(z, *downs)


def assemble_kernel(z_ref, *refs):
    downs, (other_ref, out_ref) = refs[:X], refs[X:]
    rows = other_ref.shape[0] // X
    depth = rows // 4
    start = z_ref[0] * rows
    for d, ref in enumerate(downs):
        for c in range(4):
            cols = pl.ds(c * LANES, LANES)
            out_ref[pl.ds(d * depth, depth), cols] = ref[pl.ds(pl.multiple_of(start + c * depth, LANES), depth), :]
            out_ref[pl.ds((X + d) * depth, depth), cols] = other_ref[pl.ds(d * rows + c * depth, depth), :]


def assemble(z, downs, other):
    shape = jax.ShapeDtypeStruct((other.shape[0] // 2, 4 * LANES), BF)
    cost = pl.CostEstimate(flops=HOLD, bytes_accessed=4 * other.size, transcendentals=0)
    return call(assemble_kernel, "assemble", shape, [in_smem()] + [in_vmem()] * (X + 1), cost=cost)(z, *downs, other)


def stacked(chunks_ref):
    sources, depth, _ = chunks_ref.shape
    tiles = depth // 16
    main = [chunks_ref[:, c * 16 : (c + 1) * 16, :].reshape(sources * 16, LANES) for c in range(tiles)]
    tail = chunks_ref[:, tiles * 16 : tiles * 16 + 8, :].reshape(sources * 8, LANES)
    row = lax.broadcasted_iota(jnp.int32, (sources, sources * 8), 0)
    col = lax.broadcasted_iota(jnp.int32, (sources, sources * 8), 1)
    last = [
        jnp.dot((col == row * 8 + c).astype(BF), tail, preferred_element_type=F32).astype(BF) for c in range(tiles)
    ]
    return jnp.concatenate(main, axis=1), jnp.concatenate(last, axis=1)


def project(chunks, packs, dtype, name):
    sources, depth, _ = chunks.shape
    quarter = depth // 16 * LANES

    def kernel(chunks_ref, *refs):
        count = len(packs)
        sent, outs, (weight_ref, sems) = refs[:count], refs[count : 2 * count], refs[2 * count :]
        copies = []
        for d in range(count):
            for half in range(2):
                rows, cols = pl.ds(half * quarter, quarter), pl.ds(half * LANES, LANES)
                copy = pltpu.make_async_copy(sent[d].at[rows, :], weight_ref.at[d, :, cols], sems.at[d, half])
                copy.start()
                copies.append(copy)
        main, last = stacked(chunks_ref)
        for d in range(count):
            copies[2 * d].wait()
            copies[2 * d + 1].wait()
            weight = weight_ref[d]
            outs[d][pl.ds(0, sources * 16), :] = jnp.dot(main, weight, preferred_element_type=F32).astype(dtype)
            outs[d][pl.ds(sources * 16, sources), :] = jnp.dot(last, weight, preferred_element_type=F32).astype(dtype)

    shapes = [jax.ShapeDtypeStruct((sources * 17, 2 * LANES), dtype)] * len(packs)
    scratch = [pltpu.VMEM((len(packs), quarter, 2 * LANES), BF), pltpu.SemaphoreType.DMA((len(packs), 2))]
    specs = [in_vmem()] + [anywhere()] * len(packs)
    return call(kernel, name, shapes, specs, scratch=scratch)(chunks, *packs)


def activate_kernel(own_ref, *refs):
    parts, out_ref = refs[:-1], refs[-1]
    total = own_ref[...]
    for ref in parts:
        total += ref[...].astype(F32)
    gate, up = total[:, :LANES], total[:, LANES:]
    out_ref[...] = (gate / (1.0 + jnp.exp(-gate)) * up).astype(BF)


def activate(own, parts):
    shape = jax.ShapeDtypeStruct((own.shape[0], LANES), BF)
    return call(activate_kernel, "activate", shape, [in_vmem()] * (1 + len(parts)))(own, *parts)


def down_kernel(x_ref, weight_ref, *refs):
    hiddens, out_ref = refs[:-1], refs[-1]
    experts = out_ref.shape[0]
    hidden = jnp.concatenate([hiddens[i][...] for i in (0, 3, 2, 1, 4, 7, 6, 5)], axis=1)
    weight = weight_ref[...]
    count = experts * 16
    main = jnp.dot(hidden[:count], weight, preferred_element_type=F32)
    last = jnp.dot(hidden[count:], weight, preferred_element_type=F32)
    for c in range(3):
        out_ref[:, c * 16 : (c + 1) * 16, :] = (
            main[:, c * LANES : (c + 1) * LANES].astype(BF).reshape(experts, 16, LANES)
        )
    half = main[:, 3 * LANES :]
    turned = pltpu.roll(half, LANES // 2, 1)
    odd = lax.rem(x_ref[0], 2) == 1
    low = jnp.where(odd, turned, half).reshape(experts, 16, LANES)[:, :8]
    high = jnp.where(odd, half, turned).reshape(experts, 16, LANES)[:, 8:]
    lane = lax.broadcasted_iota(jnp.int32, low.shape, 2)
    halves = jnp.where(lane < LANES // 2, low, high)
    tail = spread([last[:, c * LANES : (c + 1) * LANES] for c in range(4)], 8)
    out_ref[:, 48:64, :] = jnp.concatenate([halves, tail], axis=1).astype(BF)


def down(x, weight, hiddens, experts):
    shape = jax.ShapeDtypeStruct((experts, 64, LANES), BF)
    specs = [in_smem()] + [in_vmem()] * (1 + len(hiddens))
    return call(down_kernel, "down", shape, specs)(x, weight, *hiddens)


def combine_kernel(x_ref, ids_ref, scale_ref, chunks_ref, out_ref):
    experts = chunks_ref.shape[0]
    ids, scale = ids_ref[...], scale_ref[...]
    topk, tokens = ids.shape
    place = slots(ids, experts)
    lane = lax.broadcasted_iota(jnp.int32, (experts, tokens), 0)
    weight = jnp.zeros((experts, tokens), F32)
    for k in range(topk):
        weight += jnp.where(ids[k : k + 1, :] == lane, scale[k : k + 1, :], 0.0)
    upper = weight.astype(BF).astype(F32)
    lower = weight - upper
    sub = lax.broadcasted_iota(jnp.int32, (experts, 16, tokens), 1)
    slot = sub.astype(F32)
    place = place[:, None, :]
    contract = (((0,), (0,)), ((), ()))
    main = jnp.concatenate(
        [chunks_ref[:, c * 16 : (c + 1) * 16, :].reshape(experts * 16, LANES) for c in range(3)], axis=1
    )
    rest = chunks_ref[:, 48:64, :].reshape(experts * 16, LANES)
    whole = jnp.zeros((tokens, 3 * LANES), F32)
    low = jnp.zeros((tokens, LANES), F32)
    high = jnp.zeros((tokens, LANES), F32)
    ends = [jnp.zeros((tokens, LANES), F32) for _ in range(4)]

    def times(hit, part, rows):
        coef = jnp.where(hit, part[:, None, :], 0.0).reshape(experts * 16, tokens).astype(BF)
        return lax.dot_general(coef, rows, contract, preferred_element_type=F32)

    for part in (upper, lower):
        whole += times(place == slot, part, main)
        low += times((place == slot) & (sub < 8), part, rest)
        high += times((place == slot + 8.0) & (sub < 8), part, rest)
        for c in range(4):
            ends[c] += times((place == 16.0) & (sub == 8 + c), part, rest)
    odd = lax.rem(x_ref[0], 2) == 1
    even_half = low + pltpu.roll(high, LANES // 2, 1) + ends[3]
    odd_half = pltpu.roll(low, LANES // 2, 1) + high + ends[3]
    half = jnp.where(odd, odd_half, even_half)
    total = jnp.concatenate([whole + jnp.concatenate(ends[:3], axis=1), half], axis=1)
    total = jnp.where(odd, pltpu.roll(total, LANES // 2, 1), total)
    out_ref[...] = total[:, : out_ref.shape[1]].astype(BF)


def combine(x, ids, scale, chunks, columns):
    shape = jax.ShapeDtypeStruct((ids.shape[1], columns), BF)
    return call(combine_kernel, "combine", shape, [in_smem()] + [in_vmem()] * 3)(x, ids, scale, chunks)


def shift(value, d):
    pairs = [(z * X + x, z * X + (x + d) % X) for z in range(2) for x in range(X)]
    return lax.ppermute(value, "pipe", pairs)


def cross(value):
    return lax.ppermute(value, "pipe", [(p, (p + X) % (2 * X)) for p in range(2 * X)])


def body(tokens, expert_ids, gate_scale, w_gate, w_up, w_down):
    groups = lax.axis_size("expert")
    pipe = lax.axis_index("pipe")
    x = (pipe & (X - 1)).reshape(1)
    z = (pipe >> 2).reshape(1)
    ids, scale = expert_ids.T, gate_scale.T
    w_gate, w_up, w_down = w_gate[0], w_up[0], w_down[0]
    buffer = dispatch(x, ids, tokens, groups)
    chunks = lax.all_to_all(buffer, "expert", split_axis=0, concat_axis=0, tiled=True)
    both, downs = pack(x, w_gate, w_up, w_down)
    both = [both[0]] + [shift(both[d], d) for d in ORDER]
    downs = [downs[0]] + [shift(downs[d], d) for d in ORDER]
    held = lax.optimization_barrier((*both, *downs))
    both, downs = held[:X], held[X:]
    other = cross(swap(z, downs))
    parts = project(chunks, both[1:], BF, "project_sent")
    arrived = [shift(part, -d) for d, part in zip(ORDER, parts)]
    chunks, weight = lax.optimization_barrier((chunks, assemble(z, downs, other)))
    (mine,) = project(chunks, both[:1], F32, "project_own")
    hidden = activate(mine, arrived)
    swapped = cross(hidden)
    hiddens = [hidden] + [shift(hidden, d) for d in ORDER[::-1]]
    hiddens += [swapped] + [shift(swapped, d) for d in ORDER[::-1]]
    output = down(x, weight, hiddens, groups)
    returned = lax.all_to_all(output, "expert", split_axis=0, concat_axis=0, tiled=True)
    return combine(x, ids, scale, returned, tokens.shape[1] // (2 * X))


def solution(mesh):
    placed = (
        P("expert", None),
        P("expert", None),
        P("expert", None),
        P("expert", None, "pipe"),
        P("expert", None, "pipe"),
        P("expert", "pipe", None),
    )
    return jax.shard_map(
        body, mesh=mesh, in_specs=placed, out_specs=P("expert", "pipe"), check_vma=False
    )
```

```python
import jax
import jax.numpy as jnp
from jax import lax
from jax.experimental import pallas as pl
from jax.experimental.pallas import tpu as pltpu
from jax.sharding import PartitionSpec as P

BF = jnp.bfloat16
F32 = jnp.float32
LANES = 128
X = 4
ORDER = (1, 3, 2)
PARTS = 4
HOLD = 50_000_000_000
FULL = 60 * 1024 * 1024
VMEM = 16 * 1024 * 1024


def call(kernel, name, out_shape, in_specs, out_specs=None, scratch=(), vmem=VMEM, cost=None):
    if out_specs is None:
        out_specs = jax.tree.map(lambda _: in_vmem(), out_shape)
    return pl.pallas_call(
        kernel,
        out_shape=out_shape,
        in_specs=in_specs,
        out_specs=out_specs,
        scratch_shapes=scratch,
        compiler_params=pltpu.CompilerParams(vmem_limit_bytes=vmem),
        cost_estimate=cost,
        name=name,
    )


def in_vmem():
    return pl.BlockSpec(memory_space=pltpu.VMEM)


def anywhere():
    return pl.BlockSpec(memory_space=pl.ANY)


def in_smem():
    return pl.BlockSpec(memory_space=pltpu.SMEM)


def slots(ids, experts):
    topk, tokens = ids.shape
    lane = lax.broadcasted_iota(jnp.int32, (experts, tokens), 0)
    named = jnp.zeros((experts, tokens), F32)
    for k in range(topk):
        named += (ids[k : k + 1, :] == lane).astype(F32)
    row = lax.broadcasted_iota(jnp.int32, (tokens, tokens), 0)
    col = lax.broadcasted_iota(jnp.int32, (tokens, tokens), 1)
    place = jnp.dot(named.astype(BF), (row < col).astype(BF), preferred_element_type=F32)
    return jnp.where(named > 0.5, place, -1.0)


def spread(tiles, rows):
    count = tiles[0].shape[0]
    sub = lax.broadcasted_iota(jnp.int32, (count, rows, LANES), 1)
    out = jnp.zeros((count, rows, LANES), F32)
    for c, tile in enumerate(tiles):
        out += jnp.where(sub == c, tile[:, None, :], 0.0)
    return out


def dispatch_kernel(x_ref, ids_ref, tok_ref, out_ref, own_ref, rows_ref, sem, sems):
    experts = out_ref.shape[0]
    tokens, quarter = own_ref.shape
    tiles = quarter // LANES
    part = pl.ds(pl.multiple_of(x_ref[0] * quarter, LANES), quarter)
    fetch = pltpu.make_async_copy(tok_ref.at[:, part], own_ref, sem)
    fetch.start()
    place = slots(ids_ref[...], experts)
    fetch.wait()
    tok = own_ref[...]
    last = jnp.dot((place == 16.0).astype(BF), tok, preferred_element_type=F32)
    tail = spread([last[:, c * LANES : (c + 1) * LANES] for c in range(tiles)], 8)
    rows_ref[:, tiles * 16 : tiles * 16 + 8, :] = tail.astype(BF)
    count = experts // PARTS
    slot = lax.broadcasted_iota(jnp.int32, (count, 16, tokens), 1).astype(F32)
    copies = []
    for g in range(PARTS):
        group = slice(g * count, (g + 1) * count)
        pick = jnp.where(place[group][:, None, :] == slot, 1.0, 0.0).reshape(count * 16, tokens).astype(BF)
        rows = jnp.dot(pick, tok, preferred_element_type=F32).astype(BF)
        for c in range(tiles):
            rows_ref[group, c * 16 : (c + 1) * 16, :] = rows[:, c * LANES : (c + 1) * LANES].reshape(count, 16, LANES)
        some = pl.ds(g * count, count)
        copies.append(pltpu.make_async_copy(rows_ref.at[some], out_ref.at[some], sems.at[g]))
        copies[g].start()
    for copy in copies:
        copy.wait()


def dispatch(x, ids, tokens, experts):
    count, width = tokens.shape
    quarter = width // X
    shape = (experts, quarter // LANES * 16 + 8, LANES)
    scratch = [
        pltpu.VMEM((count, quarter), BF),
        pltpu.VMEM(shape, BF),
        pltpu.SemaphoreType.DMA,
        pltpu.SemaphoreType.DMA((PARTS,)),
    ]
    specs = [in_smem(), in_vmem(), anywhere()]
    out = jax.ShapeDtypeStruct(shape, BF)
    return call(dispatch_kernel, "dispatch", out, specs, anywhere(), scratch, FULL)(x, ids, tokens)


def pack_kernel(x_ref, gate_ref, up_ref, down_ref, *refs):
    both, downs, (rows_ref, sems) = refs[:X], refs[X : 2 * X], refs[2 * X :]
    quarter = gate_ref.shape[0] // X
    depth = down_ref.shape[0]
    fetch = pltpu.make_async_copy(down_ref, rows_ref, sems.at[0])
    fetch.start()
    copies = []
    for d in (2, 1, 3, 0):
        q = lax.rem(x_ref[0] + d, X)
        part = pl.ds(pl.multiple_of(q * quarter, quarter), quarter)
        for half, ref in enumerate((gate_ref, up_ref)):
            rows = pl.ds(half * quarter, quarter)
            copies.append(pltpu.make_async_copy(ref.at[part, :], both[d].at[rows, :], sems.at[1 + len(copies)]))
            copies[-1].start()
    fetch.wait()
    for d in range(X):
        q = lax.rem(x_ref[0] + d, X)
        for z in range(2):
            p = z * X + q
            first = p // 2 * (quarter // LANES)
            for c in range(4):
                tile = first + 3 if c == 3 else first + c + 4 * lax.rem(p, 2)
                cols = pl.ds(pl.multiple_of(tile * LANES, LANES), LANES)
                downs[d][pl.ds((z * 4 + c) * depth, depth), :] = rows_ref[:, cols]
    for copy in copies:
        copy.wait()


def pack(x, w_gate, w_up, w_down):
    depth = w_down.shape[0]
    both = jax.ShapeDtypeStruct((2 * (w_gate.shape[0] // X), LANES), BF)
    downs = jax.ShapeDtypeStruct((8 * depth, LANES), BF)
    scratch = [pltpu.VMEM(w_down.shape, BF), pltpu.SemaphoreType.DMA((1 + 2 * X,))]
    specs = [in_smem()] + [anywhere()] * 3
    outs = call(pack_kernel, "pack", [both] * X + [downs] * X, specs, scratch=scratch, vmem=FULL)(x, w_gate, w_up, w_down)
    return outs[:X], outs[X:]


def swap_kernel(z_ref, *refs):
    downs, (out_ref, sems) = refs[:X], refs[X:]
    rows = out_ref.shape[0] // X
    start = pl.multiple_of((1 - z_ref[0]) * rows, rows)
    copies = []
    for d, ref in enumerate(downs):
        copies.append(pltpu.make_async_copy(ref.at[pl.ds(start, rows), :], out_ref.at[pl.ds(d * rows, rows), :], sems.at[d]))
        copies[d].start()
    for copy in copies:
        copy.wait()


def swap(z, downs):
    shape = jax.ShapeDtypeStruct((X * downs[0].shape[0] // 2, LANES), BF)
    scratch = [pltpu.SemaphoreType.DMA((X,))]
    return call(swap_kernel, "swap", shape, [in_smem()] + [anywhere()] * X, scratch=scratch, vmem=FULL)(z, *downs)


def assemble_kernel(z_ref, *refs):
    downs, (other_ref, out_ref) = refs[:X], refs[X:]
    rows = other_ref.shape[0] // X
    depth = rows // 4
    start = z_ref[0] * rows
    for d, ref in enumerate(downs):
        for c in range(4):
            cols = pl.ds(c * LANES, LANES)
            out_ref[pl.ds(d * depth, depth), cols] = ref[pl.ds(pl.multiple_of(start + c * depth, LANES), depth), :]
            out_ref[pl.ds((X + d) * depth, depth), cols] = other_ref[pl.ds(d * rows + c * depth, depth), :]


def assemble(z, downs, other):
    shape = jax.ShapeDtypeStruct((other.shape[0] // 2, 4 * LANES), BF)
    cost = pl.CostEstimate(flops=HOLD, bytes_accessed=4 * other.size, transcendentals=0)
    return call(assemble_kernel, "assemble", shape, [in_smem()] + [in_vmem()] * (X + 1), cost=cost)(z, *downs, other)


def stacked(chunks_ref):
    sources, depth, _ = chunks_ref.shape
    tiles = depth // 16
    main = [chunks_ref[:, c * 16 : (c + 1) * 16, :].reshape(sources * 16, LANES) for c in range(tiles)]
    tail = chunks_ref[:, tiles * 16 : tiles * 16 + 8, :].reshape(sources * 8, LANES)
    row = lax.broadcasted_iota(jnp.int32, (sources, sources * 8), 0)
    col = lax.broadcasted_iota(jnp.int32, (sources, sources * 8), 1)
    last = [
        jnp.dot((col == row * 8 + c).astype(BF), tail, preferred_element_type=F32).astype(BF) for c in range(tiles)
    ]
    return jnp.concatenate(main, axis=1), jnp.concatenate(last, axis=1)


def project(chunks, packs, dtype, name):
    sources, depth, _ = chunks.shape
    quarter = depth // 16 * LANES

    def kernel(chunks_ref, *refs):
        sent, outs = refs[: len(packs)], refs[len(packs) :]
        main, last = stacked(chunks_ref)
        for pack_ref, out_ref in zip(sent, outs):
            weight = jnp.concatenate([pack_ref[pl.ds(0, quarter), :], pack_ref[pl.ds(quarter, quarter), :]], axis=1)
            out_ref[pl.ds(0, sources * 16), :] = jnp.dot(main, weight, preferred_element_type=F32).astype(dtype)
            out_ref[pl.ds(sources * 16, sources), :] = jnp.dot(last, weight, preferred_element_type=F32).astype(dtype)

    shapes = [jax.ShapeDtypeStruct((sources * 17, 2 * LANES), dtype)] * len(packs)
    return call(kernel, name, shapes, [in_vmem()] * (1 + len(packs)))(chunks, *packs)


def activate_kernel(own_ref, *refs):
    parts, out_ref = refs[:-1], refs[-1]
    total = own_ref[...]
    for ref in parts:
        total += ref[...].astype(F32)
    gate, up = total[:, :LANES], total[:, LANES:]
    out_ref[...] = (gate / (1.0 + jnp.exp(-gate)) * up).astype(BF)


def activate(own, parts):
    shape = jax.ShapeDtypeStruct((own.shape[0], LANES), BF)
    return call(activate_kernel, "activate", shape, [in_vmem()] * (1 + len(parts)))(own, *parts)


def down_kernel(x_ref, weight_ref, *refs):
    hiddens, out_ref = refs[:-1], refs[-1]
    experts = out_ref.shape[0]
    hidden = jnp.concatenate([hiddens[i][...] for i in (0, 3, 2, 1, 4, 7, 6, 5)], axis=1)
    weight = weight_ref[...]
    count = experts * 16
    main = jnp.dot(hidden[:count], weight, preferred_element_type=F32)
    last = jnp.dot(hidden[count:], weight, preferred_element_type=F32)
    for c in range(3):
        out_ref[:, c * 16 : (c + 1) * 16, :] = (
            main[:, c * LANES : (c + 1) * LANES].astype(BF).reshape(experts, 16, LANES)
        )
    half = main[:, 3 * LANES :]
    turned = pltpu.roll(half, LANES // 2, 1)
    odd = lax.rem(x_ref[0], 2) == 1
    low = jnp.where(odd, turned, half).reshape(experts, 16, LANES)[:, :8]
    high = jnp.where(odd, half, turned).reshape(experts, 16, LANES)[:, 8:]
    lane = lax.broadcasted_iota(jnp.int32, low.shape, 2)
    halves = jnp.where(lane < LANES // 2, low, high)
    tail = spread([last[:, c * LANES : (c + 1) * LANES] for c in range(4)], 8)
    out_ref[:, 48:64, :] = jnp.concatenate([halves, tail], axis=1).astype(BF)


def down(x, weight, hiddens, experts):
    shape = jax.ShapeDtypeStruct((experts, 64, LANES), BF)
    specs = [in_smem()] + [in_vmem()] * (1 + len(hiddens))
    return call(down_kernel, "down", shape, specs)(x, weight, *hiddens)


def combine_kernel(x_ref, ids_ref, scale_ref, chunks_ref, out_ref):
    experts = chunks_ref.shape[0]
    ids, scale = ids_ref[...], scale_ref[...]
    topk, tokens = ids.shape
    place = slots(ids, experts)
    lane = lax.broadcasted_iota(jnp.int32, (experts, tokens), 0)
    weight = jnp.zeros((experts, tokens), F32)
    for k in range(topk):
        weight += jnp.where(ids[k : k + 1, :] == lane, scale[k : k + 1, :], 0.0)
    upper = weight.astype(BF).astype(F32)
    lower = weight - upper
    sub = lax.broadcasted_iota(jnp.int32, (experts, 16, tokens), 1)
    slot = sub.astype(F32)
    place = place[:, None, :]
    contract = (((0,), (0,)), ((), ()))
    main = jnp.concatenate(
        [chunks_ref[:, c * 16 : (c + 1) * 16, :].reshape(experts * 16, LANES) for c in range(3)], axis=1
    )
    rest = chunks_ref[:, 48:64, :].reshape(experts * 16, LANES)
    whole = jnp.zeros((tokens, 3 * LANES), F32)
    low = jnp.zeros((tokens, LANES), F32)
    high = jnp.zeros((tokens, LANES), F32)
    ends = [jnp.zeros((tokens, LANES), F32) for _ in range(4)]

    def times(hit, part, rows):
        coef = jnp.where(hit, part[:, None, :], 0.0).reshape(experts * 16, tokens).astype(BF)
        return lax.dot_general(coef, rows, contract, preferred_element_type=F32)

    for part in (upper, lower):
        whole += times(place == slot, part, main)
        low += times((place == slot) & (sub < 8), part, rest)
        high += times((place == slot + 8.0) & (sub < 8), part, rest)
        for c in range(4):
            ends[c] += times((place == 16.0) & (sub == 8 + c), part, rest)
    odd = lax.rem(x_ref[0], 2) == 1
    even_half = low + pltpu.roll(high, LANES // 2, 1) + ends[3]
    odd_half = pltpu.roll(low, LANES // 2, 1) + high + ends[3]
    half = jnp.where(odd, odd_half, even_half)
    total = jnp.concatenate([whole + jnp.concatenate(ends[:3], axis=1), half], axis=1)
    total = jnp.where(odd, pltpu.roll(total, LANES // 2, 1), total)
    out_ref[...] = total[:, : out_ref.shape[1]].astype(BF)


def combine(x, ids, scale, chunks, columns):
    shape = jax.ShapeDtypeStruct((ids.shape[1], columns), BF)
    return call(combine_kernel, "combine", shape, [in_smem()] + [in_vmem()] * 3)(x, ids, scale, chunks)


def shift(value, d):
    pairs = [(z * X + x, z * X + (x + d) % X) for z in range(2) for x in range(X)]
    return lax.ppermute(value, "pipe", pairs)


def cross(value):
    return lax.ppermute(value, "pipe", [(p, (p + X) % (2 * X)) for p in range(2 * X)])


def body(tokens, expert_ids, gate_scale, w_gate, w_up, w_down):
    groups = lax.axis_size("expert")
    pipe = lax.axis_index("pipe")
    x = (pipe & (X - 1)).reshape(1)
    z = (pipe >> 2).reshape(1)
    ids, scale = expert_ids.T, gate_scale.T
    w_gate, w_up, w_down = w_gate[0], w_up[0], w_down[0]
    buffer = dispatch(x, ids, tokens, groups)
    chunks = lax.all_to_all(buffer, "expert", split_axis=0, concat_axis=0, tiled=True)
    both, downs = pack(x, w_gate, w_up, w_down)
    both = [both[0]] + [shift(both[d], d) for d in ORDER]
    downs = [downs[0]] + [shift(downs[d], d) for d in ORDER]
    held = lax.optimization_barrier((*both, *downs))
    both, downs = held[:X], held[X:]
    other = cross(swap(z, downs))
    parts = project(chunks, both[1:], BF, "project_sent")
    arrived = [shift(part, -d) for d, part in zip(ORDER, parts)]
    chunks, weight = lax.optimization_barrier((chunks, assemble(z, downs, other)))
    (mine,) = project(chunks, both[:1], F32, "project_own")
    hidden = activate(mine, arrived)
    swapped = cross(hidden)
    hiddens = [hidden] + [shift(hidden, d) for d in ORDER[::-1]]
    hiddens += [swapped] + [shift(swapped, d) for d in ORDER[::-1]]
    output = down(x, weight, hiddens, groups)
    returned = lax.all_to_all(output, "expert", split_axis=0, concat_axis=0, tiled=True)
    return combine(x, ids, scale, returned, tokens.shape[1] // (2 * X))


def solution(mesh):
    placed = (
        P("expert", None),
        P("expert", None),
        P("expert", None),
        P("expert", None, "pipe"),
        P("expert", None, "pipe"),
        P("expert", "pipe", None),
    )
    return jax.shard_map(
        body, mesh=mesh, in_specs=placed, out_specs=P("expert", "pipe"), check_vma=False
    )
```

```python
import jax
import jax.numpy as jnp
from jax import lax
from jax.experimental import pallas as pl
from jax.experimental.pallas import tpu as pltpu
from jax.sharding import PartitionSpec as P

BF = jnp.bfloat16
F32 = jnp.float32
LANES = 128
X = 4
ORDER = (1, 3, 2)
PARTS = 4
HOLD = 50_000_000_000
FULL = 60 * 1024 * 1024
VMEM = 16 * 1024 * 1024


def call(kernel, name, out_shape, in_specs, out_specs=None, scratch=(), vmem=VMEM, cost=None):
    if out_specs is None:
        out_specs = jax.tree.map(lambda _: in_vmem(), out_shape)
    return pl.pallas_call(
        kernel,
        out_shape=out_shape,
        in_specs=in_specs,
        out_specs=out_specs,
        scratch_shapes=scratch,
        compiler_params=pltpu.CompilerParams(vmem_limit_bytes=vmem),
        cost_estimate=cost,
        name=name,
    )


def in_vmem():
    return pl.BlockSpec(memory_space=pltpu.VMEM)


def anywhere():
    return pl.BlockSpec(memory_space=pl.ANY)


def in_smem():
    return pl.BlockSpec(memory_space=pltpu.SMEM)


def slots(ids, experts):
    topk, tokens = ids.shape
    lane = lax.broadcasted_iota(jnp.int32, (experts, tokens), 0)
    named = jnp.zeros((experts, tokens), F32)
    for k in range(topk):
        named += (ids[k : k + 1, :] == lane).astype(F32)
    row = lax.broadcasted_iota(jnp.int32, (tokens, tokens), 0)
    col = lax.broadcasted_iota(jnp.int32, (tokens, tokens), 1)
    place = jnp.dot(named.astype(BF), (row < col).astype(BF), preferred_element_type=F32)
    return jnp.where(named > 0.5, place, -1.0)


def spread(tiles, rows):
    count = tiles[0].shape[0]
    sub = lax.broadcasted_iota(jnp.int32, (count, rows, LANES), 1)
    out = jnp.zeros((count, rows, LANES), F32)
    for c, tile in enumerate(tiles):
        out += jnp.where(sub == c, tile[:, None, :], 0.0)
    return out


def dispatch_kernel(x_ref, ids_ref, tok_ref, out_ref, own_ref, rows_ref, sem, sems):
    experts = out_ref.shape[0]
    tokens, quarter = own_ref.shape
    tiles = quarter // LANES
    part = pl.ds(pl.multiple_of(x_ref[0] * quarter, LANES), quarter)
    fetch = pltpu.make_async_copy(tok_ref.at[:, part], own_ref, sem)
    fetch.start()
    place = slots(ids_ref[...], experts)
    fetch.wait()
    tok = own_ref[...]
    last = jnp.dot((place == 16.0).astype(BF), tok, preferred_element_type=F32)
    tail = spread([last[:, c * LANES : (c + 1) * LANES] for c in range(tiles)], 8)
    rows_ref[:, tiles * 16 : tiles * 16 + 8, :] = tail.astype(BF)
    count = experts // PARTS
    slot = lax.broadcasted_iota(jnp.int32, (count, 16, tokens), 1).astype(F32)
    copies = []
    for g in range(PARTS):
        group = slice(g * count, (g + 1) * count)
        pick = jnp.where(place[group][:, None, :] == slot, 1.0, 0.0).reshape(count * 16, tokens).astype(BF)
        rows = jnp.dot(pick, tok, preferred_element_type=F32).astype(BF)
        for c in range(tiles):
            rows_ref[group, c * 16 : (c + 1) * 16, :] = rows[:, c * LANES : (c + 1) * LANES].reshape(count, 16, LANES)
        some = pl.ds(g * count, count)
        copies.append(pltpu.make_async_copy(rows_ref.at[some], out_ref.at[some], sems.at[g]))
        copies[g].start()
    for copy in copies:
        copy.wait()


def dispatch(x, ids, tokens, experts):
    count, width = tokens.shape
    quarter = width // X
    shape = (experts, quarter // LANES * 16 + 8, LANES)
    scratch = [
        pltpu.VMEM((count, quarter), BF),
        pltpu.VMEM(shape, BF),
        pltpu.SemaphoreType.DMA,
        pltpu.SemaphoreType.DMA((PARTS,)),
    ]
    specs = [in_smem(), in_vmem(), anywhere()]
    out = jax.ShapeDtypeStruct(shape, BF)
    return call(dispatch_kernel, "dispatch", out, specs, anywhere(), scratch, FULL)(x, ids, tokens)


def pack_kernel(x_ref, gate_ref, up_ref, down_ref, *refs):
    both, downs, (rows_ref, sems) = refs[:X], refs[X : 2 * X], refs[2 * X :]
    quarter = gate_ref.shape[0] // X
    depth = down_ref.shape[0]
    fetch = pltpu.make_async_copy(down_ref, rows_ref, sems.at[0])
    fetch.start()
    copies = []
    for d in (2, 1, 3, 0):
        q = lax.rem(x_ref[0] + d, X)
        part = pl.ds(pl.multiple_of(q * quarter, quarter), quarter)
        for half, ref in enumerate((gate_ref, up_ref)):
            rows = pl.ds(half * quarter, quarter)
            copies.append(pltpu.make_async_copy(ref.at[part, :], both[d].at[rows, :], sems.at[1 + len(copies)]))
            copies[-1].start()
    fetch.wait()
    for d in range(X):
        q = lax.rem(x_ref[0] + d, X)
        for z in range(2):
            p = z * X + q
            first = p // 2 * (quarter // LANES)
            for c in range(4):
                tile = first + 3 if c == 3 else first + c + 4 * lax.rem(p, 2)
                cols = pl.ds(pl.multiple_of(tile * LANES, LANES), LANES)
                downs[d][pl.ds((z * 4 + c) * depth, depth), :] = rows_ref[:, cols]
    for copy in copies:
        copy.wait()


def pack(x, w_gate, w_up, w_down):
    depth = w_down.shape[0]
    both = jax.ShapeDtypeStruct((2 * (w_gate.shape[0] // X), LANES), BF)
    downs = jax.ShapeDtypeStruct((8 * depth, LANES), BF)
    scratch = [pltpu.VMEM(w_down.shape, BF), pltpu.SemaphoreType.DMA((1 + 2 * X,))]
    specs = [in_smem()] + [anywhere()] * 3
    outs = call(pack_kernel, "pack", [both] * X + [downs] * X, specs, scratch=scratch, vmem=FULL)(x, w_gate, w_up, w_down)
    return outs[:X], outs[X:]


def swap_kernel(z_ref, *refs):
    downs, (out_ref, sems) = refs[:X], refs[X:]
    rows = out_ref.shape[0] // X
    start = pl.multiple_of((1 - z_ref[0]) * rows, rows)
    copies = []
    for d, ref in enumerate(downs):
        copies.append(pltpu.make_async_copy(ref.at[pl.ds(start, rows), :], out_ref.at[pl.ds(d * rows, rows), :], sems.at[d]))
        copies[d].start()
    for copy in copies:
        copy.wait()


def swap(z, downs):
    shape = jax.ShapeDtypeStruct((X * downs[0].shape[0] // 2, LANES), BF)
    scratch = [pltpu.SemaphoreType.DMA((X,))]
    return call(swap_kernel, "swap", shape, [in_smem()] + [anywhere()] * X, scratch=scratch, vmem=FULL)(z, *downs)


def assemble_kernel(z_ref, *refs):
    downs, (other_ref, out_ref) = refs[:X], refs[X:]
    rows = other_ref.shape[0] // X
    depth = rows // 4
    start = z_ref[0] * rows
    for d, ref in enumerate(downs):
        for c in range(4):
            cols = pl.ds(c * LANES, LANES)
            out_ref[pl.ds(d * depth, depth), cols] = ref[pl.ds(pl.multiple_of(start + c * depth, LANES), depth), :]
            out_ref[pl.ds((X + d) * depth, depth), cols] = other_ref[pl.ds(d * rows + c * depth, depth), :]


def assemble(z, downs, other):
    shape = jax.ShapeDtypeStruct((other.shape[0] // 2, 4 * LANES), BF)
    cost = pl.CostEstimate(flops=HOLD, bytes_accessed=4 * other.size, transcendentals=0)
    return call(assemble_kernel, "assemble", shape, [in_smem()] + [in_vmem()] * (X + 1), cost=cost)(z, *downs, other)


def stacked(chunks_ref):
    sources, depth, _ = chunks_ref.shape
    tiles = depth // 16
    main = [chunks_ref[:, c * 16 : (c + 1) * 16, :].reshape(sources * 16, LANES) for c in range(tiles)]
    tail = chunks_ref[:, tiles * 16 : tiles * 16 + 8, :].reshape(sources * 8, LANES)
    row = lax.broadcasted_iota(jnp.int32, (sources, sources * 8), 0)
    col = lax.broadcasted_iota(jnp.int32, (sources, sources * 8), 1)
    last = [
        jnp.dot((col == row * 8 + c).astype(BF), tail, preferred_element_type=F32).astype(BF) for c in range(tiles)
    ]
    return jnp.concatenate(main, axis=1), jnp.concatenate(last, axis=1)


def project(chunks, packs, dtype, name):
    sources, depth, _ = chunks.shape
    quarter = depth // 16 * LANES

    def kernel(chunks_ref, *refs):
        sent, outs = refs[: len(packs)], refs[len(packs) :]
        main, last = stacked(chunks_ref)
        for pack_ref, out_ref in zip(sent, outs):
            weight = jnp.concatenate([pack_ref[pl.ds(0, quarter), :], pack_ref[pl.ds(quarter, quarter), :]], axis=1)
            out_ref[pl.ds(0, sources * 16), :] = jnp.dot(main, weight, preferred_element_type=F32).astype(dtype)
            out_ref[pl.ds(sources * 16, sources), :] = jnp.dot(last, weight, preferred_element_type=F32).astype(dtype)

    shapes = [jax.ShapeDtypeStruct((sources * 17, 2 * LANES), dtype)] * len(packs)
    return call(kernel, name, shapes, [in_vmem()] * (1 + len(packs)))(chunks, *packs)


def activate_kernel(own_ref, *refs):
    parts, out_ref = refs[:-1], refs[-1]
    total = own_ref[...]
    for ref in parts:
        total += ref[...].astype(F32)
    gate, up = total[:, :LANES], total[:, LANES:]
    out_ref[...] = (gate / (1.0 + jnp.exp(-gate)) * up).astype(BF)


def activate(own, parts):
    shape = jax.ShapeDtypeStruct((own.shape[0], LANES), BF)
    return call(activate_kernel, "activate", shape, [in_vmem()] * (1 + len(parts)))(own, *parts)


def down_kernel(x_ref, weight_ref, *refs):
    hiddens, out_ref = refs[:-1], refs[-1]
    experts = out_ref.shape[0]
    hidden = jnp.concatenate([hiddens[i][...] for i in (0, 3, 2, 1, 4, 7, 6, 5)], axis=1)
    weight = weight_ref[...]
    count = experts * 16
    main = jnp.dot(hidden[:count], weight, preferred_element_type=F32)
    last = jnp.dot(hidden[count:], weight, preferred_element_type=F32)
    for c in range(3):
        out_ref[:, c * 16 : (c + 1) * 16, :] = (
            main[:, c * LANES : (c + 1) * LANES].astype(BF).reshape(experts, 16, LANES)
        )
    half = main[:, 3 * LANES :]
    turned = pltpu.roll(half, LANES // 2, 1)
    odd = lax.rem(x_ref[0], 2) == 1
    low = jnp.where(odd, turned, half).reshape(experts, 16, LANES)[:, :8]
    high = jnp.where(odd, half, turned).reshape(experts, 16, LANES)[:, 8:]
    lane = lax.broadcasted_iota(jnp.int32, low.shape, 2)
    halves = jnp.where(lane < LANES // 2, low, high)
    tail = spread([last[:, c * LANES : (c + 1) * LANES] for c in range(4)], 8)
    out_ref[:, 48:64, :] = jnp.concatenate([halves, tail], axis=1).astype(BF)


def down(x, weight, hiddens, experts):
    shape = jax.ShapeDtypeStruct((experts, 64, LANES), BF)
    specs = [in_smem()] + [in_vmem()] * (1 + len(hiddens))
    return call(down_kernel, "down", shape, specs)(x, weight, *hiddens)


def combine_kernel(x_ref, ids_ref, scale_ref, chunks_ref, out_ref):
    experts = chunks_ref.shape[0]
    ids, scale = ids_ref[...], scale_ref[...]
    topk, tokens = ids.shape
    place = slots(ids, experts)
    lane = lax.broadcasted_iota(jnp.int32, (experts, tokens), 0)
    weight = jnp.zeros((experts, tokens), F32)
    for k in range(topk):
        weight += jnp.where(ids[k : k + 1, :] == lane, scale[k : k + 1, :], 0.0)
    upper = weight.astype(BF).astype(F32)
    lower = weight - upper
    sub = lax.broadcasted_iota(jnp.int32, (experts, 16, tokens), 1)
    slot = sub.astype(F32)
    place = place[:, None, :]
    contract = (((0,), (0,)), ((), ()))
    main = jnp.concatenate(
        [chunks_ref[:, c * 16 : (c + 1) * 16, :].reshape(experts * 16, LANES) for c in range(3)], axis=1
    )
    rest = chunks_ref[:, 48:64, :].reshape(experts * 16, LANES)
    whole = jnp.zeros((tokens, 3 * LANES), F32)
    low = jnp.zeros((tokens, LANES), F32)
    high = jnp.zeros((tokens, LANES), F32)
    ends = [jnp.zeros((tokens, LANES), F32) for _ in range(4)]

    def times(hit, part, rows):
        coef = jnp.where(hit, part[:, None, :], 0.0).reshape(experts * 16, tokens).astype(BF)
        return lax.dot_general(coef, rows, contract, preferred_element_type=F32)

    for part in (upper, lower):
        whole += times(place == slot, part, main)
        low += times((place == slot) & (sub < 8), part, rest)
        high += times((place == slot + 8.0) & (sub < 8), part, rest)
        for c in range(4):
            ends[c] += times((place == 16.0) & (sub == 8 + c), part, rest)
    odd = lax.rem(x_ref[0], 2) == 1
    even_half = low + pltpu.roll(high, LANES // 2, 1) + ends[3]
    odd_half = pltpu.roll(low, LANES // 2, 1) + high + ends[3]
    half = jnp.where(odd, odd_half, even_half)
    total = jnp.concatenate([whole + jnp.concatenate(ends[:3], axis=1), half], axis=1)
    total = jnp.where(odd, pltpu.roll(total, LANES // 2, 1), total)
    out_ref[...] = total[:, : out_ref.shape[1]].astype(BF)


def combine(x, ids, scale, chunks, columns):
    shape = jax.ShapeDtypeStruct((ids.shape[1], columns), BF)
    return call(combine_kernel, "combine", shape, [in_smem()] + [in_vmem()] * 3)(x, ids, scale, chunks)


def shift(value, d):
    pairs = [(z * X + x, z * X + (x + d) % X) for z in range(2) for x in range(X)]
    return lax.ppermute(value, "pipe", pairs)


def cross(value):
    return lax.ppermute(value, "pipe", [(p, (p + X) % (2 * X)) for p in range(2 * X)])


def body(tokens, expert_ids, gate_scale, w_gate, w_up, w_down):
    groups = lax.axis_size("expert")
    pipe = lax.axis_index("pipe")
    x = (pipe & (X - 1)).reshape(1)
    z = (pipe >> 2).reshape(1)
    ids, scale = expert_ids.T, gate_scale.T
    w_gate, w_up, w_down = w_gate[0], w_up[0], w_down[0]
    buffer = dispatch(x, ids, tokens, groups)
    chunks = lax.all_to_all(buffer, "expert", split_axis=0, concat_axis=0, tiled=True)
    both, downs = pack(x, w_gate, w_up, w_down)
    both = [both[0]] + [shift(both[d], d) for d in ORDER]
    downs = [downs[0]] + [shift(downs[d], d) for d in ORDER]
    held = lax.optimization_barrier((both[0], both[2], both[1], both[3], *downs))
    both, downs = (held[0], held[2], held[1], held[3]), held[X:]
    other = cross(swap(z, downs))
    parts = project(chunks, both[1:], BF, "project_sent")
    arrived = [shift(part, -d) for d, part in zip(ORDER, parts)]
    chunks, weight = lax.optimization_barrier((chunks, assemble(z, downs, other)))
    (mine,) = project(chunks, both[:1], F32, "project_own")
    hidden = activate(mine, arrived)
    swapped = cross(hidden)
    hiddens = [hidden] + [shift(hidden, d) for d in ORDER[::-1]]
    hiddens += [swapped] + [shift(swapped, d) for d in ORDER[::-1]]
    output = down(x, weight, hiddens, groups)
    returned = lax.all_to_all(output, "expert", split_axis=0, concat_axis=0, tiled=True)
    return combine(x, ids, scale, returned, tokens.shape[1] // (2 * X))


def solution(mesh):
    placed = (
        P("expert", None),
        P("expert", None),
        P("expert", None),
        P("expert", None, "pipe"),
        P("expert", None, "pipe"),
        P("expert", "pipe", None),
    )
    return jax.shard_map(
        body, mesh=mesh, in_specs=placed, out_specs=P("expert", "pipe"), check_vma=False
    )
```

```python
import jax
import jax.numpy as jnp
from jax import lax
from jax.experimental import pallas as pl
from jax.experimental.pallas import tpu as pltpu
from jax.sharding import PartitionSpec as P

BF = jnp.bfloat16
F32 = jnp.float32
LANES = 128
X = 4
ORDER = (1, 3, 2)
PARTS = 4
HOLD = 50_000_000_000
FULL = 60 * 1024 * 1024
VMEM = 16 * 1024 * 1024


def call(kernel, name, out_shape, in_specs, out_specs=None, scratch=(), vmem=VMEM, cost=None):
    if out_specs is None:
        out_specs = jax.tree.map(lambda _: in_vmem(), out_shape)
    return pl.pallas_call(
        kernel,
        out_shape=out_shape,
        in_specs=in_specs,
        out_specs=out_specs,
        scratch_shapes=scratch,
        compiler_params=pltpu.CompilerParams(vmem_limit_bytes=vmem),
        cost_estimate=cost,
        name=name,
    )


def in_vmem():
    return pl.BlockSpec(memory_space=pltpu.VMEM)


def anywhere():
    return pl.BlockSpec(memory_space=pl.ANY)


def in_smem():
    return pl.BlockSpec(memory_space=pltpu.SMEM)


def slots(ids, experts):
    topk, tokens = ids.shape
    lane = lax.broadcasted_iota(jnp.int32, (experts, tokens), 0)
    named = jnp.zeros((experts, tokens), F32)
    for k in range(topk):
        named += (ids[k : k + 1, :] == lane).astype(F32)
    row = lax.broadcasted_iota(jnp.int32, (tokens, tokens), 0)
    col = lax.broadcasted_iota(jnp.int32, (tokens, tokens), 1)
    place = jnp.dot(named.astype(BF), (row < col).astype(BF), preferred_element_type=F32)
    return jnp.where(named > 0.5, place, -1.0)


def spread(tiles, rows):
    count = tiles[0].shape[0]
    sub = lax.broadcasted_iota(jnp.int32, (count, rows, LANES), 1)
    out = jnp.zeros((count, rows, LANES), F32)
    for c, tile in enumerate(tiles):
        out += jnp.where(sub == c, tile[:, None, :], 0.0)
    return out


def dispatch_kernel(x_ref, ids_ref, tok_ref, out_ref, own_ref, rows_ref, sem, sems):
    experts = out_ref.shape[0]
    tokens, quarter = own_ref.shape
    tiles = quarter // LANES
    part = pl.ds(pl.multiple_of(x_ref[0] * quarter, LANES), quarter)
    fetch = pltpu.make_async_copy(tok_ref.at[:, part], own_ref, sem)
    fetch.start()
    place = slots(ids_ref[...], experts)
    fetch.wait()
    tok = own_ref[...]
    last = jnp.dot((place == 16.0).astype(BF), tok, preferred_element_type=F32)
    tail = spread([last[:, c * LANES : (c + 1) * LANES] for c in range(tiles)], 8)
    rows_ref[:, tiles * 16 : tiles * 16 + 8, :] = tail.astype(BF)
    count = experts // PARTS
    slot = lax.broadcasted_iota(jnp.int32, (count, 16, tokens), 1).astype(F32)
    copies = []
    for g in range(PARTS):
        group = slice(g * count, (g + 1) * count)
        pick = jnp.where(place[group][:, None, :] == slot, 1.0, 0.0).reshape(count * 16, tokens).astype(BF)
        rows = jnp.dot(pick, tok, preferred_element_type=F32).astype(BF)
        for c in range(tiles):
            rows_ref[group, c * 16 : (c + 1) * 16, :] = rows[:, c * LANES : (c + 1) * LANES].reshape(count, 16, LANES)
        some = pl.ds(g * count, count)
        copies.append(pltpu.make_async_copy(rows_ref.at[some], out_ref.at[some], sems.at[g]))
        copies[g].start()
    for copy in copies:
        copy.wait()


def dispatch(x, ids, tokens, experts):
    count, width = tokens.shape
    quarter = width // X
    shape = (experts, quarter // LANES * 16 + 8, LANES)
    scratch = [
        pltpu.VMEM((count, quarter), BF),
        pltpu.VMEM(shape, BF),
        pltpu.SemaphoreType.DMA,
        pltpu.SemaphoreType.DMA((PARTS,)),
    ]
    specs = [in_smem(), in_vmem(), anywhere()]
    out = jax.ShapeDtypeStruct(shape, BF)
    return call(dispatch_kernel, "dispatch", out, specs, anywhere(), scratch, FULL)(x, ids, tokens)


def pack_kernel(x_ref, gate_ref, up_ref, down_ref, *refs):
    both, downs, (rows_ref, sems) = refs[:X], refs[X : 2 * X], refs[2 * X :]
    quarter = gate_ref.shape[0] // X
    depth = down_ref.shape[0]
    fetch = pltpu.make_async_copy(down_ref, rows_ref, sems.at[0])
    fetch.start()
    copies = []
    for d in (2, 1, 3, 0):
        q = lax.rem(x_ref[0] + d, X)
        part = pl.ds(pl.multiple_of(q * quarter, quarter), quarter)
        for half, ref in enumerate((gate_ref, up_ref)):
            rows = pl.ds(half * quarter, quarter)
            copies.append(pltpu.make_async_copy(ref.at[part, :], both[d].at[rows, :], sems.at[1 + len(copies)]))
            copies[-1].start()
    fetch.wait()
    for d in range(X):
        q = lax.rem(x_ref[0] + d, X)
        for z in range(2):
            p = z * X + q
            first = p // 2 * (quarter // LANES)
            for c in range(4):
                tile = first + 3 if c == 3 else first + c + 4 * lax.rem(p, 2)
                cols = pl.ds(pl.multiple_of(tile * LANES, LANES), LANES)
                downs[d][pl.ds((z * 4 + c) * depth, depth), :] = rows_ref[:, cols]
    for copy in copies:
        copy.wait()


def pack(x, w_gate, w_up, w_down):
    depth = w_down.shape[0]
    both = jax.ShapeDtypeStruct((2 * (w_gate.shape[0] // X), LANES), BF)
    downs = jax.ShapeDtypeStruct((8 * depth, LANES), BF)
    scratch = [pltpu.VMEM(w_down.shape, BF), pltpu.SemaphoreType.DMA((1 + 2 * X,))]
    specs = [in_smem()] + [anywhere()] * 3
    outs = call(pack_kernel, "pack", [both] * X + [downs] * X, specs, scratch=scratch, vmem=FULL)(x, w_gate, w_up, w_down)
    return outs[:X], outs[X:]


def swap_kernel(z_ref, *refs):
    downs, (out_ref, sems) = refs[:X], refs[X:]
    rows = out_ref.shape[0] // X
    start = pl.multiple_of((1 - z_ref[0]) * rows, rows)
    copies = []
    for d, ref in enumerate(downs):
        copies.append(pltpu.make_async_copy(ref.at[pl.ds(start, rows), :], out_ref.at[pl.ds(d * rows, rows), :], sems.at[d]))
        copies[d].start()
    for copy in copies:
        copy.wait()


def swap(z, downs):
    shape = jax.ShapeDtypeStruct((X * downs[0].shape[0] // 2, LANES), BF)
    scratch = [pltpu.SemaphoreType.DMA((X,))]
    return call(swap_kernel, "swap", shape, [in_smem()] + [anywhere()] * X, scratch=scratch, vmem=FULL)(z, *downs)


def assemble_kernel(z_ref, *refs):
    downs, (other_ref, out_ref) = refs[:X], refs[X:]
    rows = other_ref.shape[0] // X
    depth = rows // 4
    start = z_ref[0] * rows
    for d, ref in enumerate(downs):
        for c in range(4):
            cols = pl.ds(c * LANES, LANES)
            out_ref[pl.ds(d * depth, depth), cols] = ref[pl.ds(pl.multiple_of(start + c * depth, LANES), depth), :]
            out_ref[pl.ds((X + d) * depth, depth), cols] = other_ref[pl.ds(d * rows + c * depth, depth), :]


def assemble(z, downs, other):
    shape = jax.ShapeDtypeStruct((other.shape[0] // 2, 4 * LANES), BF)
    cost = pl.CostEstimate(flops=HOLD, bytes_accessed=4 * other.size, transcendentals=0)
    return call(assemble_kernel, "assemble", shape, [in_smem()] + [in_vmem()] * (X + 1), cost=cost)(z, *downs, other)


def stacked(chunks_ref):
    sources, depth, _ = chunks_ref.shape
    tiles = depth // 16
    main = [chunks_ref[:, c * 16 : (c + 1) * 16, :].reshape(sources * 16, LANES) for c in range(tiles)]
    tail = chunks_ref[:, tiles * 16 : tiles * 16 + 8, :].reshape(sources * 8, LANES)
    row = lax.broadcasted_iota(jnp.int32, (sources, sources * 8), 0)
    col = lax.broadcasted_iota(jnp.int32, (sources, sources * 8), 1)
    last = [
        jnp.dot((col == row * 8 + c).astype(BF), tail, preferred_element_type=F32).astype(BF) for c in range(tiles)
    ]
    return jnp.concatenate(main, axis=1), jnp.concatenate(last, axis=1)


def project(chunks, packs, dtype, name):
    sources, depth, _ = chunks.shape
    quarter = depth // 16 * LANES

    def kernel(chunks_ref, *refs):
        sent, outs = refs[: len(packs)], refs[len(packs) :]
        main, last = stacked(chunks_ref)
        for pack_ref, out_ref in zip(sent, outs):
            weight = jnp.concatenate([pack_ref[pl.ds(0, quarter), :], pack_ref[pl.ds(quarter, quarter), :]], axis=1)
            out_ref[pl.ds(0, sources * 16), :] = jnp.dot(main, weight, preferred_element_type=F32).astype(dtype)
            out_ref[pl.ds(sources * 16, sources), :] = jnp.dot(last, weight, preferred_element_type=F32).astype(dtype)

    shapes = [jax.ShapeDtypeStruct((sources * 17, 2 * LANES), dtype)] * len(packs)
    return call(kernel, name, shapes, [in_vmem()] * (1 + len(packs)))(chunks, *packs)


def activate_kernel(own_ref, *refs):
    parts, out_ref = refs[:-1], refs[-1]
    total = own_ref[...]
    for ref in parts:
        total += ref[...].astype(F32)
    gate, up = total[:, :LANES], total[:, LANES:]
    out_ref[...] = (gate / (1.0 + jnp.exp(-gate)) * up).astype(BF)


def activate(own, parts):
    shape = jax.ShapeDtypeStruct((own.shape[0], LANES), BF)
    return call(activate_kernel, "activate", shape, [in_vmem()] * (1 + len(parts)))(own, *parts)


def down_kernel(x_ref, weight_ref, *refs):
    hiddens, out_ref = refs[:-1], refs[-1]
    experts = out_ref.shape[0]
    hidden = jnp.concatenate([hiddens[i][...] for i in (0, 3, 2, 1, 4, 7, 6, 5)], axis=1)
    weight = weight_ref[...]
    count = experts * 16
    main = jnp.dot(hidden[:count], weight, preferred_element_type=F32)
    last = jnp.dot(hidden[count:], weight, preferred_element_type=F32)
    for c in range(3):
        out_ref[:, c * 16 : (c + 1) * 16, :] = (
            main[:, c * LANES : (c + 1) * LANES].astype(BF).reshape(experts, 16, LANES)
        )
    half = main[:, 3 * LANES :]
    turned = pltpu.roll(half, LANES // 2, 1)
    odd = lax.rem(x_ref[0], 2) == 1
    low = jnp.where(odd, turned, half).reshape(experts, 16, LANES)[:, :8]
    high = jnp.where(odd, half, turned).reshape(experts, 16, LANES)[:, 8:]
    lane = lax.broadcasted_iota(jnp.int32, low.shape, 2)
    halves = jnp.where(lane < LANES // 2, low, high)
    tail = spread([last[:, c * LANES : (c + 1) * LANES] for c in range(4)], 8)
    out_ref[:, 48:64, :] = jnp.concatenate([halves, tail], axis=1).astype(BF)


def down(x, weight, hiddens, experts):
    shape = jax.ShapeDtypeStruct((experts, 64, LANES), BF)
    specs = [in_smem()] + [in_vmem()] * (1 + len(hiddens))
    return call(down_kernel, "down", shape, specs)(x, weight, *hiddens)


def combine_kernel(x_ref, ids_ref, scale_ref, chunks_ref, out_ref):
    experts = chunks_ref.shape[0]
    ids, scale = ids_ref[...], scale_ref[...]
    topk, tokens = ids.shape
    place = slots(ids, experts)
    lane = lax.broadcasted_iota(jnp.int32, (experts, tokens), 0)
    weight = jnp.zeros((experts, tokens), F32)
    for k in range(topk):
        weight += jnp.where(ids[k : k + 1, :] == lane, scale[k : k + 1, :], 0.0)
    upper = weight.astype(BF).astype(F32)
    lower = weight - upper
    sub = lax.broadcasted_iota(jnp.int32, (experts, 16, tokens), 1)
    slot = sub.astype(F32)
    place = place[:, None, :]
    contract = (((0,), (0,)), ((), ()))
    main = jnp.concatenate(
        [chunks_ref[:, c * 16 : (c + 1) * 16, :].reshape(experts * 16, LANES) for c in range(3)], axis=1
    )
    rest = chunks_ref[:, 48:64, :].reshape(experts * 16, LANES)
    whole = jnp.zeros((tokens, 3 * LANES), F32)
    low = jnp.zeros((tokens, LANES), F32)
    high = jnp.zeros((tokens, LANES), F32)
    ends = [jnp.zeros((tokens, LANES), F32) for _ in range(4)]

    def times(hit, part, rows):
        coef = jnp.where(hit, part[:, None, :], 0.0).reshape(experts * 16, tokens).astype(BF)
        return lax.dot_general(coef, rows, contract, preferred_element_type=F32)

    for part in (upper, lower):
        whole += times(place == slot, part, main)
        low += times((place == slot) & (sub < 8), part, rest)
        high += times((place == slot + 8.0) & (sub < 8), part, rest)
        for c in range(4):
            ends[c] += times((place == 16.0) & (sub == 8 + c), part, rest)
    odd = lax.rem(x_ref[0], 2) == 1
    even_half = low + pltpu.roll(high, LANES // 2, 1) + ends[3]
    odd_half = pltpu.roll(low, LANES // 2, 1) + high + ends[3]
    half = jnp.where(odd, odd_half, even_half)
    total = jnp.concatenate([whole + jnp.concatenate(ends[:3], axis=1), half], axis=1)
    total = jnp.where(odd, pltpu.roll(total, LANES // 2, 1), total)
    out_ref[...] = total[:, : out_ref.shape[1]].astype(BF)


def combine(x, ids, scale, chunks, columns):
    shape = jax.ShapeDtypeStruct((ids.shape[1], columns), BF)
    return call(combine_kernel, "combine", shape, [in_smem()] + [in_vmem()] * 3)(x, ids, scale, chunks)


def shift(value, d):
    pairs = [(z * X + x, z * X + (x + d) % X) for z in range(2) for x in range(X)]
    return lax.ppermute(value, "pipe", pairs)


def cross(value):
    return lax.ppermute(value, "pipe", [(p, (p + X) % (2 * X)) for p in range(2 * X)])


def body(tokens, expert_ids, gate_scale, w_gate, w_up, w_down):
    groups = lax.axis_size("expert")
    pipe = lax.axis_index("pipe")
    x = (pipe & (X - 1)).reshape(1)
    z = (pipe >> 2).reshape(1)
    ids, scale = expert_ids.T, gate_scale.T
    w_gate, w_up, w_down = w_gate[0], w_up[0], w_down[0]
    buffer = dispatch(x, ids, tokens, groups)
    chunks = lax.all_to_all(buffer, "expert", split_axis=0, concat_axis=0, tiled=True)
    both, downs = pack(x, w_gate, w_up, w_down)
    both = [both[0]] + [shift(both[d], d) for d in ORDER]
    downs = [downs[0]] + [shift(downs[d], d) for d in ORDER]
    held = lax.optimization_barrier((both[0], both[2], both[1], both[3], *downs))
    both, downs = (held[0], held[2], held[1], held[3]), held[X:]
    other = cross(swap(z, downs))
    parts = project(chunks, [both[i] for i in (2, 1, 3)], BF, "project_sent")
    arrived = [shift(part, -d) for d, part in zip((3, 1, 2), parts)]
    chunks, weight = lax.optimization_barrier((chunks, assemble(z, downs, other)))
    (mine,) = project(chunks, both[:1], F32, "project_own")
    hidden = activate(mine, arrived)
    swapped = cross(hidden)
    hiddens = [hidden] + [shift(hidden, d) for d in ORDER[::-1]]
    hiddens += [swapped] + [shift(swapped, d) for d in ORDER[::-1]]
    output = down(x, weight, hiddens, groups)
    returned = lax.all_to_all(output, "expert", split_axis=0, concat_axis=0, tiled=True)
    return combine(x, ids, scale, returned, tokens.shape[1] // (2 * X))


def solution(mesh):
    placed = (
        P("expert", None),
        P("expert", None),
        P("expert", None),
        P("expert", None, "pipe"),
        P("expert", None, "pipe"),
        P("expert", "pipe", None),
    )
    return jax.shard_map(
        body, mesh=mesh, in_specs=placed, out_specs=P("expert", "pipe"), check_vma=False
    )
```
